32 devices in a mesh: yz: 8 (over y, x, core), gx: 4 (over z).
Axes of the slice: x: 2, y: 2, z: 4, core: 2. Of those that a mesh axis runs over, the one named last changes fastest.
Arguments:
- state: float32 [7, 64, 64, 128], P(None, 'gx', 'yz'), may hold values from -2.5 to 2.5
- register: float32 [7, 64, 64, 128], P(None, 'gx', 'yz'), may hold values from -3 to 3
- forcing: float32 [3, 64, 64, 128], P(None, 'gx', 'yz'), may hold values from -3 to 3
- y_shift: int32 [1], replicated, may hold values from 0 to 63
Outputs:
- new_state: float32 [7, 64, 64, 128], P(None, 'gx', 'yz')
- new_register: float32 [7, 64, 64, 128], P(None, 'gx', 'yz')
The draws below stay inside these ranges and needn't reach their ends.
All inputs are finite; a program needn't handle non-finite values.
Results may differ from the reference program's by a relative error of at most 0.000092.
Values sent between devices are 32-bit elements; how exact they have to be, the bound alone decides.
No kernel may reach another device: no remote copies, remote signals or barrier semaphores. Data moves between devices by JAX's collectives and lax.ppermute only.
A program may use at most 64 MiB of HBM per device.

```python
import jax
import jax.numpy as jnp
from jax import lax

NZ = 128
NX = 64
NY = 64


def level_of(stream_key, extent, split, smallest, high):
    gain, own = 1.0, jax.random.fold_in(stream_key, 6)
    for position, shards_of in split:
        draws = jnp.exp(jax.random.uniform(jax.random.fold_in(own, position), (shards_of,), jnp.float32, smallest / len(split), high / len(split)))
        gain = gain * jnp.repeat(draws, extent[position] // shards_of).reshape([-1 if axis == position else 1 for axis in range(len(extent))])
    return gain


def bell_draw(own_key, extent, spread, limit, split=(), held_as=jnp.bfloat16):
    factor_of = level_of(own_key, extent, split, -0.22, 0.18) if split else 1.0
    drawn = jax.random.normal(own_key, extent, jnp.float32) * spread * factor_of
    return jnp.minimum(jnp.maximum(drawn, -limit), limit).astype(held_as)


def setup_inputs(seed: int = 0) -> dict:
    streams_of = jax.random.split(jax.random.key(seed), 5)
    return {
        "state": bell_draw(streams_of[0], (7, NX, NY, NZ), 0.4, 2.5, ((1, 4), (2, 8)), jnp.float32),
        "register": bell_draw(streams_of[1], (7, NX, NY, NZ), 0.5, 3.0, ((1, 4), (2, 8)), jnp.float32),
        "forcing": bell_draw(streams_of[2], (3, NX, NY, NZ), 0.5, 3.0, ((1, 4), (2, 8)), jnp.float32),
        "y_shift": jax.random.randint(streams_of[3], (1,), 0, NY).astype(jnp.int32),
    }


def first_diff(field, axis):
    count = field.shape[axis] - 6

    def part(offset):
        return lax.slice_in_dim(field, 3 + offset, 3 + offset + count, axis=axis)
    return (45.0 * (part(1) - part(-1)) - 9.0 * (part(2) - part(-2)) + (part(3) - part(-3))) / 60.0

def second_diff(field, axis):
    count = field.shape[axis] - 6

    def part(offset):
        return lax.slice_in_dim(field, 3 + offset, 3 + offset + count, axis=axis)
    return (-490.0 * part(0) + 270.0 * (part(1) + part(-1)) - 27.0 * (part(2) + part(-2)) + 2.0 * (part(3) + part(-3))) / 180.0

def inner(field, axes):
    for axis in axes:
        field = lax.slice_in_dim(field, 3, field.shape[axis] - 3, axis=axis)
    return field

def tendency(padded, forcing, xfrac, inv_width):
    grads = [inner(first_diff(padded, 1), (2, 3)), inner(first_diff(padded, 2), (1, 3)), inner(first_diff(padded, 3), (1, 2))]
    vectors = padded[:6]
    curv = [inner(second_diff(vectors, 1), (2, 3)), inner(second_diff(vectors, 2), (1, 3)), inner(second_diff(vectors, 3), (1, 2))]
    cross_xy = inner(first_diff(first_diff(vectors, 2), 1), (3,))
    cross_xz = inner(first_diff(first_diff(vectors, 3), 1), (2,))
    cross_yz = inner(first_diff(first_diff(vectors, 3), 2), (1,))
    center = inner(padded, (1, 2, 3))
    velx, vely, velz = (center[0], center[1], center[2])
    potx, poty = (center[3], center[4])

    def grad(axis, comp):
        return grads[axis][comp]

    def lapl(comp):
        return curv[0][comp] + curv[1][comp] + curv[2][comp]

    def grad_div(first):
        return (curv[0][first] + cross_xy[first + 1] + cross_xz[first + 2], cross_xy[first] + curv[1][first + 1] + cross_yz[first + 2], cross_xz[first] + cross_yz[first + 1] + curv[2][first + 2])
    fieldx = grad(1, 5) - grad(2, 4)
    fieldy = grad(2, 3) - grad(0, 5)
    fieldz = grad(0, 4) - grad(1, 3) + 0.5
    potdiv = grad_div(3)
    currx = potdiv[0] - lapl(3)
    curry = potdiv[1] - lapl(4)
    currz = potdiv[2] - lapl(5)
    veldiv = grad_div(0)
    inv_rho = jnp.exp(-center[6])
    flow = -1.5 * xfrac
    shear_rate = -1.5 * inv_width

    def advect(comp):
        return velx * grad(0, comp) + (vely + flow) * grad(1, comp) + velz * grad(2, comp)
    divu = grad(0, 0) + grad(1, 1) + grad(2, 2)

    def strain_term(row):
        total = jnp.zeros_like(velx)
        for col in range(3):
            strain = 0.5 * (grad(col, row) + grad(row, col))
            if col == row:
                strain = strain - divu / 3.0
            total = total + 2.0 * strain * grad(col, 6)
        return total
    lorentz = (curry * fieldz - currz * fieldy, currz * fieldx - currx * fieldz, currx * fieldy - curry * fieldx)
    emf = (vely * fieldz - velz * fieldy, velz * fieldx - velx * fieldz, velx * fieldy - vely * fieldx)
    curr = (currx, curry, currz)
    rates = []
    for comp in range(3):
        rate = -advect(comp) - grad(comp, 6) + lorentz[comp] * inv_rho
        rate = rate + 0.05 * (lapl(comp) + veldiv[comp] / 3.0 + strain_term(comp)) + forcing[comp]
        if comp == 0:
            rate = rate + 2.0 * 0.5 * vely
        if comp == 1:
            rate = rate - 2.0 * 0.5 * velx - shear_rate * velx
        rates.append(rate)
    for comp in range(3):
        rate = emf[comp] - flow * grad(1, 3 + comp) - 0.05 * curr[comp]
        if comp == 0:
            rate = rate - shear_rate * poty
        rates.append(rate)
    rates.append(-advect(6) - divu)
    return jnp.stack(rates)

def reference(state, register, forcing, y_shift):
    shift = y_shift[0]
    nx = state.shape[1]
    low = jnp.roll(state[:, nx - 3:], -shift, axis=2)
    high = jnp.roll(state[:, :3], shift, axis=2)
    ext = jnp.concatenate([low, state, high], axis=1)
    ext = jnp.concatenate([ext[:, :, -3:], ext, ext[:, :, :3]], axis=2)
    ext = jnp.concatenate([ext[:, :, :, -3:], ext, ext[:, :, :, :3]], axis=3)
    inv_width = 1.0 / nx
    width = 4
    starts = (jnp.arange(nx // width) * width).astype(jnp.int32)

    def block(start):
        piece = lax.dynamic_slice_in_dim(ext, start, width + 6, axis=1)
        push = lax.dynamic_slice_in_dim(forcing, start, width, axis=1)
        index = (start + jnp.arange(width)).astype(jnp.float32)
        xfrac = ((index + 0.5) * inv_width - 0.5).reshape(width, 1, 1)
        return tendency(piece, push, xfrac, inv_width)
    blocks = lax.map(block, starts)
    rate = jnp.transpose(blocks, (1, 0, 2, 3, 4)).reshape(state.shape)
    new_register = -5.0 / 9.0 * register + 0.15 * rate
    new_state = state + 15.0 / 16.0 * new_register
    return (new_state, new_register)
```

```python
import functools

import jax
import jax.numpy as jnp
import numpy as np
from jax import lax
from jax.experimental import pallas as pl
from jax.experimental.pallas import tpu as pltpu
from jax.sharding import PartitionSpec as P

LANES = 128
FIRST = ((1, 45.0), (2, -9.0), (3, 1.0))
SECOND = ((1, 270.0), (2, -27.0), (3, 2.0))
MIXED = (0, 1, 3, 4)
PLAIN = (2, 5, 6)
SHEAR_Z = (1, 2, 4, 5)
ROW = 8
TALL = 24
VMEM = 32 * 1024 * 1024


def z_weights():
    one = np.zeros((LANES, 2 * LANES), np.float32)
    cells = np.arange(LANES)
    one[cells, LANES + cells] = -490.0
    for step, weight in FIRST:
        one[(cells + step) % LANES, cells] += weight
        one[(cells - step) % LANES, cells] -= weight
    for step, weight in SECOND:
        one[(cells + step) % LANES, LANES + cells] += weight
        one[(cells - step) % LANES, LANES + cells] += weight
    return np.concatenate([one, one]).astype(jnp.bfloat16)


def along_z(value, weights):
    upper = value.astype(jnp.bfloat16)
    rest = (value - upper.astype(jnp.float32)).astype(jnp.bfloat16)
    return jnp.dot(
        jnp.concatenate([upper, rest], axis=1), weights, preferred_element_type=jnp.float32
    )


def first_diff(part):
    return (
        0.75 * (part(1) - part(-1))
        - 0.15 * (part(2) - part(-2))
        + (1.0 / 60.0) * (part(3) - part(-3))
    )


def second_diff(part):
    return (
        (-490.0 / 180.0) * part(0)
        + 1.5 * (part(1) + part(-1))
        - 0.15 * (part(2) + part(-2))
        + (1.0 / 90.0) * (part(3) + part(-3))
    )


def x_terms(planes_of, mixes_of):
    grad = [first_diff(planes_of(field)) for field in range(7)]
    mix = [first_diff(mixes_of(number)) for number in range(6)]
    viscous = (
        (4.0 / 3.0) * second_diff(planes_of(0)) + (1.0 / 3.0) * mix[0],
        second_diff(planes_of(1)) + (1.0 / 3.0) * mix[1],
        second_diff(planes_of(2)) + (1.0 / 3.0) * mix[2],
    )
    current = (
        mix[3],
        mix[4] - second_diff(planes_of(4)),
        mix[5] - second_diff(planes_of(5)),
    )
    return grad, viscous, current


def rates_of(center, force, index, inv_width, grads, viscous, curr):
    velx, vely, velz, potx, poty, potz, logr = center
    grad_x, grad_y, grad_z = grads
    field_x = grad_y[5] - grad_z[4]
    field_y = grad_z[3] - grad_x[5]
    field_z = grad_x[4] - grad_y[3] + 0.5
    lorentz = (
        curr[1] * field_z - curr[2] * field_y,
        curr[2] * field_x - curr[0] * field_z,
        curr[0] * field_y - curr[1] * field_x,
    )
    emf = (
        vely * field_z - velz * field_y,
        velz * field_x - velx * field_z,
        velx * field_y - vely * field_x,
    )
    inv_rho = jnp.exp(-logr)
    flow = -1.5 * ((index.astype(jnp.float32) + 0.5) * inv_width - 0.5)
    shear_rate = -1.5 * inv_width
    carried = vely + flow
    divu = grad_x[0] + grad_y[1] + grad_z[2]

    def advect(comp):
        return velx * grad_x[comp] + carried * grad_y[comp] + velz * grad_z[comp]

    rates = []
    for comp in range(3):
        total = (-2.0 / 3.0) * divu * grads[comp][6]
        for col in range(3):
            total = total + (grads[col][comp] + grads[comp][col]) * grads[col][6]
        rate = lorentz[comp] * inv_rho - advect(comp) - grads[comp][6] + force[comp]
        rate = rate + 0.05 * (viscous[comp] + total)
        if comp == 0:
            rate = rate + vely
        if comp == 1:
            rate = rate - (1.0 + shear_rate) * velx
        rates.append(rate)
    for comp in range(3):
        rate = emf[comp] - flow * grad_y[3 + comp] - 0.05 * curr[comp]
        if comp == 0:
            rate = rate - shear_rate * poty
        rates.append(rate)
    rates.append(-advect(6) - divu)
    return rates


def pack_kernel(cells_x, cells_y, state, held, y_near, y_far, x_near, x_far, sems):
    copies = [
        pltpu.make_async_copy(state.at[field], held.at[field], sems.at[field]) for field in range(7)
    ]
    for copy in copies:
        copy.start()
    y_odd = lax.axis_index("yz") % 2
    x_odd = lax.axis_index("gx") % 2
    for field, copy in enumerate(copies):
        copy.wait()

        def rows(first, then):
            for plane in range(cells_x):
                at = 3 * (field * cells_x + plane)
                first[at : at + 3] = held[field, plane, cells_y - 3 :]
                then[at : at + 3] = held[field, plane, :3]

        def planes(first, then):
            first[field] = held[field, cells_x - 3 :]
            then[field] = held[field, :3]

        pl.when(y_odd == 0)(functools.partial(rows, y_near, y_far))
        pl.when(y_odd == 1)(functools.partial(rows, y_far, y_near))
        pl.when(x_odd == 0)(functools.partial(planes, x_near, x_far))
        pl.when(x_odd == 1)(functools.partial(planes, x_far, x_near))


def side_kernel(
    cells_x, state, weights, y_near, y_far, dz, mixes, side_terms, block, z_block, dzz
):
    own = slice(ROW, ROW + 8)
    y_odd = lax.axis_index("yz") % 2
    for field in range(7):
        got = along_z(state[field].reshape(cells_x * 8, LANES), weights[...])
        dz[field] = (got[:, :LANES] * (1.0 / 60.0)).reshape(cells_x, 8, LANES)
        if field < 5:
            dzz[field] = (got[:, LANES:] * (1.0 / 180.0)).reshape(cells_x, 8, LANES)
        block[field, :, own] = state[field]
    for number, field in enumerate(SHEAR_Z):
        z_block[number, :, own] = dz[field]

    def ghosts(target, rows):
        for field in range(7):
            for plane in range(cells_x):
                at = 3 * (field * cells_x + plane)
                block[field, plane, target : target + 3] = rows[at : at + 3]
        got = along_z(rows[...], weights[:, :LANES]) * (1.0 / 60.0)
        for number, field in enumerate(SHEAR_Z):
            for plane in range(cells_x):
                at = 3 * (field * cells_x + plane)
                z_block[number, plane, target : target + 3] = got[at : at + 3]

    @pl.when(y_odd == 0)
    def _():
        ghosts(ROW + 8, y_near)
        ghosts(ROW - 3, y_far)

    @pl.when(y_odd == 1)
    def _():
        ghosts(ROW - 3, y_near)
        ghosts(ROW + 8, y_far)

    def yz_step(plane, carry):
        def rows_of(field):
            return lambda step: block[field, plane, ROW + step : ROW + 8 + step]

        def z_rows_of(number):
            return lambda step: z_block[number, plane, ROW + step : ROW + 8 + step]

        grad = [first_diff(rows_of(field)) for field in range(7)]
        cross = [first_diff(z_rows_of(number)) for number in range(4)]
        terms = grad + [
            second_diff(rows_of(0)) + dzz[0, plane],
            (4.0 / 3.0) * second_diff(rows_of(1)) + dzz[1, plane] + (1.0 / 3.0) * cross[1],
            second_diff(rows_of(2)) + (4.0 / 3.0) * dzz[2, plane] + (1.0 / 3.0) * cross[0],
            -(second_diff(rows_of(3)) + dzz[3, plane]),
            cross[3] - dzz[4, plane],
            cross[2] - second_diff(rows_of(5)),
        ]
        for number, term in enumerate(terms):
            side_terms[number, plane] = term
        mixes[0, plane] = grad[1] + dz[2, plane]
        mixes[1, plane] = grad[0]
        mixes[2, plane] = dz[0, plane]
        mixes[3, plane] = grad[4] + dz[5, plane]
        mixes[4, plane] = grad[3]
        mixes[5, plane] = dz[3, plane]
        return carry

    lax.fori_loop(0, cells_x, yz_step, 0)


def corner_kernel(slabs_x, x_near, x_far, after, faces, to_next, to_last):
    where_x = lax.axis_index("gx")
    x_odd = where_x % 2

    def order(low, high):
        faces[0] = low[...]
        faces[1] = high[...]

    pl.when(x_odd == 0)(functools.partial(order, x_far, x_near))
    pl.when(x_odd == 1)(functools.partial(order, x_near, x_far))
    for side in range(2):
        for number, field in enumerate(MIXED):
            for plane in range(3):
                at = 3 * (3 * (4 * side + number) + plane)
                to_next[at : at + 3] = faces[side, field, plane, 5:8]
                to_last[at : at + 3] = faces[side, field, plane, 0:3]

    def fill(side):
        for number, field in enumerate(MIXED + PLAIN):
            for plane in range(3):
                at = 72 + 4 * (3 * number + plane)
                row = 1 if field in MIXED else 4
                to_next[at : at + 4] = faces[side, field, plane, row : row + 4]
                row = 3 if field in MIXED else 0
                to_last[at : at + 4] = faces[side, field, plane, row : row + 4]

    pl.when(where_x == 0)(functools.partial(fill, 0))
    pl.when(where_x == slabs_x - 1)(functools.partial(fill, 1))


def finish(inv_width, index, center, force, old, x_parts, side, grad_z):
    grad_x, viscous, curr = x_parts
    rates = rates_of(
        center,
        force,
        index,
        inv_width,
        (grad_x, side[:7], grad_z),
        [viscous[comp] + side[7 + comp] for comp in range(3)],
        [curr[comp] + side[10 + comp] for comp in range(3)],
    )
    fresh = [(-5.0 / 9.0) * old[field] + 0.15 * rates[field] for field in range(7)]
    return [center[field] + (15.0 / 16.0) * fresh[field] for field in range(7)], fresh


def inner_kernel(
    cells_x, inv_width,
    state, register, forcing, dz, mixes, side_terms,
    new_state, new_register,
    fresh_state, fresh_register, sems,
):
    first = lax.axis_index("gx") * cells_x

    def plane_step(plane, carry):
        states, registers = finish(
            inv_width,
            first + plane,
            [state[field, plane] for field in range(7)],
            [forcing[comp, plane] for comp in range(3)],
            [register[field, plane] for field in range(7)],
            x_terms(
                lambda field: lambda step: state[field, plane + step],
                lambda number: lambda step: mixes[number, plane + step],
            ),
            [side_terms[number, plane] for number in range(13)],
            [dz[field, plane] for field in range(7)],
        )
        for field in range(7):
            fresh_register[field, plane] = registers[field]
            fresh_state[field, plane] = states[field]
        return carry

    middle = cells_x // 2
    copies = []
    for number, (begin, end) in enumerate(((3, middle), (middle, cells_x - 3))):
        lax.fori_loop(begin, end, plane_step, 0)
        for which, (fresh, final) in enumerate(((fresh_state, new_state), (fresh_register, new_register))):
            copy = pltpu.make_async_copy(
                fresh.at[:, pl.ds(begin, end - begin)],
                final.at[:, pl.ds(begin, end - begin)],
                sems.at[2 * number + which],
            )
            copy.start()
            copies.append(copy)
    for copy in copies:
        copy.wait()


def edge_kernel(
    cells_x, slabs_x, slabs_y, cells_y, inv_width,
    y_shift, state, register, forcing, weights, dz, mixes, side_terms,
    planes, from_last, from_next, kept_state, kept_register,
    new_state, new_register,
    ghost, faces, face_mixes, fresh_state, fresh_register, sems,
):
    where_x = lax.axis_index("gx")
    first = where_x * cells_x
    lean = (y_shift[0] + cells_y // 2) % cells_y - cells_y // 2
    at_low, at_high = where_x == 0, where_x == slabs_x - 1
    for side in range(2):
        for number, field in enumerate(MIXED):
            for plane in range(3):
                at = 3 * (3 * (4 * side + number) + plane)
                ghost[side, field, plane, 13:16] = from_last[at : at + 3]
                ghost[side, field, plane, 24:27] = from_next[at : at + 3]
        for field in range(7):
            for plane in range(3):
                ghost[side, field, plane, 16:24] = planes[side, field, plane]

    def put(side):
        for number, field in enumerate(MIXED + PLAIN):
            for plane in range(3):
                at = 72 + 4 * (3 * number + plane)
                row = 9 if field in MIXED else 12
                ghost[side, field, plane, row : row + 4] = from_last[at : at + 4]
                row = 27 if field in MIXED else 24
                ghost[side, field, plane, row : row + 4] = from_next[at : at + 4]

    pl.when(at_low)(functools.partial(put, 0))
    pl.when(at_high)(functools.partial(put, 1))
    for side, shift in enumerate((jnp.where(at_low, lean, 0), jnp.where(at_high, -lean, 0))):
        shift = shift + 16
        for field in range(7):
            for plane in range(3):
                faces[side, field, plane] = ghost[side, field, plane, pl.ds(shift, 8)]
        got = along_z(
            jnp.concatenate([faces[side, field].reshape(24, LANES) for field in (0, 2, 3, 5)]),
            weights[:, :LANES],
        ) * (1.0 / 60.0)
        for plane in range(3):
            def rows_of(field):
                return lambda step: ghost[side, field, plane, pl.ds(shift + step, 8)]

            def depth(number):
                return got[24 * number + 8 * plane : 24 * number + 8 * plane + 8]

            face_mixes[side, 0, plane] = first_diff(rows_of(1)) + depth(1)
            face_mixes[side, 1, plane] = first_diff(rows_of(0))
            face_mixes[side, 2, plane] = depth(0)
            face_mixes[side, 3, plane] = first_diff(rows_of(4)) + depth(3)
            face_mixes[side, 4, plane] = first_diff(rows_of(3))
            face_mixes[side, 5, plane] = depth(2)

    copies = []
    for side in range(2):
        begin = side * (cells_x - 3)
        for local in range(3):
            plane = begin + local

            def at(own, far, number, step):
                spot = plane + step
                if spot < 0:
                    return far[0, number, spot + 3]
                if spot >= cells_x:
                    return far[1, number, spot - cells_x]
                return own[number, spot]

            states, registers = finish(
                inv_width,
                first + plane,
                [state[field, plane] for field in range(7)],
                [forcing[comp, plane] for comp in range(3)],
                [register[field, plane] for field in range(7)],
                x_terms(
                    lambda field: lambda step: at(state, faces, field, step),
                    lambda number: lambda step: at(mixes, face_mixes, number, step),
                ),
                [side_terms[number, plane] for number in range(13)],
                [dz[field, plane] for field in range(7)],
            )
            for field in range(7):
                fresh_register[side, field, local] = registers[field]
                fresh_state[side, field, local] = states[field]
        for which, (fresh, final) in enumerate(((fresh_state, new_state), (fresh_register, new_register))):
            copy = pltpu.make_async_copy(
                fresh.at[side], final.at[:, pl.ds(begin, 3)], sems.at[2 * side + which]
            )
            copy.start()
            copies.append(copy)
    for copy in copies:
        copy.wait()


def per_device(slabs_x, slabs_y, state, register, forcing, y_shift):
    cells_x, cells_y = state.shape[1], state.shape[2]
    total_x, total_y = cells_x * slabs_x, cells_y * slabs_y
    steps = (y_shift[0] + cells_y // 2) // cells_y

    def shape(*dims):
        return jax.ShapeDtypeStruct(dims, jnp.float32)

    smem = pl.BlockSpec(memory_space=pltpu.SMEM)
    vmem = pl.BlockSpec(memory_space=pltpu.VMEM)
    anyspace = pl.BlockSpec(memory_space=pl.ANY)
    params = pltpu.CompilerParams(vmem_limit_bytes=VMEM)
    weights = jnp.asarray(z_weights())

    held, y_near, y_far, x_near, x_far = pl.pallas_call(
        functools.partial(pack_kernel, cells_x, cells_y),
        out_shape=[
            shape(*state.shape),
            shape(21 * cells_x, LANES), shape(21 * cells_x, LANES),
            shape(7, 3, cells_y, LANES), shape(7, 3, cells_y, LANES),
        ],
        in_specs=[anyspace],
        out_specs=[vmem] * 5,
        scratch_shapes=[pltpu.SemaphoreType.DMA((7,))],
        compiler_params=params,
    )(state)

    digit = min(slabs_y, 8)

    def place(slab, along):
        return along % slabs_y * slabs_x + slab

    def send(value, pairs):
        return lax.ppermute(value, ("yz", "gx"), pairs)

    def both(pairs):
        return pairs + [(b, a) for a, b in pairs]

    def y_pairs(odd):
        return both(
            [(place(slab, j), place(slab, j + 1)) for slab in range(slabs_x) for j in range(odd, slabs_y, 2)]
        )

    def x_pairs(odd, by):
        return both(
            [
                (place(slab, j + by * (slab == slabs_x - 1)), place((slab + 1) % slabs_x, j))
                for slab in range(odd, slabs_x, 2)
                for j in range(slabs_y)
            ]
        )

    if slabs_y > digit:
        where_x = lax.axis_index("gx")
        at_low, at_high = where_x == 0, where_x == slabs_x - 1
        groups = steps // digit
        amount = jnp.where(at_high, groups, slabs_y // digit - groups) % (slabs_y // digit)
        across = x_far
        hop = 1
        while hop < slabs_y // digit:
            pairs = [(i, (i - hop * digit) % slabs_y) for i in range(slabs_y)]
            moved = lax.ppermute(across, "yz", pairs)
            across = jnp.where((amount // hop) % 2 == 1, moved, across)
            hop *= 2
        x_far = jnp.where(at_low | at_high, across, x_far)

    def exchange(by, operands):
        y_near, y_far, x_near, x_far, state, weights = operands
        y_near = send(y_near, y_pairs(0))
        x_near = send(x_near, x_pairs(0, 0))
        x_far = send(x_far, x_pairs(1, by))
        y_far = send(y_far, y_pairs(1))
        terms = pl.pallas_call(
            functools.partial(side_kernel, cells_x),
            out_shape=[shape(*state.shape), shape(6, *state.shape[1:]), shape(13, *state.shape[1:])],
            in_specs=[vmem] * 4,
            out_specs=[vmem] * 3,
            scratch_shapes=[
                pltpu.VMEM((7, cells_x, TALL, LANES), jnp.float32),
                pltpu.VMEM((4, cells_x, TALL, LANES), jnp.float32),
                pltpu.VMEM((5, *state.shape[1:]), jnp.float32),
            ],
            compiler_params=params,
            cost_estimate=pl.CostEstimate(flops=2 * 10**8, bytes_accessed=10**6, transcendentals=0),
        )(state, weights, y_near, y_far)
        corners = pl.pallas_call(
            functools.partial(corner_kernel, slabs_x),
            out_shape=[shape(2, *x_near.shape), shape(160, LANES), shape(160, LANES)],
            in_specs=[vmem] * 2 + [anyspace],
            out_specs=[vmem] * 3,
            compiler_params=params,
        )(x_near, x_far, terms[2])
        return (*terms, *corners)

    dz, mixes, side_terms, faces, to_next, to_last = lax.switch(
        steps % digit,
        [functools.partial(exchange, by) for by in range(digit)],
        (y_near, y_far, x_near, x_far, held, weights),
    )
    beside = [
        [(place(slab, j), place(slab, j + along)) for slab in range(slabs_x) for j in range(slabs_y)]
        for along in (1, -1)
    ]
    from_last = send(to_next, beside[0])
    from_next = send(to_last, beside[1])

    new_state, new_register = pl.pallas_call(
        functools.partial(inner_kernel, cells_x, 1.0 / total_x),
        out_shape=[shape(*state.shape)] * 2,
        in_specs=[vmem] * 6,
        out_specs=[anyspace] * 2,
        scratch_shapes=[
            pltpu.VMEM(state.shape, jnp.float32),
            pltpu.VMEM(state.shape, jnp.float32),
            pltpu.SemaphoreType.DMA((4,)),
        ],
        compiler_params=params,
        cost_estimate=pl.CostEstimate(flops=2 * 10**8, bytes_accessed=2 * 10**6, transcendentals=0),
    )(held, register, forcing, dz, mixes, side_terms)

    return pl.pallas_call(
        functools.partial(edge_kernel, cells_x, slabs_x, slabs_y, cells_y, 1.0 / total_x),
        out_shape=[shape(*state.shape)] * 2,
        in_specs=[smem] + [vmem] * 10 + [anyspace] * 2,
        out_specs=[anyspace] * 2,
        input_output_aliases={11: 0, 12: 1},
        scratch_shapes=[
            pltpu.VMEM((2, 7, 3, 40, LANES), jnp.float32),
            pltpu.VMEM((2, 7, 3, 8, LANES), jnp.float32),
            pltpu.VMEM((2, 6, 3, 8, LANES), jnp.float32),
            pltpu.VMEM((2, 7, 3, 8, LANES), jnp.float32),
            pltpu.VMEM((2, 7, 3, 8, LANES), jnp.float32),
            pltpu.SemaphoreType.DMA((4,)),
        ],
        compiler_params=params,
    )(
        y_shift, held, register, forcing, weights, dz, mixes, side_terms,
        faces, from_last, from_next, new_state, new_register,
    )


def solution(mesh):
    spec = P(None, "gx", "yz", None)
    return jax.shard_map(
        functools.partial(per_device, mesh.shape["gx"], mesh.shape["yz"]),
        mesh=mesh,
        in_specs=(spec, spec, spec, P()),
        out_specs=(spec, spec),
        check_vma=False,
    )
```

```python
import functools

import jax
import jax.numpy as jnp
import numpy as np
from jax import lax
from jax.experimental import pallas as pl
from jax.experimental.pallas import tpu as pltpu
from jax.sharding import PartitionSpec as P

LANES = 128
FIRST = ((1, 45.0), (2, -9.0), (3, 1.0))
SECOND = ((1, 270.0), (2, -27.0), (3, 2.0))
MIXED = (0, 1, 3, 4)
PLAIN = (2, 5, 6)
SHEAR_Z = (1, 2, 4, 5)
ROW = 8
CORNER = 10**10
EARLY = 4
TALL = 24
VMEM = 32 * 1024 * 1024


def z_weights():
    one = np.zeros((LANES, 2 * LANES), np.float32)
    cells = np.arange(LANES)
    one[cells, LANES + cells] = -490.0
    for step, weight in FIRST:
        one[(cells + step) % LANES, cells] += weight
        one[(cells - step) % LANES, cells] -= weight
    for step, weight in SECOND:
        one[(cells + step) % LANES, LANES + cells] += weight
        one[(cells - step) % LANES, LANES + cells] += weight
    return np.concatenate([one, one]).astype(jnp.bfloat16)


def along_z(value, weights):
    upper = value.astype(jnp.bfloat16)
    rest = (value - upper.astype(jnp.float32)).astype(jnp.bfloat16)
    return jnp.dot(
        jnp.concatenate([upper, rest], axis=1), weights, preferred_element_type=jnp.float32
    )


def first_diff(part):
    return (
        0.75 * (part(1) - part(-1))
        - 0.15 * (part(2) - part(-2))
        + (1.0 / 60.0) * (part(3) - part(-3))
    )


def second_diff(part):
    return (
        (-490.0 / 180.0) * part(0)
        + 1.5 * (part(1) + part(-1))
        - 0.15 * (part(2) + part(-2))
        + (1.0 / 90.0) * (part(3) + part(-3))
    )


def x_terms(planes_of, mixes_of):
    grad = [first_diff(planes_of(field)) for field in range(7)]
    mix = [first_diff(mixes_of(number)) for number in range(6)]
    viscous = (
        (4.0 / 3.0) * second_diff(planes_of(0)) + (1.0 / 3.0) * mix[0],
        second_diff(planes_of(1)) + (1.0 / 3.0) * mix[1],
        second_diff(planes_of(2)) + (1.0 / 3.0) * mix[2],
    )
    current = (
        mix[3],
        mix[4] - second_diff(planes_of(4)),
        mix[5] - second_diff(planes_of(5)),
    )
    return grad, viscous, current


def rates_of(center, force, index, inv_width, grads, viscous, curr):
    velx, vely, velz, potx, poty, potz, logr = center
    grad_x, grad_y, grad_z = grads
    field_x = grad_y[5] - grad_z[4]
    field_y = grad_z[3] - grad_x[5]
    field_z = grad_x[4] - grad_y[3] + 0.5
    lorentz = (
        curr[1] * field_z - curr[2] * field_y,
        curr[2] * field_x - curr[0] * field_z,
        curr[0] * field_y - curr[1] * field_x,
    )
    emf = (
        vely * field_z - velz * field_y,
        velz * field_x - velx * field_z,
        velx * field_y - vely * field_x,
    )
    inv_rho = jnp.exp(-logr)
    flow = -1.5 * ((index.astype(jnp.float32) + 0.5) * inv_width - 0.5)
    shear_rate = -1.5 * inv_width
    carried = vely + flow
    divu = grad_x[0] + grad_y[1] + grad_z[2]

    def advect(comp):
        return velx * grad_x[comp] + carried * grad_y[comp] + velz * grad_z[comp]

    rates = []
    for comp in range(3):
        total = (-2.0 / 3.0) * divu * grads[comp][6]
        for col in range(3):
            total = total + (grads[col][comp] + grads[comp][col]) * grads[col][6]
        rate = lorentz[comp] * inv_rho - advect(comp) - grads[comp][6] + force[comp]
        rate = rate + 0.05 * (viscous[comp] + total)
        if comp == 0:
            rate = rate + vely
        if comp == 1:
            rate = rate - (1.0 + shear_rate) * velx
        rates.append(rate)
    for comp in range(3):
        rate = emf[comp] - flow * grad_y[3 + comp] - 0.05 * curr[comp]
        if comp == 0:
            rate = rate - shear_rate * poty
        rates.append(rate)
    rates.append(-advect(6) - divu)
    return rates


def pack_kernel(cells_x, cells_y, state, held, y_near, y_far, x_near, x_far, sems):
    copies = [
        pltpu.make_async_copy(state.at[field], held.at[field], sems.at[field]) for field in range(7)
    ]
    for copy in copies:
        copy.start()
    y_odd = lax.axis_index("yz") % 2
    x_odd = lax.axis_index("gx") % 2
    for field, copy in enumerate(copies):
        copy.wait()

        def rows(first, then):
            for plane in range(cells_x):
                at = 3 * (field * cells_x + plane)
                first[at : at + 3] = held[field, plane, cells_y - 3 :]
                then[at : at + 3] = held[field, plane, :3]

        def planes(first, then):
            first[field] = held[field, cells_x - 3 :]
            then[field] = held[field, :3]

        pl.when(y_odd == 0)(functools.partial(rows, y_near, y_far))
        pl.when(y_odd == 1)(functools.partial(rows, y_far, y_near))
        pl.when(x_odd == 0)(functools.partial(planes, x_near, x_far))
        pl.when(x_odd == 1)(functools.partial(planes, x_far, x_near))


def own_z_kernel(cells_x, state, weights, dz, dzz):
    got = along_z(state[...].reshape(7 * cells_x * 8, LANES), weights[...])
    dz[...] = (got[:, :LANES] * (1.0 / 60.0)).reshape(7, cells_x, 8, LANES)
    dzz[...] = (got[: 5 * cells_x * 8, LANES:] * (1.0 / 180.0)).reshape(5, cells_x, 8, LANES)


def side_kernel(
    cells_x, state, weights, y_near, y_far, dz, dzz, mixes, side_terms, block, z_block
):
    own = slice(ROW, ROW + 8)
    y_odd = lax.axis_index("yz") % 2
    block[:, :, own] = state[...]
    for number, field in enumerate(SHEAR_Z):
        z_block[number, :, own] = dz[field]
    count = 3 * cells_x
    got = along_z(
        jnp.concatenate(
            [rows[field * count : (field + 1) * count] for rows in (y_near, y_far) for field in SHEAR_Z]
        ),
        weights[:, :LANES],
    ) * (1.0 / 60.0)

    def ghosts(target, rows, begin):
        for field in range(7):
            for plane in range(cells_x):
                at = 3 * (field * cells_x + plane)
                block[field, plane, target : target + 3] = rows[at : at + 3]
        for number in range(4):
            for plane in range(cells_x):
                at = begin + 3 * (number * cells_x + plane)
                z_block[number, plane, target : target + 3] = got[at : at + 3]

    @pl.when(y_odd == 0)
    def _():
        ghosts(ROW + 8, y_near, 0)
        ghosts(ROW - 3, y_far, 4 * count)

    @pl.when(y_odd == 1)
    def _():
        ghosts(ROW - 3, y_near, 0)
        ghosts(ROW + 8, y_far, 4 * count)

    def yz_step(plane):
        def rows_of(field):
            return lambda step: block[field, plane, ROW + step : ROW + 8 + step]

        def z_rows_of(number):
            return lambda step: z_block[number, plane, ROW + step : ROW + 8 + step]

        grad = [first_diff(rows_of(field)) for field in range(7)]
        cross = [first_diff(z_rows_of(number)) for number in range(4)]
        terms = grad + [
            second_diff(rows_of(0)) + dzz[0, plane],
            (4.0 / 3.0) * second_diff(rows_of(1)) + dzz[1, plane] + (1.0 / 3.0) * cross[1],
            second_diff(rows_of(2)) + (4.0 / 3.0) * dzz[2, plane] + (1.0 / 3.0) * cross[0],
            -(second_diff(rows_of(3)) + dzz[3, plane]),
            cross[3] - dzz[4, plane],
            cross[2] - second_diff(rows_of(5)),
        ]
        for number, term in enumerate(terms):
            side_terms[number, plane] = term
        mixes[0, plane] = grad[1] + dz[2, plane]
        mixes[1, plane] = grad[0]
        mixes[2, plane] = dz[0, plane]
        mixes[3, plane] = grad[4] + dz[5, plane]
        mixes[4, plane] = grad[3]
        mixes[5, plane] = dz[3, plane]

    in_pairs(0, cells_x, yz_step)


def in_pairs(begin, end, step):
    def two(number, carry):
        step(begin + 2 * number)
        step(begin + 2 * number + 1)
        return carry

    lax.fori_loop(0, (end - begin) // 2, two, 0)


def corner_kernel(slabs_x, x_near, x_far, after, faces, to_next, to_last):
    where_x = lax.axis_index("gx")
    x_odd = where_x % 2

    def order(low, high):
        faces[0] = low[...]
        faces[1] = high[...]

    pl.when(x_odd == 0)(functools.partial(order, x_far, x_near))
    pl.when(x_odd == 1)(functools.partial(order, x_near, x_far))
    for side in range(2):
        for number, field in enumerate(MIXED):
            for plane in range(3):
                at = 3 * (3 * (4 * side + number) + plane)
                to_next[at : at + 3] = faces[side, field, plane, 5:8]
                to_last[at : at + 3] = faces[side, field, plane, 0:3]

    def fill(side):
        for number, field in enumerate(MIXED + PLAIN):
            for plane in range(3):
                at = 72 + 4 * (3 * number + plane)
                row = 1 if field in MIXED else 4
                to_next[at : at + 4] = faces[side, field, plane, row : row + 4]
                row = 3 if field in MIXED else 0
                to_last[at : at + 4] = faces[side, field, plane, row : row + 4]

    pl.when(where_x == 0)(functools.partial(fill, 0))
    pl.when(where_x == slabs_x - 1)(functools.partial(fill, 1))


def finish(inv_width, index, center, force, old, x_parts, side, grad_z):
    grad_x, viscous, curr = x_parts
    rates = rates_of(
        center,
        force,
        index,
        inv_width,
        (grad_x, side[:7], grad_z),
        [viscous[comp] + side[7 + comp] for comp in range(3)],
        [curr[comp] + side[10 + comp] for comp in range(3)],
    )
    fresh = [(-5.0 / 9.0) * old[field] + 0.15 * rates[field] for field in range(7)]
    return [center[field] + (15.0 / 16.0) * fresh[field] for field in range(7)], fresh


def inner_kernel(
    cells_x, inv_width,
    state, register, forcing, dz, mixes, side_terms,
    new_state, new_register, late_state, late_register,
    fresh_state, fresh_register, sems,
):
    first = lax.axis_index("gx") * cells_x
    early = EARLY

    def step_into(states_out, registers_out, begin):
        def plane_step(plane):
            states, registers = finish(
                inv_width,
                first + plane,
                [state[field, plane] for field in range(7)],
                [forcing[comp, plane] for comp in range(3)],
                [register[field, plane] for field in range(7)],
                x_terms(
                    lambda field: lambda step: state[field, plane + step],
                    lambda number: lambda step: mixes[number, plane + step],
                ),
                [side_terms[number, plane] for number in range(13)],
                [dz[field, plane] for field in range(7)],
            )
            for field in range(7):
                registers_out[field, plane - begin] = registers[field]
                states_out[field, plane - begin] = states[field]

        return plane_step

    in_pairs(3, 3 + early, step_into(fresh_state, fresh_register, 3))
    copies = [
        pltpu.make_async_copy(fresh, final.at[:, pl.ds(3, early)], sems.at[which])
        for which, (fresh, final) in enumerate(((fresh_state, new_state), (fresh_register, new_register)))
    ]
    for copy in copies:
        copy.start()
    in_pairs(3 + early, cells_x - 3, step_into(late_state, late_register, 3 + early))
    for copy in copies:
        copy.wait()


def edge_kernel(
    cells_x, slabs_x, cells_y, inv_width,
    y_shift, state, register, forcing, weights, dz, mixes, side_terms,
    planes, from_last, from_next, late_state, late_register, kept_state, kept_register,
    new_state, new_register,
    ghost, fields, mixed, fresh_state, fresh_register, sems,
):
    late = [
        pltpu.make_async_copy(part, final.at[:, pl.ds(3 + EARLY, cells_x - 6 - EARLY)], sems.at[4 + which])
        for which, (part, final) in enumerate(((late_state, new_state), (late_register, new_register)))
    ]
    for copy in late:
        copy.start()
    where_x = lax.axis_index("gx")
    first = where_x * cells_x
    lean = (y_shift[0] + cells_y // 2) % cells_y - cells_y // 2
    at_low, at_high = where_x == 0, where_x == slabs_x - 1
    for field in range(7):
        fields[0, field, 3:9] = state[field, 0:6]
        fields[1, field, 0:6] = state[field, cells_x - 6 :]
    for number in range(6):
        mixed[0, number, 3:9] = mixes[number, 0:6]
        mixed[1, number, 0:6] = mixes[number, cells_x - 6 :]
    for side in range(2):
        for number, field in enumerate(MIXED):
            for plane in range(3):
                at = 3 * (3 * (4 * side + number) + plane)
                ghost[side, field, plane, 13:16] = from_last[at : at + 3]
                ghost[side, field, plane, 24:27] = from_next[at : at + 3]
        for field in range(7):
            for plane in range(3):
                ghost[side, field, plane, 16:24] = planes[side, field, plane]

    def put(side):
        for number, field in enumerate(MIXED + PLAIN):
            for plane in range(3):
                at = 72 + 4 * (3 * number + plane)
                row = 9 if field in MIXED else 12
                ghost[side, field, plane, row : row + 4] = from_last[at : at + 4]
                row = 27 if field in MIXED else 24
                ghost[side, field, plane, row : row + 4] = from_next[at : at + 4]

    pl.when(at_low)(functools.partial(put, 0))
    pl.when(at_high)(functools.partial(put, 1))
    for side, shift in enumerate((jnp.where(at_low, lean, 0), jnp.where(at_high, -lean, 0))):
        for field in range(7):
            for plane in range(3):
                low = ghost[side, field, plane, pl.ds(shift + 13, 8)]
                if field in MIXED:
                    high = ghost[side, field, plane, pl.ds(shift + 21, 8)]
                    ghost[side, field, plane, 0:8] = low
                    ghost[side, field, plane, 8:16] = high
                    fields[side, field, plane + 6 * side] = ghost[side, field, plane, 3:11]
                else:
                    fields[side, field, plane + 6 * side] = ghost[side, field, plane, pl.ds(shift + 16, 8)]
    used = (0, 2, 3, 5)
    got = along_z(
        jnp.concatenate(
            [
                fields[side, field, 6 * side : 6 * side + 3].reshape(24, LANES)
                for side in range(2)
                for field in used
            ]
        ),
        weights[:, :LANES],
    ) * (1.0 / 60.0)
    for side in range(2):
        for plane in range(3):
            def rows_of(field):
                return lambda step: ghost[side, field, plane, 3 + step : 11 + step]

            def depth(field):
                at = 24 * (4 * side + used.index(field)) + 8 * plane
                return got[at : at + 8]

            spot = plane + 6 * side
            mixed[side, 0, spot] = first_diff(rows_of(1)) + depth(2)
            mixed[side, 1, spot] = first_diff(rows_of(0))
            mixed[side, 2, spot] = depth(0)
            mixed[side, 3, spot] = first_diff(rows_of(4)) + depth(5)
            mixed[side, 4, spot] = first_diff(rows_of(3))
            mixed[side, 5, spot] = depth(3)

    def copies_of(side):
        return [
            pltpu.make_async_copy(
                fresh.at[side], final.at[:, pl.ds(side * (cells_x - 3), 3)], sems.at[2 * side + which]
            )
            for which, (fresh, final) in enumerate(((fresh_state, new_state), (fresh_register, new_register)))
        ]

    for side in range(2):
        for local in range(3):
            plane = side * (cells_x - 3) + local
            states, registers = finish(
                inv_width,
                first + plane,
                [state[field, plane] for field in range(7)],
                [forcing[comp, plane] for comp in range(3)],
                [register[field, plane] for field in range(7)],
                x_terms(
                    lambda field: lambda step: fields[side, field, local + 3 + step],
                    lambda number: lambda step: mixed[side, number, local + 3 + step],
                ),
                [side_terms[number, plane] for number in range(13)],
                [dz[field, plane] for field in range(7)],
            )
            for field in range(7):
                fresh_register[side, field, local] = registers[field]
                fresh_state[side, field, local] = states[field]
        for copy in copies_of(side):
            copy.start()
    for copy in late + copies_of(0) + copies_of(1):
        copy.wait()


def per_device(slabs_x, slabs_y, state, register, forcing, y_shift):
    cells_x, cells_y = state.shape[1], state.shape[2]
    total_x, total_y = cells_x * slabs_x, cells_y * slabs_y
    steps = (y_shift[0] + cells_y // 2) // cells_y

    def shape(*dims):
        return jax.ShapeDtypeStruct(dims, jnp.float32)

    smem = pl.BlockSpec(memory_space=pltpu.SMEM)
    vmem = pl.BlockSpec(memory_space=pltpu.VMEM)
    anyspace = pl.BlockSpec(memory_space=pl.ANY)
    params = pltpu.CompilerParams(vmem_limit_bytes=VMEM)
    weights = jnp.asarray(z_weights())

    held, y_near, y_far, x_near, x_far = pl.pallas_call(
        functools.partial(pack_kernel, cells_x, cells_y),
        out_shape=[
            shape(*state.shape),
            shape(21 * cells_x, LANES), shape(21 * cells_x, LANES),
            shape(7, 3, cells_y, LANES), shape(7, 3, cells_y, LANES),
        ],
        in_specs=[pl.BlockSpec(memory_space=pltpu.HBM)],
        out_specs=[vmem] * 5,
        scratch_shapes=[pltpu.SemaphoreType.DMA((7,))],
        compiler_params=params,
    )(pltpu.with_memory_space_constraint(state, pltpu.HBM))

    digit = min(slabs_y, 8)

    def place(slab, along):
        return along % slabs_y * slabs_x + slab

    def send(value, pairs):
        return lax.ppermute(value, ("yz", "gx"), pairs)

    def both(pairs):
        return pairs + [(b, a) for a, b in pairs]

    def y_pairs(odd):
        return both(
            [(place(slab, j), place(slab, j + 1)) for slab in range(slabs_x) for j in range(odd, slabs_y, 2)]
        )

    def x_pairs(odd, by):
        return both(
            [
                (place(slab, j + by * (slab == slabs_x - 1)), place((slab + 1) % slabs_x, j))
                for slab in range(odd, slabs_x, 2)
                for j in range(slabs_y)
            ]
        )

    if slabs_y > digit:
        where_x = lax.axis_index("gx")
        at_low, at_high = where_x == 0, where_x == slabs_x - 1
        groups = steps // digit
        amount = jnp.where(at_high, groups, slabs_y // digit - groups) % (slabs_y // digit)
        across = x_far
        hop = 1
        while hop < slabs_y // digit:
            pairs = [(i, (i - hop * digit) % slabs_y) for i in range(slabs_y)]
            moved = lax.ppermute(across, "yz", pairs)
            across = jnp.where((amount // hop) % 2 == 1, moved, across)
            hop *= 2
        x_far = jnp.where(at_low | at_high, across, x_far)

    beside = [
        [(place(slab, j), place(slab, j + along)) for slab in range(slabs_x) for j in range(slabs_y)]
        for along in (1, -1)
    ]

    def cost(flops):
        return pl.CostEstimate(flops=flops, bytes_accessed=10**6, transcendentals=0)

    def exchange(by, operands):
        y_near, y_far, x_near, x_far, state, register, forcing, weights, y_shift = operands
        plane = state.shape[1:]
        x_far = send(x_far, x_pairs(1, by))
        x_near = send(x_near, x_pairs(0, 0))
        y_near = send(y_near, y_pairs(0))
        y_far = send(y_far, y_pairs(1))
        dz, dzz = pl.pallas_call(
            functools.partial(own_z_kernel, cells_x),
            out_shape=[shape(7, *plane), shape(5, *plane)],
            in_specs=[vmem] * 2,
            out_specs=[vmem] * 2,
            compiler_params=params,
            cost_estimate=cost(10**8),
        )(state, weights)
        faces, to_next, to_last = pl.pallas_call(
            functools.partial(corner_kernel, slabs_x),
            out_shape=[shape(2, *x_near.shape), shape(160, LANES), shape(160, LANES)],
            in_specs=[vmem] * 2 + [anyspace],
            out_specs=[vmem] * 3,
            compiler_params=params,
            cost_estimate=cost(CORNER),
        )(x_near, x_far, dz)
        from_last = send(to_next, beside[0])
        from_next = send(to_last, beside[1])
        mixes, side_terms = pl.pallas_call(
            functools.partial(side_kernel, cells_x),
            out_shape=[shape(6, *plane), shape(13, *plane)],
            in_specs=[vmem] * 6,
            out_specs=[vmem] * 2,
            scratch_shapes=[
                pltpu.VMEM((7, cells_x, TALL, LANES), jnp.float32),
                pltpu.VMEM((4, cells_x, TALL, LANES), jnp.float32),
            ],
            compiler_params=params,
            cost_estimate=cost(2 * 10**8),
        )(state, weights, y_near, y_far, dz, dzz)
        early, late = EARLY, cells_x - 6 - EARLY
        new_state, new_register, late_state, late_register = pl.pallas_call(
            functools.partial(inner_kernel, cells_x, 1.0 / total_x),
            out_shape=[shape(*state.shape)] * 2 + [shape(7, late, *plane[1:])] * 2,
            in_specs=[vmem] * 6,
            out_specs=[anyspace] * 2 + [vmem] * 2,
            scratch_shapes=[
                pltpu.VMEM((7, early, *plane[1:]), jnp.float32),
                pltpu.VMEM((7, early, *plane[1:]), jnp.float32),
                pltpu.SemaphoreType.DMA((2,)),
            ],
            compiler_params=params,
            cost_estimate=cost(2 * 10**8),
        )(state, register, forcing, dz, mixes, side_terms)
        return pl.pallas_call(
            functools.partial(edge_kernel, cells_x, slabs_x, cells_y, 1.0 / total_x),
            out_shape=[shape(*state.shape)] * 2,
            in_specs=[smem] + [vmem] * 12 + [anyspace] * 2,
            out_specs=[anyspace] * 2,
            input_output_aliases={13: 0, 14: 1},
            scratch_shapes=[
                pltpu.VMEM((2, 7, 3, 40, LANES), jnp.float32),
                pltpu.VMEM((2, 7, 9, 8, LANES), jnp.float32),
                pltpu.VMEM((2, 6, 9, 8, LANES), jnp.float32),
                pltpu.VMEM((2, 7, 3, 8, LANES), jnp.float32),
                pltpu.VMEM((2, 7, 3, 8, LANES), jnp.float32),
                pltpu.SemaphoreType.DMA((6,)),
            ],
            compiler_params=params,
        )(
            y_shift, state, register, forcing, weights, dz, mixes, side_terms,
            faces, from_last, from_next, late_state, late_register, new_state, new_register,
        )

    return lax.switch(
        steps % digit,
        [functools.partial(exchange, by) for by in range(digit)],
        (y_near, y_far, x_near, x_far, held, register, forcing, weights, y_shift),
    )


def solution(mesh):
    spec = P(None, "gx", "yz", None)
    return jax.shard_map(
        functools.partial(per_device, mesh.shape["gx"], mesh.shape["yz"]),
        mesh=mesh,
        in_specs=(spec, spec, spec, P()),
        out_specs=(spec, spec),
        check_vma=False,
    )
```

```python
import functools

import jax
import jax.numpy as jnp
import numpy as np
from jax import lax
from jax.experimental import pallas as pl
from jax.experimental.pallas import tpu as pltpu
from jax.sharding import PartitionSpec as P

LANES = 128
FIRST = ((1, 45.0), (2, -9.0), (3, 1.0))
SECOND = ((1, 270.0), (2, -27.0), (3, 2.0))
MIXED = (0, 1, 3, 4)
PLAIN = (2, 5, 6)
SHEAR_Z = (1, 2, 4, 5)
ROW = 8
CORNER = 10**10
EARLY = 4
TALL = 24
VMEM = 32 * 1024 * 1024


def z_weights():
    one = np.zeros((LANES, 2 * LANES), np.float32)
    cells = np.arange(LANES)
    one[cells, LANES + cells] = -490.0
    for step, weight in FIRST:
        one[(cells + step) % LANES, cells] += weight
        one[(cells - step) % LANES, cells] -= weight
    for step, weight in SECOND:
        one[(cells + step) % LANES, LANES + cells] += weight
        one[(cells - step) % LANES, LANES + cells] += weight
    return np.concatenate([one, one]).astype(jnp.bfloat16)


def along_z(value, weights):
    upper = value.astype(jnp.bfloat16)
    rest = (value - upper.astype(jnp.float32)).astype(jnp.bfloat16)
    return jnp.dot(
        jnp.concatenate([upper, rest], axis=1), weights, preferred_element_type=jnp.float32
    )


def first_diff(part):
    return (
        0.75 * (part(1) - part(-1))
        - 0.15 * (part(2) - part(-2))
        + (1.0 / 60.0) * (part(3) - part(-3))
    )


def second_diff(part):
    return (
        (-490.0 / 180.0) * part(0)
        + 1.5 * (part(1) + part(-1))
        - 0.15 * (part(2) + part(-2))
        + (1.0 / 90.0) * (part(3) + part(-3))
    )


def x_terms(planes_of, mixes_of):
    grad = [first_diff(planes_of(field)) for field in range(7)]
    mix = [first_diff(mixes_of(number)) for number in range(6)]
    viscous = (
        (4.0 / 3.0) * second_diff(planes_of(0)) + (1.0 / 3.0) * mix[0],
        second_diff(planes_of(1)) + (1.0 / 3.0) * mix[1],
        second_diff(planes_of(2)) + (1.0 / 3.0) * mix[2],
    )
    current = (
        mix[3],
        mix[4] - second_diff(planes_of(4)),
        mix[5] - second_diff(planes_of(5)),
    )
    return grad, viscous, current


def rates_of(center, force, index, inv_width, grads, viscous, curr):
    velx, vely, velz, potx, poty, potz, logr = center
    grad_x, grad_y, grad_z = grads
    field_x = grad_y[5] - grad_z[4]
    field_y = grad_z[3] - grad_x[5]
    field_z = grad_x[4] - grad_y[3] + 0.5
    lorentz = (
        curr[1] * field_z - curr[2] * field_y,
        curr[2] * field_x - curr[0] * field_z,
        curr[0] * field_y - curr[1] * field_x,
    )
    emf = (
        vely * field_z - velz * field_y,
        velz * field_x - velx * field_z,
        velx * field_y - vely * field_x,
    )
    inv_rho = jnp.exp(-logr)
    flow = -1.5 * ((index.astype(jnp.float32) + 0.5) * inv_width - 0.5)
    shear_rate = -1.5 * inv_width
    carried = vely + flow
    divu = grad_x[0] + grad_y[1] + grad_z[2]

    def advect(comp):
        return velx * grad_x[comp] + carried * grad_y[comp] + velz * grad_z[comp]

    rates = []
    for comp in range(3):
        total = (-2.0 / 3.0) * divu * grads[comp][6]
        for col in range(3):
            total = total + (grads[col][comp] + grads[comp][col]) * grads[col][6]
        rate = lorentz[comp] * inv_rho - advect(comp) - grads[comp][6] + force[comp]
        rate = rate + 0.05 * (viscous[comp] + total)
        if comp == 0:
            rate = rate + vely
        if comp == 1:
            rate = rate - (1.0 + shear_rate) * velx
        rates.append(rate)
    for comp in range(3):
        rate = emf[comp] - flow * grad_y[3 + comp] - 0.05 * curr[comp]
        if comp == 0:
            rate = rate - shear_rate * poty
        rates.append(rate)
    rates.append(-advect(6) - divu)
    return rates


def face_kernel(cells_x, cells_y, state, weights, y_shift, up, down, held, lean, scalar, sems):
    shift = pltpu.make_async_copy(y_shift, scalar, sems.at[3])
    copies = [
        pltpu.make_async_copy(state.at[:, pl.ds(cells_x - 3, 3)], up, sems.at[0]),
        pltpu.make_async_copy(state.at[:, pl.ds(0, 3)], down, sems.at[1]),
        pltpu.make_async_copy(weights, held, sems.at[2]),
    ]
    shift.start()
    for copy in copies:
        copy.start()
    shift.wait()
    rows = (scalar[0] + cells_y // 2) % cells_y - cells_y // 2
    lean[...] = jnp.full(lean.shape, rows, jnp.int32)
    for copy in copies:
        copy.wait()


def row_kernel(cells_x, cells_y, state, y_near, y_far):
    y_odd = lax.axis_index("yz") % 2

    def rows(first, then):
        for field in range(7):
            for plane in range(cells_x):
                at = 3 * (field * cells_x + plane)
                first[at : at + 3] = state[field, plane, cells_y - 3 :]
                then[at : at + 3] = state[field, plane, :3]

    pl.when(y_odd == 0)(functools.partial(rows, y_near, y_far))
    pl.when(y_odd == 1)(functools.partial(rows, y_far, y_near))


def own_z_kernel(cells_x, state, weights, dz, dzz):
    got = along_z(state[...].reshape(7 * cells_x * 8, LANES), weights[...])
    dz[...] = (got[:, :LANES] * (1.0 / 60.0)).reshape(7, cells_x, 8, LANES)
    dzz[...] = (got[: 5 * cells_x * 8, LANES:] * (1.0 / 180.0)).reshape(5, cells_x, 8, LANES)


def side_kernel(
    cells_x, state, weights, y_near, y_far, dz, dzz, mixes, side_terms, block, z_block
):
    own = slice(ROW, ROW + 8)
    y_odd = lax.axis_index("yz") % 2
    block[:, :, own] = state[...]
    for number, field in enumerate(SHEAR_Z):
        z_block[number, :, own] = dz[field]
    count = 3 * cells_x
    got = along_z(
        jnp.concatenate(
            [rows[field * count : (field + 1) * count] for rows in (y_near, y_far) for field in SHEAR_Z]
        ),
        weights[:, :LANES],
    ) * (1.0 / 60.0)

    def ghosts(target, rows, begin):
        for field in range(7):
            for plane in range(cells_x):
                at = 3 * (field * cells_x + plane)
                block[field, plane, target : target + 3] = rows[at : at + 3]
        for number in range(4):
            for plane in range(cells_x):
                at = begin + 3 * (number * cells_x + plane)
                z_block[number, plane, target : target + 3] = got[at : at + 3]

    @pl.when(y_odd == 0)
    def _():
        ghosts(ROW + 8, y_near, 0)
        ghosts(ROW - 3, y_far, 4 * count)

    @pl.when(y_odd == 1)
    def _():
        ghosts(ROW - 3, y_near, 0)
        ghosts(ROW + 8, y_far, 4 * count)

    def yz_step(plane):
        def rows_of(field):
            return lambda step: block[field, plane, ROW + step : ROW + 8 + step]

        def z_rows_of(number):
            return lambda step: z_block[number, plane, ROW + step : ROW + 8 + step]

        grad = [first_diff(rows_of(field)) for field in range(7)]
        cross = [first_diff(z_rows_of(number)) for number in range(4)]
        terms = grad + [
            second_diff(rows_of(0)) + dzz[0, plane],
            (4.0 / 3.0) * second_diff(rows_of(1)) + dzz[1, plane] + (1.0 / 3.0) * cross[1],
            second_diff(rows_of(2)) + (4.0 / 3.0) * dzz[2, plane] + (1.0 / 3.0) * cross[0],
            -(second_diff(rows_of(3)) + dzz[3, plane]),
            cross[3] - dzz[4, plane],
            cross[2] - second_diff(rows_of(5)),
        ]
        for number, term in enumerate(terms):
            side_terms[number, plane] = term
        mixes[0, plane] = grad[1] + dz[2, plane]
        mixes[1, plane] = grad[0]
        mixes[2, plane] = dz[0, plane]
        mixes[3, plane] = grad[4] + dz[5, plane]
        mixes[4, plane] = grad[3]
        mixes[5, plane] = dz[3, plane]

    in_pairs(0, cells_x, yz_step)


def in_pairs(begin, end, step):
    def two(number, carry):
        step(begin + 2 * number)
        step(begin + 2 * number + 1)
        return carry

    lax.fori_loop(0, (end - begin) // 2, two, 0)


def corner_kernel(slabs_x, x_low, x_high, after, faces, near, far):
    where_x = lax.axis_index("gx")
    y_odd = lax.axis_index("yz") % 2
    faces[0] = x_low[...]
    faces[1] = x_high[...]

    def fill(to_next, to_last):
        for side in range(2):
            for number, field in enumerate(MIXED):
                for plane in range(3):
                    at = 3 * (3 * (4 * side + number) + plane)
                    to_next[at : at + 3] = faces[side, field, plane, 5:8]
                    to_last[at : at + 3] = faces[side, field, plane, 0:3]

        def sheared(side):
            for number, field in enumerate(MIXED + PLAIN):
                for plane in range(3):
                    at = 72 + 4 * (3 * number + plane)
                    row = 1 if field in MIXED else 4
                    to_next[at : at + 4] = faces[side, field, plane, row : row + 4]
                    row = 3 if field in MIXED else 0
                    to_last[at : at + 4] = faces[side, field, plane, row : row + 4]

        pl.when(where_x == 0)(functools.partial(sheared, 0))
        pl.when(where_x == slabs_x - 1)(functools.partial(sheared, 1))

    pl.when(y_odd == 0)(functools.partial(fill, near, far))
    pl.when(y_odd == 1)(functools.partial(fill, far, near))


def copies_out(parts, finals, begin, count, sems, base):
    return [
        pltpu.make_async_copy(
            part.at[field], final.at[field, pl.ds(begin, count)], sems.at[base + 7 * which + field]
        )
        for which, (part, final) in enumerate(zip(parts, finals))
        for field in range(7)
    ]


def finish(inv_width, index, center, force, old, x_parts, side, grad_z):
    grad_x, viscous, curr = x_parts
    rates = rates_of(
        center,
        force,
        index,
        inv_width,
        (grad_x, side[:7], grad_z),
        [viscous[comp] + side[7 + comp] for comp in range(3)],
        [curr[comp] + side[10 + comp] for comp in range(3)],
    )
    fresh = [(-5.0 / 9.0) * old[field] + 0.15 * rates[field] for field in range(7)]
    return [center[field] + (15.0 / 16.0) * fresh[field] for field in range(7)], fresh


def inner_kernel(
    cells_x, inv_width,
    state, register, forcing, dz, mixes, side_terms,
    new_state, new_register, late_state, late_register,
    fresh_state, fresh_register, sems,
):
    first = lax.axis_index("gx") * cells_x
    early = EARLY

    def step_into(states_out, registers_out, begin):
        def plane_step(plane):
            states, registers = finish(
                inv_width,
                first + plane,
                [state[field, plane] for field in range(7)],
                [forcing[comp, plane] for comp in range(3)],
                [register[field, plane] for field in range(7)],
                x_terms(
                    lambda field: lambda step: state[field, plane + step],
                    lambda number: lambda step: mixes[number, plane + step],
                ),
                [side_terms[number, plane] for number in range(13)],
                [dz[field, plane] for field in range(7)],
            )
            for field in range(7):
                registers_out[field, plane - begin] = registers[field]
                states_out[field, plane - begin] = states[field]

        return plane_step

    in_pairs(3, 3 + early, step_into(fresh_state, fresh_register, 3))
    copies = copies_out((fresh_state, fresh_register), (new_state, new_register), 3, early, sems, 0)
    for copy in copies:
        copy.start()
    in_pairs(3 + early, cells_x - 3, step_into(late_state, late_register, 3 + early))
    for copy in copies:
        copy.wait()


def edge_kernel(
    cells_x, slabs_x, inv_width,
    lean_tile, state, register, forcing, weights, dz, mixes, side_terms,
    planes, near, far, late_state, late_register, kept_state, kept_register,
    new_state, new_register,
    ghost, fields, mixed, fresh_state, fresh_register, sems,
):
    finals = (new_state, new_register)
    late = copies_out((late_state, late_register), finals, 3 + EARLY, cells_x - 6 - EARLY, sems, 0)
    for copy in late:
        copy.start()
    where_x = lax.axis_index("gx")
    y_odd = lax.axis_index("yz") % 2
    first = where_x * cells_x
    lean = lean_tile[...][0, 0]
    at_low, at_high = where_x == 0, where_x == slabs_x - 1
    for field in range(7):
        fields[0, field, 3:9] = state[field, 0:6]
        fields[1, field, 0:6] = state[field, cells_x - 6 :]
    for number in range(6):
        mixed[0, number, 3:9] = mixes[number, 0:6]
        mixed[1, number, 0:6] = mixes[number, cells_x - 6 :]
    for side in range(2):
        for field in range(7):
            for plane in range(3):
                ghost[side, field, plane, 16:24] = planes[side, field, plane]

    def put(from_last, from_next):
        for side in range(2):
            for number, field in enumerate(MIXED):
                for plane in range(3):
                    at = 3 * (3 * (4 * side + number) + plane)
                    ghost[side, field, plane, 13:16] = from_last[at : at + 3]
                    ghost[side, field, plane, 24:27] = from_next[at : at + 3]

        def sheared(side):
            for number, field in enumerate(MIXED + PLAIN):
                for plane in range(3):
                    at = 72 + 4 * (3 * number + plane)
                    row = 9 if field in MIXED else 12
                    ghost[side, field, plane, row : row + 4] = from_last[at : at + 4]
                    row = 27 if field in MIXED else 24
                    ghost[side, field, plane, row : row + 4] = from_next[at : at + 4]

        pl.when(at_low)(functools.partial(sheared, 0))
        pl.when(at_high)(functools.partial(sheared, 1))

    pl.when(y_odd == 0)(functools.partial(put, far, near))
    pl.when(y_odd == 1)(functools.partial(put, near, far))
    for side, shift in enumerate((jnp.where(at_low, lean, 0), jnp.where(at_high, -lean, 0))):
        for field in range(7):
            for plane in range(3):
                low = ghost[side, field, plane, pl.ds(shift + 13, 8)]
                if field in MIXED:
                    high = ghost[side, field, plane, pl.ds(shift + 21, 8)]
                    ghost[side, field, plane, 0:8] = low
                    ghost[side, field, plane, 8:16] = high
                    fields[side, field, plane + 6 * side] = ghost[side, field, plane, 3:11]
                else:
                    fields[side, field, plane + 6 * side] = ghost[side, field, plane, pl.ds(shift + 16, 8)]
    used = (0, 2, 3, 5)
    got = along_z(
        jnp.concatenate(
            [
                fields[side, field, 6 * side : 6 * side + 3].reshape(24, LANES)
                for side in range(2)
                for field in used
            ]
        ),
        weights[:, :LANES],
    ) * (1.0 / 60.0)
    for side in range(2):
        for plane in range(3):
            def rows_of(field):
                return lambda step: ghost[side, field, plane, 3 + step : 11 + step]

            def depth(field):
                at = 24 * (4 * side + used.index(field)) + 8 * plane
                return got[at : at + 8]

            spot = plane + 6 * side
            mixed[side, 0, spot] = first_diff(rows_of(1)) + depth(2)
            mixed[side, 1, spot] = first_diff(rows_of(0))
            mixed[side, 2, spot] = depth(0)
            mixed[side, 3, spot] = first_diff(rows_of(4)) + depth(5)
            mixed[side, 4, spot] = first_diff(rows_of(3))
            mixed[side, 5, spot] = depth(3)

    def copies_of(side):
        parts = (fresh_state.at[side], fresh_register.at[side])
        return copies_out(parts, finals, side * (cells_x - 3), 3, sems, 14 * (side + 1))

    for side in range(2):
        for local in range(3):
            plane = side * (cells_x - 3) + local
            states, registers = finish(
                inv_width,
                first + plane,
                [state[field, plane] for field in range(7)],
                [forcing[comp, plane] for comp in range(3)],
                [register[field, plane] for field in range(7)],
                x_terms(
                    lambda field: lambda step: fields[side, field, local + 3 + step],
                    lambda number: lambda step: mixed[side, number, local + 3 + step],
                ),
                [side_terms[number, plane] for number in range(13)],
                [dz[field, plane] for field in range(7)],
            )
            for field in range(7):
                fresh_register[side, field, local] = registers[field]
                fresh_state[side, field, local] = states[field]
        for copy in copies_of(side):
            copy.start()
    for copy in late + copies_of(0) + copies_of(1):
        copy.wait()


def per_device(slabs_x, slabs_y, state, register, forcing, y_shift):
    cells_x, cells_y = state.shape[1], state.shape[2]
    total_x, total_y = cells_x * slabs_x, cells_y * slabs_y
    steps = (y_shift[0] + cells_y // 2) // cells_y

    def shape(*dims):
        return jax.ShapeDtypeStruct(dims, jnp.float32)

    vmem = pl.BlockSpec(memory_space=pltpu.VMEM)
    anyspace = pl.BlockSpec(memory_space=pl.ANY)
    params = pltpu.CompilerParams(vmem_limit_bytes=VMEM)
    def in_hbm(value):
        return pltpu.with_memory_space_constraint(value, pltpu.HBM)

    up, down, weights, lean = pl.pallas_call(
        functools.partial(face_kernel, cells_x, cells_y),
        out_shape=[
            shape(7, 3, cells_y, LANES), shape(7, 3, cells_y, LANES),
            jax.ShapeDtypeStruct((2 * LANES, 2 * LANES), jnp.bfloat16),
            jax.ShapeDtypeStruct((8, LANES), jnp.int32),
        ],
        in_specs=[pl.BlockSpec(memory_space=pltpu.HBM)] * 2 + [anyspace],
        out_specs=[vmem] * 4,
        scratch_shapes=[pltpu.SMEM((1,), jnp.int32), pltpu.SemaphoreType.DMA((4,))],
        compiler_params=params,
    )(in_hbm(state), in_hbm(jnp.asarray(z_weights())), y_shift)

    digit = min(slabs_y, 8)

    def place(slab, along):
        return along % slabs_y * slabs_x + slab

    def send(value, pairs):
        return lax.ppermute(value, ("yz", "gx"), pairs)

    def both(pairs):
        return pairs + [(b, a) for a, b in pairs]

    def y_pairs(odd):
        return both(
            [(place(slab, j), place(slab, j + 1)) for slab in range(slabs_x) for j in range(odd, slabs_y, 2)]
        )

    def upward(by):
        pairs = [(place(slab, j), place(slab + 1, j)) for slab in range(last) for j in range(slabs_y)]
        return pairs + [(place(last, j + by), place(0, j)) for j in range(slabs_y)]

    def downward(by):
        pairs = [(place(slab + 1, j), place(slab, j)) for slab in range(last) for j in range(slabs_y)]
        return pairs + [(place(0, j - by), place(last, j)) for j in range(slabs_y)]

    last = slabs_x - 1
    if slabs_y > digit:
        where_x = lax.axis_index("gx")
        at_low, at_high = where_x == 0, where_x == last
        groups = steps // digit
        amount = jnp.where(at_high, groups, slabs_y // digit - groups) % (slabs_y // digit)
        across = jnp.where(at_high, up, down)
        hop = 1
        while hop < slabs_y // digit:
            pairs = [(i, (i - hop * digit) % slabs_y) for i in range(slabs_y)]
            moved = lax.ppermute(across, "yz", pairs)
            across = jnp.where((amount // hop) % 2 == 1, moved, across)
            hop *= 2
        up = jnp.where(at_high, across, up)
        down = jnp.where(at_low, across, down)

    def cost(flops):
        return pl.CostEstimate(flops=flops, bytes_accessed=10**6, transcendentals=0)

    def exchange(by, operands):
        up, down, state, register, forcing, weights, lean = operands
        plane = state.shape[1:]
        x_low = send(up, upward(by))
        x_high = send(down, downward(by))
        y_near, y_far = pl.pallas_call(
            functools.partial(row_kernel, cells_x, cells_y),
            out_shape=[shape(21 * cells_x, LANES), shape(21 * cells_x, LANES)],
            in_specs=[vmem],
            out_specs=[vmem] * 2,
            compiler_params=params,
        )(state)
        y_near = send(y_near, y_pairs(0))
        y_far = send(y_far, y_pairs(1))
        dz, dzz = pl.pallas_call(
            functools.partial(own_z_kernel, cells_x),
            out_shape=[shape(7, *plane), shape(5, *plane)],
            in_specs=[vmem] * 2,
            out_specs=[vmem] * 2,
            compiler_params=params,
            cost_estimate=cost(10**8),
        )(state, weights)
        faces, near, far = pl.pallas_call(
            functools.partial(corner_kernel, slabs_x),
            out_shape=[shape(2, *up.shape), shape(160, LANES), shape(160, LANES)],
            in_specs=[vmem] * 2 + [anyspace],
            out_specs=[vmem] * 3,
            compiler_params=params,
            cost_estimate=cost(CORNER),
        )(x_low, x_high, dz)
        near = send(near, y_pairs(0))
        far = send(far, y_pairs(1))
        mixes, side_terms = pl.pallas_call(
            functools.partial(side_kernel, cells_x),
            out_shape=[shape(6, *plane), shape(13, *plane)],
            in_specs=[vmem] * 6,
            out_specs=[vmem] * 2,
            scratch_shapes=[
                pltpu.VMEM((7, cells_x, TALL, LANES), jnp.float32),
                pltpu.VMEM((4, cells_x, TALL, LANES), jnp.float32),
            ],
            compiler_params=params,
            cost_estimate=cost(2 * 10**8),
        )(state, weights, y_near, y_far, dz, dzz)
        early, late = EARLY, cells_x - 6 - EARLY
        new_state, new_register, late_state, late_register = pl.pallas_call(
            functools.partial(inner_kernel, cells_x, 1.0 / total_x),
            out_shape=[shape(*state.shape)] * 2 + [shape(7, late, *plane[1:])] * 2,
            in_specs=[vmem] * 6,
            out_specs=[anyspace] * 2 + [vmem] * 2,
            scratch_shapes=[
                pltpu.VMEM((7, early, *plane[1:]), jnp.float32),
                pltpu.VMEM((7, early, *plane[1:]), jnp.float32),
                pltpu.SemaphoreType.DMA((14,)),
            ],
            compiler_params=params,
            cost_estimate=cost(2 * 10**8),
        )(state, register, forcing, dz, mixes, side_terms)
        return pl.pallas_call(
            functools.partial(edge_kernel, cells_x, slabs_x, 1.0 / total_x),
            out_shape=[shape(*state.shape)] * 2,
            in_specs=[vmem] * 13 + [anyspace] * 2,
            out_specs=[anyspace] * 2,
            input_output_aliases={13: 0, 14: 1},
            scratch_shapes=[
                pltpu.VMEM((2, 7, 3, 40, LANES), jnp.float32),
                pltpu.VMEM((2, 7, 9, 8, LANES), jnp.float32),
                pltpu.VMEM((2, 6, 9, 8, LANES), jnp.float32),
                pltpu.VMEM((2, 7, 3, 8, LANES), jnp.float32),
                pltpu.VMEM((2, 7, 3, 8, LANES), jnp.float32),
                pltpu.SemaphoreType.DMA((42,)),
            ],
            compiler_params=params,
        )(
            lean, state, register, forcing, weights, dz, mixes, side_terms,
            faces, near, far, late_state, late_register, new_state, new_register,
        )

    return lax.switch(
        steps % digit,
        [functools.partial(exchange, by) for by in range(digit)],
        (up, down, state, register, forcing, weights, lean),
    )


def solution(mesh):
    spec = P(None, "gx", "yz", None)
    return jax.shard_map(
        functools.partial(per_device, mesh.shape["gx"], mesh.shape["yz"]),
        mesh=mesh,
        in_specs=(spec, spec, spec, P()),
        out_specs=(spec, spec),
        check_vma=False,
    )
```

```python
import functools

import jax
import jax.numpy as jnp
from jax import lax
from jax.experimental import pallas as pl
from jax.experimental.pallas import tpu as pltpu
from jax.sharding import PartitionSpec as P

LANES = 128
FIRST = ((1, 45.0), (2, -9.0), (3, 1.0))
SECOND = ((1, 270.0), (2, -27.0), (3, 2.0))
MIXED = (0, 1, 3, 4)
PLAIN = (2, 5, 6)
DEEP = (0, 2, 3, 5)
SHEAR_Z = (1, 2, 4, 5)
ROW = 8
CORNER = 10**10
ACROSS = 10**7
EARLY = 4
TALL = 24
VMEM = 32 * 1024 * 1024


def z_weights():
    source = lax.broadcasted_iota(jnp.int32, (LANES, LANES), 0)
    cell = lax.broadcasted_iota(jnp.int32, (LANES, LANES), 1)
    ahead = (source - cell) & (LANES - 1)
    first = jnp.zeros((LANES, LANES), jnp.float32)
    second = jnp.where(ahead == 0, -490.0, 0.0)
    for step, weight in FIRST:
        first = jnp.where(ahead == step, weight, jnp.where(ahead == LANES - step, -weight, first))
    for step, weight in SECOND:
        second = jnp.where((ahead == step) | (ahead == LANES - step), weight, second)
    one = jnp.concatenate([first, second], axis=1)
    return jnp.concatenate([one, one]).astype(jnp.bfloat16)


def along_z(value, weights):
    upper = value.astype(jnp.bfloat16)
    rest = (value - upper.astype(jnp.float32)).astype(jnp.bfloat16)
    return jnp.dot(
        jnp.concatenate([upper, rest], axis=1), weights, preferred_element_type=jnp.float32
    )


def first_diff(part):
    return (
        0.75 * (part(1) - part(-1))
        - 0.15 * (part(2) - part(-2))
        + (1.0 / 60.0) * (part(3) - part(-3))
    )


def second_diff(part):
    return (
        (-490.0 / 180.0) * part(0)
        + 1.5 * (part(1) + part(-1))
        - 0.15 * (part(2) + part(-2))
        + (1.0 / 90.0) * (part(3) + part(-3))
    )


def x_terms(planes_of, deep_of):
    grad = [first_diff(planes_of(field)) for field in range(7)]
    viscous = [
        (4.0 / 3.0) * second_diff(planes_of(0)) + (1.0 / 3.0) * first_diff(deep_of(2)),
        second_diff(planes_of(1)),
        second_diff(planes_of(2)) + (1.0 / 3.0) * first_diff(deep_of(0)),
    ]
    current = [
        first_diff(deep_of(5)),
        -second_diff(planes_of(4)),
        first_diff(deep_of(3)) - second_diff(planes_of(5)),
    ]
    return grad + viscous + current


def xy_terms(parts, side_of):
    parts = list(parts)
    parts[7] = parts[7] + (1.0 / 3.0) * first_diff(side_of(1))
    parts[8] = parts[8] + (1.0 / 3.0) * first_diff(side_of(0))
    parts[10] = parts[10] + first_diff(side_of(4))
    parts[11] = parts[11] + first_diff(side_of(3))
    return parts


def rates_of(center, force, index, inv_width, grads, viscous, curr):
    velx, vely, velz, potx, poty, potz, logr = center
    grad_x, grad_y, grad_z = grads
    field_x = grad_y[5] - grad_z[4]
    field_y = grad_z[3] - grad_x[5]
    field_z = grad_x[4] - grad_y[3] + 0.5
    lorentz = (
        curr[1] * field_z - curr[2] * field_y,
        curr[2] * field_x - curr[0] * field_z,
        curr[0] * field_y - curr[1] * field_x,
    )
    emf = (
        vely * field_z - velz * field_y,
        velz * field_x - velx * field_z,
        velx * field_y - vely * field_x,
    )
    inv_rho = jnp.exp(-logr)
    flow = -1.5 * ((index.astype(jnp.float32) + 0.5) * inv_width - 0.5)
    shear_rate = -1.5 * inv_width
    carried = vely + flow
    divu = grad_x[0] + grad_y[1] + grad_z[2]

    def advect(comp):
        return velx * grad_x[comp] + carried * grad_y[comp] + velz * grad_z[comp]

    rates = []
    for comp in range(3):
        total = (-2.0 / 3.0) * divu * grads[comp][6]
        for col in range(3):
            total = total + (grads[col][comp] + grads[comp][col]) * grads[col][6]
        rate = lorentz[comp] * inv_rho - advect(comp) - grads[comp][6] + force[comp]
        rate = rate + 0.05 * (viscous[comp] + total)
        if comp == 0:
            rate = rate + vely
        if comp == 1:
            rate = rate - (1.0 + shear_rate) * velx
        rates.append(rate)
    for comp in range(3):
        rate = emf[comp] - flow * grad_y[3 + comp] - 0.05 * curr[comp]
        if comp == 0:
            rate = rate - shear_rate * poty
        rates.append(rate)
    rates.append(-advect(6) - divu)
    return rates


def face_kernel(cells_x, state, up, down):
    up[...] = state[:, cells_x - 3 :]
    down[...] = state[:, :3]


def row_kernel(cells_x, cells_y, state, y_near, y_far):
    y_odd = lax.axis_index("yz") % 2

    def rows(first, then):
        for field in range(7):
            for plane in range(cells_x):
                at = 3 * (field * cells_x + plane)
                first[at : at + 3] = state[field, plane, cells_y - 3 :]
                then[at : at + 3] = state[field, plane, :3]

    pl.when(y_odd == 0)(functools.partial(rows, y_near, y_far))
    pl.when(y_odd == 1)(functools.partial(rows, y_far, y_near))


def weight_kernel(weights):
    weights[...] = z_weights()


def own_z_kernel(cells_x, state, weights, dz, dzz):
    got = along_z(state[...].reshape(7 * cells_x * 8, LANES), weights[...])
    dz[...] = (got[:, :LANES] * (1.0 / 60.0)).reshape(7, cells_x, 8, LANES)
    dzz[...] = (got[: 5 * cells_x * 8, LANES:] * (1.0 / 180.0)).reshape(5, cells_x, 8, LANES)


def across_kernel(cells_x, state, dz, after, x_parts):
    def plane_step(plane):
        terms = x_terms(
            lambda field: lambda step: state[field, plane + step],
            lambda field: lambda step: dz[field, plane + step],
        )
        for number, term in enumerate(terms):
            x_parts[number, plane - 3] = term

    in_pairs(3, cells_x - 3, plane_step)


def side_kernel(
    cells_x, state, weights, y_near, y_far, dz, dzz, after, side_terms, block, z_block
):
    own = slice(ROW, ROW + 8)
    y_odd = lax.axis_index("yz") % 2
    block[:, :, own] = state[...]
    for number, field in enumerate(SHEAR_Z):
        z_block[number, :, own] = dz[field]
    count = 3 * cells_x
    got = along_z(
        jnp.concatenate(
            [rows[field * count : (field + 1) * count] for rows in (y_near, y_far) for field in SHEAR_Z]
        ),
        weights[:, :LANES],
    ) * (1.0 / 60.0)

    def ghosts(target, rows, begin):
        for field in range(7):
            for plane in range(cells_x):
                at = 3 * (field * cells_x + plane)
                block[field, plane, target : target + 3] = rows[at : at + 3]
        for number in range(4):
            for plane in range(cells_x):
                at = begin + 3 * (number * cells_x + plane)
                z_block[number, plane, target : target + 3] = got[at : at + 3]

    @pl.when(y_odd == 0)
    def _():
        ghosts(ROW + 8, y_near, 0)
        ghosts(ROW - 3, y_far, 4 * count)

    @pl.when(y_odd == 1)
    def _():
        ghosts(ROW - 3, y_near, 0)
        ghosts(ROW + 8, y_far, 4 * count)

    def yz_step(plane):
        def rows_of(field):
            return lambda step: block[field, plane, ROW + step : ROW + 8 + step]

        def z_rows_of(number):
            return lambda step: z_block[number, plane, ROW + step : ROW + 8 + step]

        grad = [first_diff(rows_of(field)) for field in range(7)]
        cross = [first_diff(z_rows_of(number)) for number in range(4)]
        terms = grad + [
            second_diff(rows_of(0)) + dzz[0, plane],
            (4.0 / 3.0) * second_diff(rows_of(1)) + dzz[1, plane] + (1.0 / 3.0) * cross[1],
            second_diff(rows_of(2)) + (4.0 / 3.0) * dzz[2, plane] + (1.0 / 3.0) * cross[0],
            -(second_diff(rows_of(3)) + dzz[3, plane]),
            cross[3] - dzz[4, plane],
            cross[2] - second_diff(rows_of(5)),
        ]
        for number, term in enumerate(terms):
            side_terms[number, plane] = term

    in_pairs(0, cells_x, yz_step)


def in_pairs(begin, end, step):
    def two(number, carry):
        step(begin + 2 * number)
        step(begin + 2 * number + 1)
        return carry

    lax.fori_loop(0, (end - begin) // 2, two, 0)


def corner_kernel(slabs_x, x_low, x_high, after, faces, near, far):
    where_x = lax.axis_index("gx")
    y_odd = lax.axis_index("yz") % 2
    faces[0] = x_low[...]
    faces[1] = x_high[...]

    def fill(to_next, to_last):
        for side in range(2):
            for number, field in enumerate(MIXED):
                for plane in range(3):
                    at = 3 * (3 * (4 * side + number) + plane)
                    to_next[at : at + 3] = faces[side, field, plane, 5:8]
                    to_last[at : at + 3] = faces[side, field, plane, 0:3]

        def sheared(side):
            for number, field in enumerate(MIXED + PLAIN):
                for plane in range(3):
                    at = 72 + 4 * (3 * number + plane)
                    row = 1 if field in MIXED else 4
                    to_next[at : at + 4] = faces[side, field, plane, row : row + 4]
                    row = 3 if field in MIXED else 0
                    to_last[at : at + 4] = faces[side, field, plane, row : row + 4]

        pl.when(where_x == 0)(functools.partial(sheared, 0))
        pl.when(where_x == slabs_x - 1)(functools.partial(sheared, 1))

    pl.when(y_odd == 0)(functools.partial(fill, near, far))
    pl.when(y_odd == 1)(functools.partial(fill, far, near))


def copies_out(parts, finals, begin, count, sems, base):
    return [
        pltpu.make_async_copy(
            part.at[field], final.at[field, pl.ds(begin, count)], sems.at[base + 7 * which + field]
        )
        for which, (part, final) in enumerate(zip(parts, finals))
        for field in range(7)
    ]


def finish(inv_width, index, center, force, old, x_parts, side, grad_z):
    rates = rates_of(
        center,
        force,
        index,
        inv_width,
        (x_parts[:7], side[:7], grad_z),
        [x_parts[7 + comp] + side[7 + comp] for comp in range(3)],
        [x_parts[10 + comp] + side[10 + comp] for comp in range(3)],
    )
    fresh = [(-5.0 / 9.0) * old[field] + 0.15 * rates[field] for field in range(7)]
    return [center[field] + (15.0 / 16.0) * fresh[field] for field in range(7)], fresh


def inner_kernel(
    cells_x, inv_width,
    state, register, forcing, dz, x_parts, side_terms,
    new_state, new_register, late_state, late_register,
    fresh_state, fresh_register, sems,
):
    first = lax.axis_index("gx") * cells_x
    early = EARLY

    def step_into(states_out, registers_out, begin):
        def plane_step(plane):
            states, registers = finish(
                inv_width,
                first + plane,
                [state[field, plane] for field in range(7)],
                [forcing[comp, plane] for comp in range(3)],
                [register[field, plane] for field in range(7)],
                xy_terms(
                    [x_parts[number, plane - 3] for number in range(13)],
                    lambda field: lambda step: side_terms[field, plane + step],
                ),
                [side_terms[number, plane] for number in range(13)],
                [dz[field, plane] for field in range(7)],
            )
            for field in range(7):
                registers_out[field, plane - begin] = registers[field]
                states_out[field, plane - begin] = states[field]

        return plane_step

    in_pairs(3, 3 + early, step_into(fresh_state, fresh_register, 3))
    copies = copies_out((fresh_state, fresh_register), (new_state, new_register), 3, early, sems, 0)
    for copy in copies:
        copy.start()
    in_pairs(3 + early, cells_x - 3, step_into(late_state, late_register, 3 + early))
    for copy in copies:
        copy.wait()


def edge_kernel(
    cells_x, slabs_x, inv_width,
    lean_tile, state, register, forcing, weights, dz, side_terms,
    planes, near, far, late_state, late_register, kept_state, kept_register,
    new_state, new_register,
    ghost, fields, deep, slope, fresh_state, fresh_register, sems,
):
    finals = (new_state, new_register)
    late = copies_out((late_state, late_register), finals, 3 + EARLY, cells_x - 6 - EARLY, sems, 0)
    for copy in late:
        copy.start()
    where_x = lax.axis_index("gx")
    y_odd = lax.axis_index("yz") % 2
    first = where_x * cells_x
    lean = lean_tile[...][0, 0]
    at_low, at_high = where_x == 0, where_x == slabs_x - 1
    for field in range(7):
        fields[0, field, 3:9] = state[field, 0:6]
        fields[1, field, 0:6] = state[field, cells_x - 6 :]
    for number, field in enumerate(DEEP):
        deep[0, number, 3:9] = dz[field, 0:6]
        deep[1, number, 0:6] = dz[field, cells_x - 6 :]
    for number, field in enumerate(MIXED):
        slope[0, number, 3:9] = side_terms[field, 0:6]
        slope[1, number, 0:6] = side_terms[field, cells_x - 6 :]
    for side in range(2):
        for field in range(7):
            for plane in range(3):
                ghost[side, field, plane, 16:24] = planes[side, field, plane]

    def put(from_last, from_next):
        for side in range(2):
            for number, field in enumerate(MIXED):
                for plane in range(3):
                    at = 3 * (3 * (4 * side + number) + plane)
                    ghost[side, field, plane, 13:16] = from_last[at : at + 3]
                    ghost[side, field, plane, 24:27] = from_next[at : at + 3]

        def sheared(side):
            for number, field in enumerate(MIXED + PLAIN):
                for plane in range(3):
                    at = 72 + 4 * (3 * number + plane)
                    row = 9 if field in MIXED else 12
                    ghost[side, field, plane, row : row + 4] = from_last[at : at + 4]
                    row = 27 if field in MIXED else 24
                    ghost[side, field, plane, row : row + 4] = from_next[at : at + 4]

        pl.when(at_low)(functools.partial(sheared, 0))
        pl.when(at_high)(functools.partial(sheared, 1))

    pl.when(y_odd == 0)(functools.partial(put, far, near))
    pl.when(y_odd == 1)(functools.partial(put, near, far))
    for side, shift in enumerate((jnp.where(at_low, lean, 0), jnp.where(at_high, -lean, 0))):
        for field in range(7):
            for plane in range(3):
                low = ghost[side, field, plane, pl.ds(shift + 13, 8)]
                if field in MIXED:
                    high = ghost[side, field, plane, pl.ds(shift + 21, 8)]
                    ghost[side, field, plane, 0:8] = low
                    ghost[side, field, plane, 8:16] = high
                    fields[side, field, plane + 6 * side] = ghost[side, field, plane, 3:11]
                else:
                    fields[side, field, plane + 6 * side] = ghost[side, field, plane, pl.ds(shift + 16, 8)]
    got = along_z(
        jnp.concatenate(
            [
                fields[side, field, 6 * side : 6 * side + 3].reshape(24, LANES)
                for side in range(2)
                for field in DEEP
            ]
        ),
        weights[:, :LANES],
    ) * (1.0 / 60.0)
    for side in range(2):
        for number in range(4):
            at = 24 * (4 * side + number)
            deep[side, number, 6 * side : 6 * side + 3] = got[at : at + 24].reshape(3, 8, LANES)
        for number, field in enumerate(MIXED):
            for plane in range(3):
                slope[side, number, plane + 6 * side] = first_diff(
                    lambda step: ghost[side, field, plane, 3 + step : 11 + step]
                )

    def copies_of(side):
        parts = (fresh_state.at[side], fresh_register.at[side])
        return copies_out(parts, finals, side * (cells_x - 3), 3, sems, 14 * (side + 1))

    for side in range(2):
        for local in range(3):
            plane = side * (cells_x - 3) + local
            states, registers = finish(
                inv_width,
                first + plane,
                [state[field, plane] for field in range(7)],
                [forcing[comp, plane] for comp in range(3)],
                [register[field, plane] for field in range(7)],
                xy_terms(
                    x_terms(
                        lambda field: lambda step: fields[side, field, local + 3 + step],
                        lambda field: lambda step: deep[side, DEEP.index(field), local + 3 + step],
                    ),
                    lambda field: lambda step: slope[side, MIXED.index(field), local + 3 + step],
                ),
                [side_terms[number, plane] for number in range(13)],
                [dz[field, plane] for field in range(7)],
            )
            for field in range(7):
                fresh_register[side, field, local] = registers[field]
                fresh_state[side, field, local] = states[field]
        for copy in copies_of(side):
            copy.start()
    for copy in late + copies_of(0) + copies_of(1):
        copy.wait()


def per_device(slabs_x, slabs_y, state, register, forcing, y_shift):
    cells_x, cells_y = state.shape[1], state.shape[2]
    total_x, total_y = cells_x * slabs_x, cells_y * slabs_y
    offset = y_shift[0]
    steps = (offset + cells_y // 2) // cells_y

    def shape(*dims):
        return jax.ShapeDtypeStruct(dims, jnp.float32)

    vmem = pl.BlockSpec(memory_space=pltpu.VMEM)
    anyspace = pl.BlockSpec(memory_space=pl.ANY)
    params = pltpu.CompilerParams(vmem_limit_bytes=VMEM)
    lean = jnp.full((8, LANES), offset - steps * cells_y, jnp.int32)

    digit = min(slabs_y, 8)

    def place(slab, along):
        return along % slabs_y * slabs_x + slab

    def send(value, pairs):
        return lax.ppermute(value, ("yz", "gx"), pairs)

    def both(pairs):
        return pairs + [(b, a) for a, b in pairs]

    def y_pairs(odd):
        return both(
            [(place(slab, j), place(slab, j + 1)) for slab in range(slabs_x) for j in range(odd, slabs_y, 2)]
        )

    def upward(by):
        pairs = [(place(slab, j), place(slab + 1, j)) for slab in range(last) for j in range(slabs_y)]
        return pairs + [(place(last, j + by), place(0, j)) for j in range(slabs_y)]

    def downward(by):
        pairs = [(place(slab + 1, j), place(slab, j)) for slab in range(last) for j in range(slabs_y)]
        return pairs + [(place(0, j - by), place(last, j)) for j in range(slabs_y)]

    last = slabs_x - 1

    def cost(flops):
        return pl.CostEstimate(flops=flops, bytes_accessed=10**6, transcendentals=0)

    weights = pl.pallas_call(
        weight_kernel,
        out_shape=jax.ShapeDtypeStruct((2 * LANES, 2 * LANES), jnp.bfloat16),
        out_specs=vmem,
        compiler_params=params,
        cost_estimate=cost(2 * 10**8),
    )()

    def faces_of(state):
        return pl.pallas_call(
            functools.partial(face_kernel, cells_x),
            out_shape=[shape(7, 3, cells_y, LANES)] * 2,
            in_specs=[vmem],
            out_specs=[vmem] * 2,
            compiler_params=params,
        )(state)

    up = down = None
    if slabs_y > digit:
        up, down = faces_of(state)
        where_x = lax.axis_index("gx")
        at_low, at_high = where_x == 0, where_x == last
        groups = steps // digit
        amount = jnp.where(at_high, groups, slabs_y // digit - groups) % (slabs_y // digit)
        across = jnp.where(at_high, up, down)
        hop = 1
        while hop < slabs_y // digit:
            pairs = [(i, (i - hop * digit) % slabs_y) for i in range(slabs_y)]
            moved = lax.ppermute(across, "yz", pairs)
            across = jnp.where((amount // hop) % 2 == 1, moved, across)
            hop *= 2
        up = jnp.where(at_high, across, up)
        down = jnp.where(at_low, across, down)

    def exchange(by, operands):
        up, down, state, register, forcing, weights, lean = operands
        plane = state.shape[1:]
        if up is None:
            up, down = faces_of(state)
        x_low = send(up, upward(by))
        x_high = send(down, downward(by))
        y_near, y_far = pl.pallas_call(
            functools.partial(row_kernel, cells_x, cells_y),
            out_shape=[shape(21 * cells_x, LANES), shape(21 * cells_x, LANES)],
            in_specs=[vmem],
            out_specs=[vmem] * 2,
            compiler_params=params,
        )(state)
        y_near = send(y_near, y_pairs(0))
        y_far = send(y_far, y_pairs(1))
        dz, dzz = pl.pallas_call(
            functools.partial(own_z_kernel, cells_x),
            out_shape=[shape(7, *plane), shape(5, *plane)],
            in_specs=[vmem] * 2,
            out_specs=[vmem] * 2,
            compiler_params=params,
            cost_estimate=cost(10**8),
        )(state, weights)
        faces, near, far = pl.pallas_call(
            functools.partial(corner_kernel, slabs_x),
            out_shape=[shape(2, *up.shape), shape(160, LANES), shape(160, LANES)],
            in_specs=[vmem] * 2 + [anyspace],
            out_specs=[vmem] * 3,
            compiler_params=params,
            cost_estimate=cost(CORNER),
        )(x_low, x_high, dz)
        near = send(near, y_pairs(0))
        far = send(far, y_pairs(1))
        x_parts = pl.pallas_call(
            functools.partial(across_kernel, cells_x),
            out_shape=shape(13, cells_x - 6, *plane[1:]),
            in_specs=[vmem] * 2 + [anyspace],
            out_specs=vmem,
            compiler_params=params,
            cost_estimate=cost(ACROSS),
        )(state, dz, faces)
        side_terms = pl.pallas_call(
            functools.partial(side_kernel, cells_x),
            out_shape=shape(13, *plane),
            in_specs=[vmem] * 6 + [anyspace],
            out_specs=vmem,
            scratch_shapes=[
                pltpu.VMEM((7, cells_x, TALL, LANES), jnp.float32),
                pltpu.VMEM((4, cells_x, TALL, LANES), jnp.float32),
            ],
            compiler_params=params,
            cost_estimate=cost(2 * 10**8),
        )(state, weights, y_near, y_far, dz, dzz, x_parts)
        early, late = EARLY, cells_x - 6 - EARLY
        new_state, new_register, late_state, late_register = pl.pallas_call(
            functools.partial(inner_kernel, cells_x, 1.0 / total_x),
            out_shape=[shape(*state.shape)] * 2 + [shape(7, late, *plane[1:])] * 2,
            in_specs=[vmem] * 6,
            out_specs=[anyspace] * 2 + [vmem] * 2,
            scratch_shapes=[
                pltpu.VMEM((7, early, *plane[1:]), jnp.float32),
                pltpu.VMEM((7, early, *plane[1:]), jnp.float32),
                pltpu.SemaphoreType.DMA((14,)),
            ],
            compiler_params=params,
            cost_estimate=cost(2 * 10**8),
        )(state, register, forcing, dz, x_parts, side_terms)
        return pl.pallas_call(
            functools.partial(edge_kernel, cells_x, slabs_x, 1.0 / total_x),
            out_shape=[shape(*state.shape)] * 2,
            in_specs=[vmem] * 12 + [anyspace] * 2,
            out_specs=[anyspace] * 2,
            input_output_aliases={12: 0, 13: 1},
            scratch_shapes=[
                pltpu.VMEM((2, 7, 3, 40, LANES), jnp.float32),
                pltpu.VMEM((2, 7, 9, 8, LANES), jnp.float32),
                pltpu.VMEM((2, 4, 9, 8, LANES), jnp.float32),
                pltpu.VMEM((2, 4, 9, 8, LANES), jnp.float32),
                pltpu.VMEM((2, 7, 3, 8, LANES), jnp.float32),
                pltpu.VMEM((2, 7, 3, 8, LANES), jnp.float32),
                pltpu.SemaphoreType.DMA((42,)),
            ],
            compiler_params=params,
        )(
            lean, state, register, forcing, weights, dz, side_terms,
            faces, near, far, late_state, late_register, new_state, new_register,
        )

    return lax.switch(
        steps % digit,
        [functools.partial(exchange, by) for by in range(digit)],
        (up, down, state, register, forcing, weights, lean),
    )


def solution(mesh):
    spec = P(None, "gx", "yz", None)
    return jax.shard_map(
        functools.partial(per_device, mesh.shape["gx"], mesh.shape["yz"]),
        mesh=mesh,
        in_specs=(spec, spec, spec, P()),
        out_specs=(spec, spec),
        check_vma=False,
    )
```

```python
import functools

import jax
import jax.numpy as jnp
from jax import lax
from jax.experimental import pallas as pl
from jax.experimental.pallas import tpu as pltpu
from jax.sharding import PartitionSpec as P

LANES = 128
FIRST = ((1, 45.0), (2, -9.0), (3, 1.0))
SECOND = ((1, 270.0), (2, -27.0), (3, 2.0))
MIXED = (0, 1, 3, 4)
PLAIN = (2, 5, 6)
DEEP = (0, 2, 3, 5)
SHEAR_Z = (1, 2, 4, 5)
ROW = 8
CORNER = 10**10
ACROSS = 10**7
EARLY = 4
TALL = 24
VMEM = 32 * 1024 * 1024


def z_weights():
    source = lax.broadcasted_iota(jnp.int32, (LANES, LANES), 0)
    cell = lax.broadcasted_iota(jnp.int32, (LANES, LANES), 1)
    ahead = (source - cell) & (LANES - 1)
    first = jnp.zeros((LANES, LANES), jnp.float32)
    second = jnp.where(ahead == 0, -490.0, 0.0)
    for step, weight in FIRST:
        first = jnp.where(ahead == step, weight, jnp.where(ahead == LANES - step, -weight, first))
    for step, weight in SECOND:
        second = jnp.where((ahead == step) | (ahead == LANES - step), weight, second)
    one = jnp.concatenate([first, second], axis=1)
    return jnp.concatenate([one, one]).astype(jnp.bfloat16)


def along_z(value, weights):
    upper = value.astype(jnp.bfloat16)
    rest = (value - upper.astype(jnp.float32)).astype(jnp.bfloat16)
    return jnp.dot(
        jnp.concatenate([upper, rest], axis=1), weights, preferred_element_type=jnp.float32
    )


def first_diff(part):
    return (
        0.75 * (part(1) - part(-1))
        - 0.15 * (part(2) - part(-2))
        + (1.0 / 60.0) * (part(3) - part(-3))
    )


def second_diff(part):
    return (
        (-490.0 / 180.0) * part(0)
        + 1.5 * (part(1) + part(-1))
        - 0.15 * (part(2) + part(-2))
        + (1.0 / 90.0) * (part(3) + part(-3))
    )


def x_terms(planes_of, deep_of):
    grad = [first_diff(planes_of(field)) for field in range(7)]
    viscous = [
        (4.0 / 3.0) * second_diff(planes_of(0)) + (1.0 / 3.0) * first_diff(deep_of(2)),
        second_diff(planes_of(1)),
        second_diff(planes_of(2)) + (1.0 / 3.0) * first_diff(deep_of(0)),
    ]
    current = [
        first_diff(deep_of(5)),
        -second_diff(planes_of(4)),
        first_diff(deep_of(3)) - second_diff(planes_of(5)),
    ]
    return grad + viscous + current


def xy_terms(parts, side_of):
    parts = list(parts)
    parts[7] = parts[7] + (1.0 / 3.0) * first_diff(side_of(1))
    parts[8] = parts[8] + (1.0 / 3.0) * first_diff(side_of(0))
    parts[10] = parts[10] + first_diff(side_of(4))
    parts[11] = parts[11] + first_diff(side_of(3))
    return parts


def rates_of(center, force, index, inv_width, grads, viscous, curr):
    velx, vely, velz, potx, poty, potz, logr = center
    grad_x, grad_y, grad_z = grads
    field_x = grad_y[5] - grad_z[4]
    field_y = grad_z[3] - grad_x[5]
    field_z = grad_x[4] - grad_y[3] + 0.5
    lorentz = (
        curr[1] * field_z - curr[2] * field_y,
        curr[2] * field_x - curr[0] * field_z,
        curr[0] * field_y - curr[1] * field_x,
    )
    emf = (
        vely * field_z - velz * field_y,
        velz * field_x - velx * field_z,
        velx * field_y - vely * field_x,
    )
    inv_rho = jnp.exp(-logr)
    flow = -1.5 * ((index.astype(jnp.float32) + 0.5) * inv_width - 0.5)
    shear_rate = -1.5 * inv_width
    carried = vely + flow
    divu = grad_x[0] + grad_y[1] + grad_z[2]

    def advect(comp):
        return velx * grad_x[comp] + carried * grad_y[comp] + velz * grad_z[comp]

    rates = []
    for comp in range(3):
        total = (-2.0 / 3.0) * divu * grads[comp][6]
        for col in range(3):
            total = total + (grads[col][comp] + grads[comp][col]) * grads[col][6]
        rate = lorentz[comp] * inv_rho - advect(comp) - grads[comp][6] + force[comp]
        rate = rate + 0.05 * (viscous[comp] + total)
        if comp == 0:
            rate = rate + vely
        if comp == 1:
            rate = rate - (1.0 + shear_rate) * velx
        rates.append(rate)
    for comp in range(3):
        rate = emf[comp] - flow * grad_y[3 + comp] - 0.05 * curr[comp]
        if comp == 0:
            rate = rate - shear_rate * poty
        rates.append(rate)
    rates.append(-advect(6) - divu)
    return rates


def face_kernel(cells_x, state, x_near, x_far):
    x_odd = lax.axis_index("gx") % 2

    def planes(first, then):
        first[...] = state[:, cells_x - 3 :]
        then[...] = state[:, :3]

    pl.when(x_odd == 0)(functools.partial(planes, x_near, x_far))
    pl.when(x_odd == 1)(functools.partial(planes, x_far, x_near))


def row_kernel(cells_x, cells_y, state, y_near, y_far):
    y_odd = lax.axis_index("yz") % 2

    def rows(first, then):
        for field in range(7):
            for plane in range(cells_x):
                at = 3 * (field * cells_x + plane)
                first[at : at + 3] = state[field, plane, cells_y - 3 :]
                then[at : at + 3] = state[field, plane, :3]

    pl.when(y_odd == 0)(functools.partial(rows, y_near, y_far))
    pl.when(y_odd == 1)(functools.partial(rows, y_far, y_near))


def weight_kernel(weights):
    weights[...] = z_weights()


def own_z_kernel(cells_x, state, weights, dz, dzz):
    got = along_z(state[...].reshape(7 * cells_x * 8, LANES), weights[...])
    dz[...] = (got[:, :LANES] * (1.0 / 60.0)).reshape(7, cells_x, 8, LANES)
    dzz[...] = (got[: 5 * cells_x * 8, LANES:] * (1.0 / 180.0)).reshape(5, cells_x, 8, LANES)


def across_kernel(cells_x, state, dz, forcing, after, x_parts, force, sem):
    copy = pltpu.make_async_copy(forcing, force, sem)
    copy.start()

    def plane_step(plane):
        terms = x_terms(
            lambda field: lambda step: state[field, plane + step],
            lambda field: lambda step: dz[field, plane + step],
        )
        for number, term in enumerate(terms):
            x_parts[number, plane - 3] = term

    in_pairs(3, cells_x - 3, plane_step)
    copy.wait()


def side_kernel(
    cells_x, state, weights, y_far, y_near, dz, dzz, after, side_terms, block, z_block
):
    own = slice(ROW, ROW + 8)
    y_odd = lax.axis_index("yz") % 2
    block[:, :, own] = state[...]
    for number, field in enumerate(SHEAR_Z):
        z_block[number, :, own] = dz[field]
    count = 3 * cells_x
    got = along_z(
        jnp.concatenate(
            [rows[field * count : (field + 1) * count] for rows in (y_near, y_far) for field in SHEAR_Z]
        ),
        weights[:, :LANES],
    ) * (1.0 / 60.0)

    def ghosts(target, rows, begin):
        for field in range(7):
            for plane in range(cells_x):
                at = 3 * (field * cells_x + plane)
                block[field, plane, target : target + 3] = rows[at : at + 3]
        for number in range(4):
            for plane in range(cells_x):
                at = begin + 3 * (number * cells_x + plane)
                z_block[number, plane, target : target + 3] = got[at : at + 3]

    @pl.when(y_odd == 0)
    def _():
        ghosts(ROW + 8, y_near, 0)
        ghosts(ROW - 3, y_far, 4 * count)

    @pl.when(y_odd == 1)
    def _():
        ghosts(ROW - 3, y_near, 0)
        ghosts(ROW + 8, y_far, 4 * count)

    def yz_step(plane):
        def rows_of(field):
            return lambda step: block[field, plane, ROW + step : ROW + 8 + step]

        def z_rows_of(number):
            return lambda step: z_block[number, plane, ROW + step : ROW + 8 + step]

        grad = [first_diff(rows_of(field)) for field in range(7)]
        cross = [first_diff(z_rows_of(number)) for number in range(4)]
        terms = grad + [
            second_diff(rows_of(0)) + dzz[0, plane],
            (4.0 / 3.0) * second_diff(rows_of(1)) + dzz[1, plane] + (1.0 / 3.0) * cross[1],
            second_diff(rows_of(2)) + (4.0 / 3.0) * dzz[2, plane] + (1.0 / 3.0) * cross[0],
            -(second_diff(rows_of(3)) + dzz[3, plane]),
            cross[3] - dzz[4, plane],
            cross[2] - second_diff(rows_of(5)),
        ]
        for number, term in enumerate(terms):
            side_terms[number, plane] = term

    in_pairs(0, cells_x, yz_step)


def in_pairs(begin, end, step):
    def two(number, carry):
        step(begin + 2 * number)
        step(begin + 2 * number + 1)
        return carry

    lax.fori_loop(0, (end - begin) // 2, two, 0)


def corner_kernel(slabs_x, x_far, x_near, after, faces, far, near):
    where_x = lax.axis_index("gx")
    y_odd = lax.axis_index("yz") % 2

    def order(low, high):
        faces[0] = low[...]
        faces[1] = high[...]

    pl.when(where_x % 2 == 0)(functools.partial(order, x_far, x_near))
    pl.when(where_x % 2 == 1)(functools.partial(order, x_near, x_far))

    def fill(to_next, to_last):
        for side in range(2):
            for number, field in enumerate(MIXED):
                for plane in range(3):
                    at = 3 * (3 * (4 * side + number) + plane)
                    to_next[at : at + 3] = faces[side, field, plane, 5:8]
                    to_last[at : at + 3] = faces[side, field, plane, 0:3]

        def sheared(side):
            for number, field in enumerate(MIXED + PLAIN):
                for plane in range(3):
                    at = 72 + 4 * (3 * number + plane)
                    row = 1 if field in MIXED else 4
                    to_next[at : at + 4] = faces[side, field, plane, row : row + 4]
                    row = 3 if field in MIXED else 0
                    to_last[at : at + 4] = faces[side, field, plane, row : row + 4]

        pl.when(where_x == 0)(functools.partial(sheared, 0))
        pl.when(where_x == slabs_x - 1)(functools.partial(sheared, 1))

    pl.when(y_odd == 0)(functools.partial(fill, near, far))
    pl.when(y_odd == 1)(functools.partial(fill, far, near))


def copies_out(parts, finals, begin, count, sems, base):
    return [
        pltpu.make_async_copy(
            part.at[field], final.at[field, pl.ds(begin, count)], sems.at[base + 7 * which + field]
        )
        for which, (part, final) in enumerate(zip(parts, finals))
        for field in range(7)
    ]


def finish(inv_width, index, center, force, old, x_parts, side, grad_z):
    rates = rates_of(
        center,
        force,
        index,
        inv_width,
        (x_parts[:7], side[:7], grad_z),
        [x_parts[7 + comp] + side[7 + comp] for comp in range(3)],
        [x_parts[10 + comp] + side[10 + comp] for comp in range(3)],
    )
    fresh = [(-5.0 / 9.0) * old[field] + 0.15 * rates[field] for field in range(7)]
    return [center[field] + (15.0 / 16.0) * fresh[field] for field in range(7)], fresh


def inner_kernel(
    cells_x, inv_width,
    state, register, forcing, dz, x_parts, side_terms,
    new_state, new_register, late_state, late_register,
    fresh_state, fresh_register, sems,
):
    first = lax.axis_index("gx") * cells_x
    early = EARLY

    def step_into(states_out, registers_out, begin):
        def plane_step(plane):
            states, registers = finish(
                inv_width,
                first + plane,
                [state[field, plane] for field in range(7)],
                [forcing[comp, plane] for comp in range(3)],
                [register[field, plane] for field in range(7)],
                xy_terms(
                    [x_parts[number, plane - 3] for number in range(13)],
                    lambda field: lambda step: side_terms[field, plane + step],
                ),
                [side_terms[number, plane] for number in range(13)],
                [dz[field, plane] for field in range(7)],
            )
            for field in range(7):
                registers_out[field, plane - begin] = registers[field]
                states_out[field, plane - begin] = states[field]

        return plane_step

    in_pairs(3, 3 + early, step_into(fresh_state, fresh_register, 3))
    copies = copies_out((fresh_state, fresh_register), (new_state, new_register), 3, early, sems, 0)
    for copy in copies:
        copy.start()
    in_pairs(3 + early, cells_x - 3, step_into(late_state, late_register, 3 + early))
    for copy in copies:
        copy.wait()


def edge_kernel(
    cells_x, slabs_x, inv_width,
    lean_tile, state, register, forcing, weights, dz, side_terms,
    planes, far, near, late_state, late_register, kept_state, kept_register,
    new_state, new_register,
    ghost, fields, deep, slope, fresh_state, fresh_register, sems,
):
    finals = (new_state, new_register)
    late = copies_out((late_state, late_register), finals, 3 + EARLY, cells_x - 6 - EARLY, sems, 0)
    for copy in late:
        copy.start()
    where_x = lax.axis_index("gx")
    y_odd = lax.axis_index("yz") % 2
    first = where_x * cells_x
    lean = lean_tile[...][0, 0]
    at_low, at_high = where_x == 0, where_x == slabs_x - 1
    for field in range(7):
        fields[0, field, 3:9] = state[field, 0:6]
        fields[1, field, 0:6] = state[field, cells_x - 6 :]
    for number, field in enumerate(DEEP):
        deep[0, number, 3:9] = dz[field, 0:6]
        deep[1, number, 0:6] = dz[field, cells_x - 6 :]
    for number, field in enumerate(MIXED):
        slope[0, number, 3:9] = side_terms[field, 0:6]
        slope[1, number, 0:6] = side_terms[field, cells_x - 6 :]
    for side in range(2):
        for field in range(7):
            for plane in range(3):
                ghost[side, field, plane, 16:24] = planes[side, field, plane]

    def put(from_last, from_next):
        for side in range(2):
            for number, field in enumerate(MIXED):
                for plane in range(3):
                    at = 3 * (3 * (4 * side + number) + plane)
                    ghost[side, field, plane, 13:16] = from_last[at : at + 3]
                    ghost[side, field, plane, 24:27] = from_next[at : at + 3]

        def sheared(side):
            for number, field in enumerate(MIXED + PLAIN):
                for plane in range(3):
                    at = 72 + 4 * (3 * number + plane)
                    row = 9 if field in MIXED else 12
                    ghost[side, field, plane, row : row + 4] = from_last[at : at + 4]
                    row = 27 if field in MIXED else 24
                    ghost[side, field, plane, row : row + 4] = from_next[at : at + 4]

        pl.when(at_low)(functools.partial(sheared, 0))
        pl.when(at_high)(functools.partial(sheared, 1))

    pl.when(y_odd == 0)(functools.partial(put, far, near))
    pl.when(y_odd == 1)(functools.partial(put, near, far))
    for side, shift in enumerate((jnp.where(at_low, lean, 0), jnp.where(at_high, -lean, 0))):
        for field in range(7):
            for plane in range(3):
                low = ghost[side, field, plane, pl.ds(shift + 13, 8)]
                if field in MIXED:
                    high = ghost[side, field, plane, pl.ds(shift + 21, 8)]
                    ghost[side, field, plane, 0:8] = low
                    ghost[side, field, plane, 8:16] = high
                    fields[side, field, plane + 6 * side] = ghost[side, field, plane, 3:11]
                else:
                    fields[side, field, plane + 6 * side] = ghost[side, field, plane, pl.ds(shift + 16, 8)]
    got = along_z(
        jnp.concatenate(
            [
                fields[side, field, 6 * side : 6 * side + 3].reshape(24, LANES)
                for side in range(2)
                for field in DEEP
            ]
        ),
        weights[:, :LANES],
    ) * (1.0 / 60.0)
    for side in range(2):
        for number in range(4):
            at = 24 * (4 * side + number)
            deep[side, number, 6 * side : 6 * side + 3] = got[at : at + 24].reshape(3, 8, LANES)
        for number, field in enumerate(MIXED):
            for plane in range(3):
                slope[side, number, plane + 6 * side] = first_diff(
                    lambda step: ghost[side, field, plane, 3 + step : 11 + step]
                )

    def copies_of(side):
        parts = (fresh_state.at[side], fresh_register.at[side])
        return copies_out(parts, finals, side * (cells_x - 3), 3, sems, 14 * (side + 1))

    for side in range(2):
        for local in range(3):
            plane = side * (cells_x - 3) + local
            states, registers = finish(
                inv_width,
                first + plane,
                [state[field, plane] for field in range(7)],
                [forcing[comp, plane] for comp in range(3)],
                [register[field, plane] for field in range(7)],
                xy_terms(
                    x_terms(
                        lambda field: lambda step: fields[side, field, local + 3 + step],
                        lambda field: lambda step: deep[side, DEEP.index(field), local + 3 + step],
                    ),
                    lambda field: lambda step: slope[side, MIXED.index(field), local + 3 + step],
                ),
                [side_terms[number, plane] for number in range(13)],
                [dz[field, plane] for field in range(7)],
            )
            for field in range(7):
                fresh_register[side, field, local] = registers[field]
                fresh_state[side, field, local] = states[field]
        for copy in copies_of(side):
            copy.start()
    for copy in late + copies_of(0) + copies_of(1):
        copy.wait()


def per_device(slabs_x, slabs_y, state, register, forcing, y_shift):
    cells_x, cells_y = state.shape[1], state.shape[2]
    total_x, total_y = cells_x * slabs_x, cells_y * slabs_y
    offset = y_shift[0]
    steps = (offset + cells_y // 2) // cells_y

    def shape(*dims):
        return jax.ShapeDtypeStruct(dims, jnp.float32)

    vmem = pl.BlockSpec(memory_space=pltpu.VMEM)
    anyspace = pl.BlockSpec(memory_space=pl.ANY)
    params = pltpu.CompilerParams(vmem_limit_bytes=VMEM)
    lean = lax.optimization_barrier(jnp.full((8, LANES), offset - steps * cells_y, jnp.int32))

    digit = min(slabs_y, 8)

    def place(slab, along):
        return along % slabs_y * slabs_x + slab

    def send(value, pairs):
        return lax.ppermute(value, ("yz", "gx"), pairs)

    def both(pairs):
        return pairs + [(b, a) for a, b in pairs]

    def y_pairs(odd):
        return both(
            [(place(slab, j), place(slab, j + 1)) for slab in range(slabs_x) for j in range(odd, slabs_y, 2)]
        )

    def x_pairs(odd, by):
        return both(
            [
                (place(slab, j + by * (slab == last)), place((slab + 1) % slabs_x, j))
                for slab in range(odd, slabs_x, 2)
                for j in range(slabs_y)
            ]
        )

    last = slabs_x - 1

    def cost(flops):
        return pl.CostEstimate(flops=flops, bytes_accessed=10**6, transcendentals=0)

    weights = pl.pallas_call(
        weight_kernel,
        out_shape=jax.ShapeDtypeStruct((2 * LANES, 2 * LANES), jnp.bfloat16),
        out_specs=vmem,
        compiler_params=params,
        cost_estimate=cost(2 * 10**8),
    )()

    def in_hbm(value):
        return pltpu.with_memory_space_constraint(value, pltpu.HBM)

    def faces_of(state):
        return pl.pallas_call(
            functools.partial(face_kernel, cells_x),
            out_shape=[shape(7, 3, cells_y, LANES)] * 2,
            in_specs=[vmem],
            out_specs=[vmem] * 2,
            compiler_params=params,
        )(state)

    x_near = x_far = None
    if slabs_y > digit:
        x_near, x_far = faces_of(state)
        where_x = lax.axis_index("gx")
        at_low, at_high = where_x == 0, where_x == last
        groups = steps // digit
        amount = jnp.where(at_high, groups, slabs_y // digit - groups) % (slabs_y // digit)
        across = x_far
        hop = 1
        while hop < slabs_y // digit:
            pairs = [(i, (i - hop * digit) % slabs_y) for i in range(slabs_y)]
            moved = lax.ppermute(across, "yz", pairs)
            across = jnp.where((amount // hop) % 2 == 1, moved, across)
            hop *= 2
        x_far = jnp.where(at_low | at_high, across, x_far)

    def exchange(by, operands):
        x_near, x_far, state, register, forcing, weights, lean = operands
        plane = state.shape[1:]
        if x_far is None:
            x_near, x_far = faces_of(state)
        x_far = send(x_far, x_pairs(1, by))
        x_near = send(x_near, x_pairs(0, 0))
        y_near, y_far = pl.pallas_call(
            functools.partial(row_kernel, cells_x, cells_y),
            out_shape=[shape(21 * cells_x, LANES), shape(21 * cells_x, LANES)],
            in_specs=[vmem],
            out_specs=[vmem] * 2,
            compiler_params=params,
        )(state)
        y_far = send(y_far, y_pairs(1))
        y_near = send(y_near, y_pairs(0))
        dz, dzz = pl.pallas_call(
            functools.partial(own_z_kernel, cells_x),
            out_shape=[shape(7, *plane), shape(5, *plane)],
            in_specs=[vmem] * 2,
            out_specs=[vmem] * 2,
            compiler_params=params,
            cost_estimate=cost(10**8),
        )(state, weights)
        faces, far, near = pl.pallas_call(
            functools.partial(corner_kernel, slabs_x),
            out_shape=[shape(2, *x_far.shape), shape(160, LANES), shape(160, LANES)],
            in_specs=[vmem] * 2 + [anyspace],
            out_specs=[vmem] * 3,
            compiler_params=params,
            cost_estimate=cost(CORNER),
        )(x_far, x_near, dz)
        far = send(far, y_pairs(1))
        near = send(near, y_pairs(0))
        x_parts, force = pl.pallas_call(
            functools.partial(across_kernel, cells_x),
            out_shape=[shape(13, cells_x - 6, *plane[1:]), shape(*forcing.shape)],
            in_specs=[vmem] * 2 + [pl.BlockSpec(memory_space=pltpu.HBM), anyspace],
            out_specs=[vmem] * 2,
            scratch_shapes=[pltpu.SemaphoreType.DMA],
            compiler_params=params,
            cost_estimate=cost(ACROSS),
        )(state, dz, forcing, faces)
        side_terms = pl.pallas_call(
            functools.partial(side_kernel, cells_x),
            out_shape=shape(13, *plane),
            in_specs=[vmem] * 6 + [anyspace],
            out_specs=vmem,
            scratch_shapes=[
                pltpu.VMEM((7, cells_x, TALL, LANES), jnp.float32),
                pltpu.VMEM((4, cells_x, TALL, LANES), jnp.float32),
            ],
            compiler_params=params,
            cost_estimate=cost(2 * 10**8),
        )(state, weights, y_far, y_near, dz, dzz, x_parts)
        early, late = EARLY, cells_x - 6 - EARLY
        new_state, new_register, late_state, late_register = pl.pallas_call(
            functools.partial(inner_kernel, cells_x, 1.0 / total_x),
            out_shape=[shape(*state.shape)] * 2 + [shape(7, late, *plane[1:])] * 2,
            in_specs=[vmem] * 6,
            out_specs=[anyspace] * 2 + [vmem] * 2,
            scratch_shapes=[
                pltpu.VMEM((7, early, *plane[1:]), jnp.float32),
                pltpu.VMEM((7, early, *plane[1:]), jnp.float32),
                pltpu.SemaphoreType.DMA((14,)),
            ],
            compiler_params=params,
            cost_estimate=cost(2 * 10**8),
        )(state, register, force, dz, x_parts, side_terms)
        return pl.pallas_call(
            functools.partial(edge_kernel, cells_x, slabs_x, 1.0 / total_x),
            out_shape=[shape(*state.shape)] * 2,
            in_specs=[vmem] * 12 + [anyspace] * 2,
            out_specs=[anyspace] * 2,
            input_output_aliases={12: 0, 13: 1},
            scratch_shapes=[
                pltpu.VMEM((2, 7, 3, 40, LANES), jnp.float32),
                pltpu.VMEM((2, 7, 9, 8, LANES), jnp.float32),
                pltpu.VMEM((2, 4, 9, 8, LANES), jnp.float32),
                pltpu.VMEM((2, 4, 9, 8, LANES), jnp.float32),
                pltpu.VMEM((2, 7, 3, 8, LANES), jnp.float32),
                pltpu.VMEM((2, 7, 3, 8, LANES), jnp.float32),
                pltpu.SemaphoreType.DMA((42,)),
            ],
            compiler_params=params,
        )(
            lean, state, register, force, weights, dz, side_terms,
            faces, far, near, late_state, late_register, new_state, new_register,
        )

    return lax.switch(
        steps % digit,
        [functools.partial(exchange, by) for by in range(digit)],
        (x_near, x_far, state, register, in_hbm(forcing), weights, lean),
    )


def solution(mesh):
    spec = P(None, "gx", "yz", None)
    return jax.shard_map(
        functools.partial(per_device, mesh.shape["gx"], mesh.shape["yz"]),
        mesh=mesh,
        in_specs=(spec, spec, spec, P()),
        out_specs=(spec, spec),
        check_vma=False,
    )
```

```python
import functools

import jax
import jax.numpy as jnp
from jax import lax
from jax.experimental import pallas as pl
from jax.experimental.pallas import tpu as pltpu
from jax.sharding import PartitionSpec as P

LANES = 128
FIRST = ((1, 45.0), (2, -9.0), (3, 1.0))
SECOND = ((1, 270.0), (2, -27.0), (3, 2.0))
MIXED = (0, 1, 3, 4)
PLAIN = (2, 5, 6)
DEEP = (0, 2, 3, 5)
SHEAR_Z = (1, 2, 4, 5)
ROW = 8
LOW = 10**9
EARLY = 4
TALL = 24
VMEM = 32 * 1024 * 1024


def z_weights():
    source = lax.broadcasted_iota(jnp.int32, (LANES, LANES), 0)
    cell = lax.broadcasted_iota(jnp.int32, (LANES, LANES), 1)
    ahead = (source - cell) & (LANES - 1)
    first = jnp.zeros((LANES, LANES), jnp.float32)
    second = jnp.where(ahead == 0, -490.0, 0.0)
    for step, weight in FIRST:
        first = jnp.where(ahead == step, weight, jnp.where(ahead == LANES - step, -weight, first))
    for step, weight in SECOND:
        second = jnp.where((ahead == step) | (ahead == LANES - step), weight, second)
    one = jnp.concatenate([first, second], axis=1)
    return jnp.concatenate([one, one]).astype(jnp.bfloat16)


def along_z(value, weights):
    upper = value.astype(jnp.bfloat16)
    rest = (value - upper.astype(jnp.float32)).astype(jnp.bfloat16)
    return jnp.dot(
        jnp.concatenate([upper, rest], axis=1), weights, preferred_element_type=jnp.float32
    )


def first_diff(part):
    return (
        0.75 * (part(1) - part(-1))
        - 0.15 * (part(2) - part(-2))
        + (1.0 / 60.0) * (part(3) - part(-3))
    )


def second_diff(part):
    return (
        (-490.0 / 180.0) * part(0)
        + 1.5 * (part(1) + part(-1))
        - 0.15 * (part(2) + part(-2))
        + (1.0 / 90.0) * (part(3) + part(-3))
    )


def x_terms(planes_of, deep_of):
    grad = [first_diff(planes_of(field)) for field in range(7)]
    viscous = [
        (4.0 / 3.0) * second_diff(planes_of(0)) + (1.0 / 3.0) * first_diff(deep_of(2)),
        second_diff(planes_of(1)),
        second_diff(planes_of(2)) + (1.0 / 3.0) * first_diff(deep_of(0)),
    ]
    current = [
        first_diff(deep_of(5)),
        -second_diff(planes_of(4)),
        first_diff(deep_of(3)) - second_diff(planes_of(5)),
    ]
    return grad + viscous + current


def xy_terms(parts, side_of):
    parts = list(parts)
    parts[7] = parts[7] + (1.0 / 3.0) * first_diff(side_of(1))
    parts[8] = parts[8] + (1.0 / 3.0) * first_diff(side_of(0))
    parts[10] = parts[10] + first_diff(side_of(4))
    parts[11] = parts[11] + first_diff(side_of(3))
    return parts


def rates_of(center, force, index, inv_width, grads, viscous, curr):
    velx, vely, velz, potx, poty, potz, logr = center
    grad_x, grad_y, grad_z = grads
    field_x = grad_y[5] - grad_z[4]
    field_y = grad_z[3] - grad_x[5]
    field_z = grad_x[4] - grad_y[3] + 0.5
    lorentz = (
        curr[1] * field_z - curr[2] * field_y,
        curr[2] * field_x - curr[0] * field_z,
        curr[0] * field_y - curr[1] * field_x,
    )
    emf = (
        vely * field_z - velz * field_y,
        velz * field_x - velx * field_z,
        velx * field_y - vely * field_x,
    )
    inv_rho = jnp.exp(-logr)
    flow = -1.5 * ((index.astype(jnp.float32) + 0.5) * inv_width - 0.5)
    shear_rate = -1.5 * inv_width
    carried = vely + flow
    divu = grad_x[0] + grad_y[1] + grad_z[2]

    def advect(comp):
        return velx * grad_x[comp] + carried * grad_y[comp] + velz * grad_z[comp]

    rates = []
    for comp in range(3):
        total = (-2.0 / 3.0) * divu * grads[comp][6]
        for col in range(3):
            total = total + (grads[col][comp] + grads[comp][col]) * grads[col][6]
        rate = lorentz[comp] * inv_rho - advect(comp) - grads[comp][6] + force[comp]
        rate = rate + 0.05 * (viscous[comp] + total)
        if comp == 0:
            rate = rate + vely
        if comp == 1:
            rate = rate - (1.0 + shear_rate) * velx
        rates.append(rate)
    for comp in range(3):
        rate = emf[comp] - flow * grad_y[3 + comp] - 0.05 * curr[comp]
        if comp == 0:
            rate = rate - shear_rate * poty
        rates.append(rate)
    rates.append(-advect(6) - divu)
    return rates


def face_kernel(cells_x, state, up, down):
    up[...] = state[:, cells_x - 3 :]
    down[...] = state[:, :3]


def low_kernel(x_low, after, low):
    low[...] = x_low[...]


def row_kernel(cells_x, cells_y, state, y_near, y_far):
    y_odd = lax.axis_index("yz") % 2

    def rows(first, then):
        for field in range(7):
            for plane in range(cells_x):
                at = 3 * (field * cells_x + plane)
                first[at : at + 3] = state[field, plane, cells_y - 3 :]
                then[at : at + 3] = state[field, plane, :3]

    pl.when(y_odd == 0)(functools.partial(rows, y_near, y_far))
    pl.when(y_odd == 1)(functools.partial(rows, y_far, y_near))


def weight_kernel(weights):
    weights[...] = z_weights()


def own_z_kernel(cells_x, state, weights, forcing, dz, dzz, force, sem):
    copy = pltpu.make_async_copy(forcing, force, sem)
    copy.start()
    got = along_z(state[...].reshape(7 * cells_x * 8, LANES), weights[...])
    dz[...] = (got[:, :LANES] * (1.0 / 60.0)).reshape(7, cells_x, 8, LANES)
    dzz[...] = (got[: 5 * cells_x * 8, LANES:] * (1.0 / 180.0)).reshape(5, cells_x, 8, LANES)
    copy.wait()


def across_kernel(cells_x, state, dz, after, x_parts):
    def plane_step(plane):
        terms = x_terms(
            lambda field: lambda step: state[field, plane + step],
            lambda field: lambda step: dz[field, plane + step],
        )
        for number, term in enumerate(terms):
            x_parts[number, plane - 3] = term

    in_pairs(3, cells_x - 3, plane_step)


def side_kernel(
    cells_x, state, weights, y_far, y_near, dz, dzz, after, side_terms, block, z_block
):
    own = slice(ROW, ROW + 8)
    y_odd = lax.axis_index("yz") % 2
    block[:, :, own] = state[...]
    for number, field in enumerate(SHEAR_Z):
        z_block[number, :, own] = dz[field]
    count = 3 * cells_x
    got = along_z(
        jnp.concatenate(
            [rows[field * count : (field + 1) * count] for rows in (y_near, y_far) for field in SHEAR_Z]
        ),
        weights[:, :LANES],
    ) * (1.0 / 60.0)

    def ghosts(target, rows, begin):
        for field in range(7):
            for plane in range(cells_x):
                at = 3 * (field * cells_x + plane)
                block[field, plane, target : target + 3] = rows[at : at + 3]
        for number in range(4):
            for plane in range(cells_x):
                at = begin + 3 * (number * cells_x + plane)
                z_block[number, plane, target : target + 3] = got[at : at + 3]

    @pl.when(y_odd == 0)
    def _():
        ghosts(ROW + 8, y_near, 0)
        ghosts(ROW - 3, y_far, 4 * count)

    @pl.when(y_odd == 1)
    def _():
        ghosts(ROW - 3, y_near, 0)
        ghosts(ROW + 8, y_far, 4 * count)

    def yz_step(plane):
        def rows_of(field):
            return lambda step: block[field, plane, ROW + step : ROW + 8 + step]

        def z_rows_of(number):
            return lambda step: z_block[number, plane, ROW + step : ROW + 8 + step]

        grad = [first_diff(rows_of(field)) for field in range(7)]
        cross = [first_diff(z_rows_of(number)) for number in range(4)]
        terms = grad + [
            second_diff(rows_of(0)) + dzz[0, plane],
            (4.0 / 3.0) * second_diff(rows_of(1)) + dzz[1, plane] + (1.0 / 3.0) * cross[1],
            second_diff(rows_of(2)) + (4.0 / 3.0) * dzz[2, plane] + (1.0 / 3.0) * cross[0],
            -(second_diff(rows_of(3)) + dzz[3, plane]),
            cross[3] - dzz[4, plane],
            cross[2] - second_diff(rows_of(5)),
        ]
        for number, term in enumerate(terms):
            side_terms[number, plane] = term

    in_pairs(0, cells_x, yz_step)


def in_pairs(begin, end, step):
    def two(number, carry):
        step(begin + 2 * number)
        step(begin + 2 * number + 1)
        return carry

    lax.fori_loop(0, (end - begin) // 2, two, 0)


def corner_kernel(slabs_x, low, x_high, faces, far, near):
    where_x = lax.axis_index("gx")
    y_odd = lax.axis_index("yz") % 2
    faces[0] = low[...]
    faces[1] = x_high[...]

    def fill(to_next, to_last):
        for side in range(2):
            for number, field in enumerate(MIXED):
                for plane in range(3):
                    at = 3 * (3 * (4 * side + number) + plane)
                    to_next[at : at + 3] = faces[side, field, plane, 5:8]
                    to_last[at : at + 3] = faces[side, field, plane, 0:3]

        def sheared(side):
            for number, field in enumerate(MIXED + PLAIN):
                for plane in range(3):
                    at = 72 + 4 * (3 * number + plane)
                    row = 1 if field in MIXED else 4
                    to_next[at : at + 4] = faces[side, field, plane, row : row + 4]
                    row = 3 if field in MIXED else 0
                    to_last[at : at + 4] = faces[side, field, plane, row : row + 4]

        pl.when(where_x == 0)(functools.partial(sheared, 0))
        pl.when(where_x == slabs_x - 1)(functools.partial(sheared, 1))

    pl.when(y_odd == 0)(functools.partial(fill, near, far))
    pl.when(y_odd == 1)(functools.partial(fill, far, near))


def copies_out(parts, finals, begin, count, sems, base):
    return [
        pltpu.make_async_copy(
            part.at[field], final.at[field, pl.ds(begin, count)], sems.at[base + 7 * which + field]
        )
        for which, (part, final) in enumerate(zip(parts, finals))
        for field in range(7)
    ]


def finish(inv_width, index, center, force, old, x_parts, side, grad_z):
    rates = rates_of(
        center,
        force,
        index,
        inv_width,
        (x_parts[:7], side[:7], grad_z),
        [x_parts[7 + comp] + side[7 + comp] for comp in range(3)],
        [x_parts[10 + comp] + side[10 + comp] for comp in range(3)],
    )
    fresh = [(-5.0 / 9.0) * old[field] + 0.15 * rates[field] for field in range(7)]
    return [center[field] + (15.0 / 16.0) * fresh[field] for field in range(7)], fresh


def inner_kernel(
    cells_x, inv_width,
    state, register, forcing, dz, x_parts, side_terms,
    new_state, new_register, late_state, late_register,
    fresh_state, fresh_register, sems,
):
    first = lax.axis_index("gx") * cells_x
    early = EARLY

    def step_into(states_out, registers_out, begin):
        def plane_step(plane):
            states, registers = finish(
                inv_width,
                first + plane,
                [state[field, plane] for field in range(7)],
                [forcing[comp, plane] for comp in range(3)],
                [register[field, plane] for field in range(7)],
                xy_terms(
                    [x_parts[number, plane - 3] for number in range(13)],
                    lambda field: lambda step: side_terms[field, plane + step],
                ),
                [side_terms[number, plane] for number in range(13)],
                [dz[field, plane] for field in range(7)],
            )
            for field in range(7):
                registers_out[field, plane - begin] = registers[field]
                states_out[field, plane - begin] = states[field]

        return plane_step

    in_pairs(3, 3 + early, step_into(fresh_state, fresh_register, 3))
    copies = copies_out((fresh_state, fresh_register), (new_state, new_register), 3, early, sems, 0)
    for copy in copies:
        copy.start()
    in_pairs(3 + early, cells_x - 3, step_into(late_state, late_register, 3 + early))
    for copy in copies:
        copy.wait()


def edge_kernel(
    cells_x, slabs_x, inv_width,
    lean_tile, state, register, forcing, weights, dz, side_terms,
    planes, far, near, late_state, late_register, kept_state, kept_register,
    new_state, new_register,
    ghost, fields, deep, slope, fresh_state, fresh_register, sems,
):
    finals = (new_state, new_register)
    late = copies_out((late_state, late_register), finals, 3 + EARLY, cells_x - 6 - EARLY, sems, 0)
    for copy in late:
        copy.start()
    where_x = lax.axis_index("gx")
    y_odd = lax.axis_index("yz") % 2
    first = where_x * cells_x
    lean = lean_tile[...][0, 0]
    at_low, at_high = where_x == 0, where_x == slabs_x - 1
    for field in range(7):
        fields[0, field, 3:9] = state[field, 0:6]
        fields[1, field, 0:6] = state[field, cells_x - 6 :]
    for number, field in enumerate(DEEP):
        deep[0, number, 3:9] = dz[field, 0:6]
        deep[1, number, 0:6] = dz[field, cells_x - 6 :]
    for number, field in enumerate(MIXED):
        slope[0, number, 3:9] = side_terms[field, 0:6]
        slope[1, number, 0:6] = side_terms[field, cells_x - 6 :]
    for side in range(2):
        for field in range(7):
            for plane in range(3):
                ghost[side, field, plane, 16:24] = planes[side, field, plane]

    def put(from_last, from_next):
        for side in range(2):
            for number, field in enumerate(MIXED):
                for plane in range(3):
                    at = 3 * (3 * (4 * side + number) + plane)
                    ghost[side, field, plane, 13:16] = from_last[at : at + 3]
                    ghost[side, field, plane, 24:27] = from_next[at : at + 3]

        def sheared(side):
            for number, field in enumerate(MIXED + PLAIN):
                for plane in range(3):
                    at = 72 + 4 * (3 * number + plane)
                    row = 9 if field in MIXED else 12
                    ghost[side, field, plane, row : row + 4] = from_last[at : at + 4]
                    row = 27 if field in MIXED else 24
                    ghost[side, field, plane, row : row + 4] = from_next[at : at + 4]

        pl.when(at_low)(functools.partial(sheared, 0))
        pl.when(at_high)(functools.partial(sheared, 1))

    pl.when(y_odd == 0)(functools.partial(put, far, near))
    pl.when(y_odd == 1)(functools.partial(put, near, far))
    for side, shift in enumerate((jnp.where(at_low, lean, 0), jnp.where(at_high, -lean, 0))):
        for field in range(7):
            for plane in range(3):
                low = ghost[side, field, plane, pl.ds(shift + 13, 8)]
                if field in MIXED:
                    high = ghost[side, field, plane, pl.ds(shift + 21, 8)]
                    ghost[side, field, plane, 0:8] = low
                    ghost[side, field, plane, 8:16] = high
                    fields[side, field, plane + 6 * side] = ghost[side, field, plane, 3:11]
                else:
                    fields[side, field, plane + 6 * side] = ghost[side, field, plane, pl.ds(shift + 16, 8)]
    got = along_z(
        jnp.concatenate(
            [
                fields[side, field, 6 * side : 6 * side + 3].reshape(24, LANES)
                for side in range(2)
                for field in DEEP
            ]
        ),
        weights[:, :LANES],
    ) * (1.0 / 60.0)
    for side in range(2):
        for number in range(4):
            at = 24 * (4 * side + number)
            deep[side, number, 6 * side : 6 * side + 3] = got[at : at + 24].reshape(3, 8, LANES)
        for number, field in enumerate(MIXED):
            for plane in range(3):
                slope[side, number, plane + 6 * side] = first_diff(
                    lambda step: ghost[side, field, plane, 3 + step : 11 + step]
                )

    def copies_of(side):
        parts = (fresh_state.at[side], fresh_register.at[side])
        return copies_out(parts, finals, side * (cells_x - 3), 3, sems, 14 * (side + 1))

    for side in range(2):
        for local in range(3):
            plane = side * (cells_x - 3) + local
            states, registers = finish(
                inv_width,
                first + plane,
                [state[field, plane] for field in range(7)],
                [forcing[comp, plane] for comp in range(3)],
                [register[field, plane] for field in range(7)],
                xy_terms(
                    x_terms(
                        lambda field: lambda step: fields[side, field, local + 3 + step],
                        lambda field: lambda step: deep[side, DEEP.index(field), local + 3 + step],
                    ),
                    lambda field: lambda step: slope[side, MIXED.index(field), local + 3 + step],
                ),
                [side_terms[number, plane] for number in range(13)],
                [dz[field, plane] for field in range(7)],
            )
            for field in range(7):
                fresh_register[side, field, local] = registers[field]
                fresh_state[side, field, local] = states[field]
        for copy in copies_of(side):
            copy.start()
    for copy in late + copies_of(0) + copies_of(1):
        copy.wait()


def per_device(slabs_x, slabs_y, state, register, forcing, y_shift):
    cells_x, cells_y = state.shape[1], state.shape[2]
    total_x, total_y = cells_x * slabs_x, cells_y * slabs_y
    offset = y_shift[0]
    steps = (offset + cells_y // 2) // cells_y

    def shape(*dims):
        return jax.ShapeDtypeStruct(dims, jnp.float32)

    vmem = pl.BlockSpec(memory_space=pltpu.VMEM)
    anyspace = pl.BlockSpec(memory_space=pl.ANY)
    params = pltpu.CompilerParams(vmem_limit_bytes=VMEM)
    lean = lax.optimization_barrier(jnp.full((8, LANES), offset - steps * cells_y, jnp.int32))

    digit = min(slabs_y, 8)

    def place(slab, along):
        return along % slabs_y * slabs_x + slab

    def send(value, pairs):
        return lax.ppermute(value, ("yz", "gx"), pairs)

    def both(pairs):
        return pairs + [(b, a) for a, b in pairs]

    def y_pairs(odd):
        return both(
            [(place(slab, j), place(slab, j + 1)) for slab in range(slabs_x) for j in range(odd, slabs_y, 2)]
        )

    def upward(by):
        pairs = [(place(slab, j), place(slab + 1, j)) for slab in range(last) for j in range(slabs_y)]
        return pairs + [(place(last, j + by), place(0, j)) for j in range(slabs_y)]

    def downward(by):
        pairs = [(place(slab + 1, j), place(slab, j)) for slab in range(last) for j in range(slabs_y)]
        return pairs + [(place(0, j - by), place(last, j)) for j in range(slabs_y)]

    last = slabs_x - 1

    def cost(flops, moved=10**6):
        return pl.CostEstimate(flops=flops, bytes_accessed=moved, transcendentals=0)

    weights = pl.pallas_call(
        weight_kernel,
        out_shape=jax.ShapeDtypeStruct((2 * LANES, 2 * LANES), jnp.bfloat16),
        out_specs=vmem,
        compiler_params=params,
        cost_estimate=cost(2 * 10**8),
    )()

    def in_hbm(value):
        return pltpu.with_memory_space_constraint(value, pltpu.HBM)

    def faces_of(state):
        return pl.pallas_call(
            functools.partial(face_kernel, cells_x),
            out_shape=[shape(7, 3, cells_y, LANES)] * 2,
            in_specs=[vmem],
            out_specs=[vmem] * 2,
            compiler_params=params,
        )(state)

    up = down = None
    if slabs_y > digit:
        up, down = faces_of(state)
        where_x = lax.axis_index("gx")
        at_low, at_high = where_x == 0, where_x == last
        groups = steps // digit
        amount = jnp.where(at_high, groups, slabs_y // digit - groups) % (slabs_y // digit)
        across = jnp.where(at_high, up, down)
        hop = 1
        while hop < slabs_y // digit:
            pairs = [(i, (i - hop * digit) % slabs_y) for i in range(slabs_y)]
            moved = lax.ppermute(across, "yz", pairs)
            across = jnp.where((amount // hop) % 2 == 1, moved, across)
            hop *= 2
        up = jnp.where(at_high, across, up)
        down = jnp.where(at_low, across, down)

    def exchange(by, operands):
        up, down, state, register, forcing, weights, lean = operands
        plane = state.shape[1:]
        if up is None:
            up, down = faces_of(state)
        x_low = send(up, upward(by))
        x_high = send(down, downward(by))
        y_near, y_far = pl.pallas_call(
            functools.partial(row_kernel, cells_x, cells_y),
            out_shape=[shape(21 * cells_x, LANES), shape(21 * cells_x, LANES)],
            in_specs=[vmem],
            out_specs=[vmem] * 2,
            compiler_params=params,
        )(state)
        y_far = send(y_far, y_pairs(1))
        y_near = send(y_near, y_pairs(0))
        hbm = pl.BlockSpec(memory_space=pltpu.HBM)
        dz, dzz, force = pl.pallas_call(
            functools.partial(own_z_kernel, cells_x),
            out_shape=[shape(7, *plane), shape(5, *plane), shape(*forcing.shape)],
            in_specs=[vmem] * 2 + [hbm],
            out_specs=[vmem] * 3,
            scratch_shapes=[pltpu.SemaphoreType.DMA],
            compiler_params=params,
            cost_estimate=cost(10**8),
        )(state, weights, forcing)
        low = pl.pallas_call(
            low_kernel,
            out_shape=shape(*up.shape),
            in_specs=[vmem, anyspace],
            out_specs=vmem,
            compiler_params=params,
            cost_estimate=cost(LOW, 1),
        )(x_low, dz)
        faces, far, near = pl.pallas_call(
            functools.partial(corner_kernel, slabs_x),
            out_shape=[shape(2, *up.shape), shape(160, LANES), shape(160, LANES)],
            in_specs=[vmem] * 2,
            out_specs=[vmem] * 3,
            compiler_params=params,
            cost_estimate=cost(1, 1),
        )(low, x_high)
        far = send(far, y_pairs(1))
        near = send(near, y_pairs(0))
        x_parts = pl.pallas_call(
            functools.partial(across_kernel, cells_x),
            out_shape=shape(13, cells_x - 6, *plane[1:]),
            in_specs=[vmem] * 2 + [anyspace],
            out_specs=vmem,
            compiler_params=params,
            cost_estimate=cost(1, 1),
        )(state, dz, faces)
        side_terms = pl.pallas_call(
            functools.partial(side_kernel, cells_x),
            out_shape=shape(13, *plane),
            in_specs=[vmem] * 6 + [anyspace],
            out_specs=vmem,
            scratch_shapes=[
                pltpu.VMEM((7, cells_x, TALL, LANES), jnp.float32),
                pltpu.VMEM((4, cells_x, TALL, LANES), jnp.float32),
            ],
            compiler_params=params,
            cost_estimate=cost(2 * 10**8),
        )(state, weights, y_far, y_near, dz, dzz, x_parts)
        early, late = EARLY, cells_x - 6 - EARLY
        new_state, new_register, late_state, late_register = pl.pallas_call(
            functools.partial(inner_kernel, cells_x, 1.0 / total_x),
            out_shape=[shape(*state.shape)] * 2 + [shape(7, late, *plane[1:])] * 2,
            in_specs=[vmem] * 6,
            out_specs=[anyspace] * 2 + [vmem] * 2,
            scratch_shapes=[
                pltpu.VMEM((7, early, *plane[1:]), jnp.float32),
                pltpu.VMEM((7, early, *plane[1:]), jnp.float32),
                pltpu.SemaphoreType.DMA((14,)),
            ],
            compiler_params=params,
            cost_estimate=cost(2 * 10**8),
        )(state, register, force, dz, x_parts, side_terms)
        return pl.pallas_call(
            functools.partial(edge_kernel, cells_x, slabs_x, 1.0 / total_x),
            out_shape=[shape(*state.shape)] * 2,
            in_specs=[vmem] * 12 + [anyspace] * 2,
            out_specs=[anyspace] * 2,
            input_output_aliases={12: 0, 13: 1},
            scratch_shapes=[
                pltpu.VMEM((2, 7, 3, 40, LANES), jnp.float32),
                pltpu.VMEM((2, 7, 9, 8, LANES), jnp.float32),
                pltpu.VMEM((2, 4, 9, 8, LANES), jnp.float32),
                pltpu.VMEM((2, 4, 9, 8, LANES), jnp.float32),
                pltpu.VMEM((2, 7, 3, 8, LANES), jnp.float32),
                pltpu.VMEM((2, 7, 3, 8, LANES), jnp.float32),
                pltpu.SemaphoreType.DMA((42,)),
            ],
            compiler_params=params,
        )(
            lean, state, register, force, weights, dz, side_terms,
            faces, far, near, late_state, late_register, new_state, new_register,
        )

    return lax.switch(
        steps % digit,
        [functools.partial(exchange, by) for by in range(digit)],
        (up, down, state, register, in_hbm(forcing), weights, lean),
    )


def solution(mesh):
    spec = P(None, "gx", "yz", None)
    return jax.shard_map(
        functools.partial(per_device, mesh.shape["gx"], mesh.shape["yz"]),
        mesh=mesh,
        in_specs=(spec, spec, spec, P()),
        out_specs=(spec, spec),
        check_vma=False,
    )
```

```python
import functools

import jax
import jax.numpy as jnp
from jax import lax
from jax.experimental import pallas as pl
from jax.experimental.pallas import tpu as pltpu
from jax.sharding import PartitionSpec as P

LANES = 128
FIRST = ((1, 45.0), (2, -9.0), (3, 1.0))
SECOND = ((1, 270.0), (2, -27.0), (3, 2.0))
MIXED = (0, 1, 3, 4)
PLAIN = (2, 5, 6)
DEEP = (0, 2, 3, 5)
SHEAR_Z = (1, 2, 4, 5)
ROW = 8
NEAR = 6 * 10**8
EARLY = 4
TALL = 24
VMEM = 32 * 1024 * 1024


def z_weights():
    source = lax.broadcasted_iota(jnp.int32, (LANES, LANES), 0)
    cell = lax.broadcasted_iota(jnp.int32, (LANES, LANES), 1)
    ahead = (source - cell) & (LANES - 1)
    first = jnp.zeros((LANES, LANES), jnp.float32)
    second = jnp.where(ahead == 0, -490.0, 0.0)
    for step, weight in FIRST:
        first = jnp.where(ahead == step, weight, jnp.where(ahead == LANES - step, -weight, first))
    for step, weight in SECOND:
        second = jnp.where((ahead == step) | (ahead == LANES - step), weight, second)
    one = jnp.concatenate([first, second], axis=1)
    return jnp.concatenate([one, one]).astype(jnp.bfloat16)


def along_z(value, weights):
    upper = value.astype(jnp.bfloat16)
    rest = (value - upper.astype(jnp.float32)).astype(jnp.bfloat16)
    return jnp.dot(
        jnp.concatenate([upper, rest], axis=1), weights, preferred_element_type=jnp.float32
    )


def first_diff(part):
    return (
        0.75 * (part(1) - part(-1))
        - 0.15 * (part(2) - part(-2))
        + (1.0 / 60.0) * (part(3) - part(-3))
    )


def second_diff(part):
    return (
        (-490.0 / 180.0) * part(0)
        + 1.5 * (part(1) + part(-1))
        - 0.15 * (part(2) + part(-2))
        + (1.0 / 90.0) * (part(3) + part(-3))
    )


def x_terms(planes_of, deep_of):
    grad = [first_diff(planes_of(field)) for field in range(7)]
    viscous = [
        (4.0 / 3.0) * second_diff(planes_of(0)) + (1.0 / 3.0) * first_diff(deep_of(2)),
        second_diff(planes_of(1)),
        second_diff(planes_of(2)) + (1.0 / 3.0) * first_diff(deep_of(0)),
    ]
    current = [
        first_diff(deep_of(5)),
        -second_diff(planes_of(4)),
        first_diff(deep_of(3)) - second_diff(planes_of(5)),
    ]
    return grad + viscous + current


def xy_terms(parts, side_of):
    parts = list(parts)
    parts[7] = parts[7] + (1.0 / 3.0) * first_diff(side_of(1))
    parts[8] = parts[8] + (1.0 / 3.0) * first_diff(side_of(0))
    parts[10] = parts[10] + first_diff(side_of(4))
    parts[11] = parts[11] + first_diff(side_of(3))
    return parts


def rates_of(center, force, index, inv_width, grads, viscous, curr):
    velx, vely, velz, potx, poty, potz, logr = center
    grad_x, grad_y, grad_z = grads
    field_x = grad_y[5] - grad_z[4]
    field_y = grad_z[3] - grad_x[5]
    field_z = grad_x[4] - grad_y[3] + 0.5
    lorentz = (
        curr[1] * field_z - curr[2] * field_y,
        curr[2] * field_x - curr[0] * field_z,
        curr[0] * field_y - curr[1] * field_x,
    )
    emf = (
        vely * field_z - velz * field_y,
        velz * field_x - velx * field_z,
        velx * field_y - vely * field_x,
    )
    inv_rho = jnp.exp(-logr)
    flow = -1.5 * ((index.astype(jnp.float32) + 0.5) * inv_width - 0.5)
    shear_rate = -1.5 * inv_width
    carried = vely + flow
    divu = grad_x[0] + grad_y[1] + grad_z[2]

    def advect(comp):
        return velx * grad_x[comp] + carried * grad_y[comp] + velz * grad_z[comp]

    rates = []
    for comp in range(3):
        total = (-2.0 / 3.0) * divu * grads[comp][6]
        for col in range(3):
            total = total + (grads[col][comp] + grads[comp][col]) * grads[col][6]
        rate = lorentz[comp] * inv_rho - advect(comp) - grads[comp][6] + force[comp]
        rate = rate + 0.05 * (viscous[comp] + total)
        if comp == 0:
            rate = rate + vely
        if comp == 1:
            rate = rate - (1.0 + shear_rate) * velx
        rates.append(rate)
    for comp in range(3):
        rate = emf[comp] - flow * grad_y[3 + comp] - 0.05 * curr[comp]
        if comp == 0:
            rate = rate - shear_rate * poty
        rates.append(rate)
    rates.append(-advect(6) - divu)
    return rates


def face_kernel(cells_x, state, up, down):
    up[...] = state[:, cells_x - 3 :]
    down[...] = state[:, :3]


def keep_kernel(received, after, kept):
    kept[...] = received[...]


def row_kernel(cells_x, cells_y, state, y_near, y_far):
    y_odd = lax.axis_index("yz") % 2

    def rows(first, then):
        for field in range(7):
            for plane in range(cells_x):
                at = 3 * (field * cells_x + plane)
                first[at : at + 3] = state[field, plane, cells_y - 3 :]
                then[at : at + 3] = state[field, plane, :3]

    pl.when(y_odd == 0)(functools.partial(rows, y_near, y_far))
    pl.when(y_odd == 1)(functools.partial(rows, y_far, y_near))


def weight_kernel(weights):
    weights[...] = z_weights()


def own_z_kernel(cells_x, state, weights, forcing, dz, dzz, force, sem):
    copy = pltpu.make_async_copy(forcing, force, sem)
    copy.start()
    got = along_z(state[...].reshape(7 * cells_x * 8, LANES), weights[...])
    dz[...] = (got[:, :LANES] * (1.0 / 60.0)).reshape(7, cells_x, 8, LANES)
    dzz[...] = (got[: 5 * cells_x * 8, LANES:] * (1.0 / 180.0)).reshape(5, cells_x, 8, LANES)
    copy.wait()


def across_kernel(cells_x, state, dz, after, x_parts):
    def plane_step(plane):
        terms = x_terms(
            lambda field: lambda step: state[field, plane + step],
            lambda field: lambda step: dz[field, plane + step],
        )
        for number, term in enumerate(terms):
            x_parts[number, plane - 3] = term

    in_pairs(3, cells_x - 3, plane_step)


def side_kernel(
    cells_x, state, weights, y_far, y_near, dz, dzz, after, side_terms, block, z_block
):
    own = slice(ROW, ROW + 8)
    y_odd = lax.axis_index("yz") % 2
    block[:, :, own] = state[...]
    for number, field in enumerate(SHEAR_Z):
        z_block[number, :, own] = dz[field]
    count = 3 * cells_x
    got = along_z(
        jnp.concatenate(
            [rows[field * count : (field + 1) * count] for rows in (y_near, y_far) for field in SHEAR_Z]
        ),
        weights[:, :LANES],
    ) * (1.0 / 60.0)

    def ghosts(target, rows, begin):
        for field in range(7):
            for plane in range(cells_x):
                at = 3 * (field * cells_x + plane)
                block[field, plane, target : target + 3] = rows[at : at + 3]
        for number in range(4):
            for plane in range(cells_x):
                at = begin + 3 * (number * cells_x + plane)
                z_block[number, plane, target : target + 3] = got[at : at + 3]

    @pl.when(y_odd == 0)
    def _():
        ghosts(ROW + 8, y_near, 0)
        ghosts(ROW - 3, y_far, 4 * count)

    @pl.when(y_odd == 1)
    def _():
        ghosts(ROW - 3, y_near, 0)
        ghosts(ROW + 8, y_far, 4 * count)

    def yz_step(plane):
        def rows_of(field):
            return lambda step: block[field, plane, ROW + step : ROW + 8 + step]

        def z_rows_of(number):
            return lambda step: z_block[number, plane, ROW + step : ROW + 8 + step]

        grad = [first_diff(rows_of(field)) for field in range(7)]
        cross = [first_diff(z_rows_of(number)) for number in range(4)]
        terms = grad + [
            second_diff(rows_of(0)) + dzz[0, plane],
            (4.0 / 3.0) * second_diff(rows_of(1)) + dzz[1, plane] + (1.0 / 3.0) * cross[1],
            second_diff(rows_of(2)) + (4.0 / 3.0) * dzz[2, plane] + (1.0 / 3.0) * cross[0],
            -(second_diff(rows_of(3)) + dzz[3, plane]),
            cross[3] - dzz[4, plane],
            cross[2] - second_diff(rows_of(5)),
        ]
        for number, term in enumerate(terms):
            side_terms[number, plane] = term

    in_pairs(0, cells_x, yz_step)


def in_pairs(begin, end, step):
    def two(number, carry):
        step(begin + 2 * number)
        step(begin + 2 * number + 1)
        return carry

    lax.fori_loop(0, (end - begin) // 2, two, 0)


def corner_kernel(slabs_x, low, high, wrapped, faces, far, near):
    where_x = lax.axis_index("gx")
    y_odd = lax.axis_index("yz") % 2
    faces[0] = low[...]

    def take(source):
        faces[1] = source[...]

    pl.when(where_x != slabs_x - 1)(functools.partial(take, high))
    pl.when(where_x == slabs_x - 1)(functools.partial(take, wrapped))

    def fill(to_next, to_last):
        for side in range(2):
            for number, field in enumerate(MIXED):
                for plane in range(3):
                    at = 3 * (3 * (4 * side + number) + plane)
                    to_next[at : at + 3] = faces[side, field, plane, 5:8]
                    to_last[at : at + 3] = faces[side, field, plane, 0:3]

        def sheared(side):
            for number, field in enumerate(MIXED + PLAIN):
                for plane in range(3):
                    at = 72 + 4 * (3 * number + plane)
                    row = 1 if field in MIXED else 4
                    to_next[at : at + 4] = faces[side, field, plane, row : row + 4]
                    row = 3 if field in MIXED else 0
                    to_last[at : at + 4] = faces[side, field, plane, row : row + 4]

        pl.when(where_x == 0)(functools.partial(sheared, 0))
        pl.when(where_x == slabs_x - 1)(functools.partial(sheared, 1))

    pl.when(y_odd == 0)(functools.partial(fill, near, far))
    pl.when(y_odd == 1)(functools.partial(fill, far, near))


def copies_out(parts, finals, begin, count, sems, base):
    return [
        pltpu.make_async_copy(
            part.at[field], final.at[field, pl.ds(begin, count)], sems.at[base + 7 * which + field]
        )
        for which, (part, final) in enumerate(zip(parts, finals))
        for field in range(7)
    ]


def finish(inv_width, index, center, force, old, x_parts, side, grad_z):
    rates = rates_of(
        center,
        force,
        index,
        inv_width,
        (x_parts[:7], side[:7], grad_z),
        [x_parts[7 + comp] + side[7 + comp] for comp in range(3)],
        [x_parts[10 + comp] + side[10 + comp] for comp in range(3)],
    )
    fresh = [(-5.0 / 9.0) * old[field] + 0.15 * rates[field] for field in range(7)]
    return [center[field] + (15.0 / 16.0) * fresh[field] for field in range(7)], fresh


def inner_kernel(
    cells_x, inv_width,
    state, register, forcing, dz, x_parts, side_terms,
    new_state, new_register, late_state, late_register,
    fresh_state, fresh_register, sems,
):
    first = lax.axis_index("gx") * cells_x
    early = EARLY

    def step_into(states_out, registers_out, begin):
        def plane_step(plane):
            states, registers = finish(
                inv_width,
                first + plane,
                [state[field, plane] for field in range(7)],
                [forcing[comp, plane] for comp in range(3)],
                [register[field, plane] for field in range(7)],
                xy_terms(
                    [x_parts[number, plane - 3] for number in range(13)],
                    lambda field: lambda step: side_terms[field, plane + step],
                ),
                [side_terms[number, plane] for number in range(13)],
                [dz[field, plane] for field in range(7)],
            )
            for field in range(7):
                registers_out[field, plane - begin] = registers[field]
                states_out[field, plane - begin] = states[field]

        return plane_step

    in_pairs(3, 3 + early, step_into(fresh_state, fresh_register, 3))
    copies = copies_out((fresh_state, fresh_register), (new_state, new_register), 3, early, sems, 0)
    for copy in copies:
        copy.start()
    in_pairs(3 + early, cells_x - 3, step_into(late_state, late_register, 3 + early))
    for copy in copies:
        copy.wait()


def edge_kernel(
    cells_x, slabs_x, inv_width,
    lean_tile, state, register, forcing, weights, dz, side_terms,
    planes, far, near, late_state, late_register, kept_state, kept_register,
    new_state, new_register,
    ghost, fields, deep, slope, fresh_state, fresh_register, sems,
):
    finals = (new_state, new_register)
    late = copies_out((late_state, late_register), finals, 3 + EARLY, cells_x - 6 - EARLY, sems, 0)
    for copy in late:
        copy.start()
    where_x = lax.axis_index("gx")
    y_odd = lax.axis_index("yz") % 2
    first = where_x * cells_x
    lean = lean_tile[...][0, 0]
    at_low, at_high = where_x == 0, where_x == slabs_x - 1
    for field in range(7):
        fields[0, field, 3:9] = state[field, 0:6]
        fields[1, field, 0:6] = state[field, cells_x - 6 :]
    for number, field in enumerate(DEEP):
        deep[0, number, 3:9] = dz[field, 0:6]
        deep[1, number, 0:6] = dz[field, cells_x - 6 :]
    for number, field in enumerate(MIXED):
        slope[0, number, 3:9] = side_terms[field, 0:6]
        slope[1, number, 0:6] = side_terms[field, cells_x - 6 :]
    for side in range(2):
        for field in range(7):
            for plane in range(3):
                ghost[side, field, plane, 16:24] = planes[side, field, plane]

    def put(from_last, from_next):
        for side in range(2):
            for number, field in enumerate(MIXED):
                for plane in range(3):
                    at = 3 * (3 * (4 * side + number) + plane)
                    ghost[side, field, plane, 13:16] = from_last[at : at + 3]
                    ghost[side, field, plane, 24:27] = from_next[at : at + 3]

        def sheared(side):
            for number, field in enumerate(MIXED + PLAIN):
                for plane in range(3):
                    at = 72 + 4 * (3 * number + plane)
                    row = 9 if field in MIXED else 12
                    ghost[side, field, plane, row : row + 4] = from_last[at : at + 4]
                    row = 27 if field in MIXED else 24
                    ghost[side, field, plane, row : row + 4] = from_next[at : at + 4]

        pl.when(at_low)(functools.partial(sheared, 0))
        pl.when(at_high)(functools.partial(sheared, 1))

    pl.when(y_odd == 0)(functools.partial(put, far, near))
    pl.when(y_odd == 1)(functools.partial(put, near, far))
    for side, shift in enumerate((jnp.where(at_low, lean, 0), jnp.where(at_high, -lean, 0))):
        for field in range(7):
            for plane in range(3):
                low = ghost[side, field, plane, pl.ds(shift + 13, 8)]
                if field in MIXED:
                    high = ghost[side, field, plane, pl.ds(shift + 21, 8)]
                    ghost[side, field, plane, 0:8] = low
                    ghost[side, field, plane, 8:16] = high
                    fields[side, field, plane + 6 * side] = ghost[side, field, plane, 3:11]
                else:
                    fields[side, field, plane + 6 * side] = ghost[side, field, plane, pl.ds(shift + 16, 8)]
    got = along_z(
        jnp.concatenate(
            [
                fields[side, field, 6 * side : 6 * side + 3].reshape(24, LANES)
                for side in range(2)
                for field in DEEP
            ]
        ),
        weights[:, :LANES],
    ) * (1.0 / 60.0)
    for side in range(2):
        for number in range(4):
            at = 24 * (4 * side + number)
            deep[side, number, 6 * side : 6 * side + 3] = got[at : at + 24].reshape(3, 8, LANES)
        for number, field in enumerate(MIXED):
            for plane in range(3):
                slope[side, number, plane + 6 * side] = first_diff(
                    lambda step: ghost[side, field, plane, 3 + step : 11 + step]
                )

    def copies_of(side):
        parts = (fresh_state.at[side], fresh_register.at[side])
        return copies_out(parts, finals, side * (cells_x - 3), 3, sems, 14 * (side + 1))

    for side in range(2):
        for local in range(3):
            plane = side * (cells_x - 3) + local
            states, registers = finish(
                inv_width,
                first + plane,
                [state[field, plane] for field in range(7)],
                [forcing[comp, plane] for comp in range(3)],
                [register[field, plane] for field in range(7)],
                xy_terms(
                    x_terms(
                        lambda field: lambda step: fields[side, field, local + 3 + step],
                        lambda field: lambda step: deep[side, DEEP.index(field), local + 3 + step],
                    ),
                    lambda field: lambda step: slope[side, MIXED.index(field), local + 3 + step],
                ),
                [side_terms[number, plane] for number in range(13)],
                [dz[field, plane] for field in range(7)],
            )
            for field in range(7):
                fresh_register[side, field, local] = registers[field]
                fresh_state[side, field, local] = states[field]
        for copy in copies_of(side):
            copy.start()
    for copy in late + copies_of(0) + copies_of(1):
        copy.wait()


def per_device(slabs_x, slabs_y, state, register, forcing, y_shift):
    cells_x, cells_y = state.shape[1], state.shape[2]
    total_x, total_y = cells_x * slabs_x, cells_y * slabs_y
    offset = y_shift[0]
    steps = (offset + cells_y // 2) // cells_y

    def shape(*dims):
        return jax.ShapeDtypeStruct(dims, jnp.float32)

    vmem = pl.BlockSpec(memory_space=pltpu.VMEM)
    anyspace = pl.BlockSpec(memory_space=pl.ANY)
    params = pltpu.CompilerParams(vmem_limit_bytes=VMEM)
    lean = lax.optimization_barrier(jnp.full((8, LANES), offset - steps * cells_y, jnp.int32))

    digit = min(slabs_y, 8)

    def place(slab, along):
        return along % slabs_y * slabs_x + slab

    def send(value, pairs):
        return lax.ppermute(value, ("yz", "gx"), pairs)

    def both(pairs):
        return pairs + [(b, a) for a, b in pairs]

    def y_pairs(odd):
        return both(
            [(place(slab, j), place(slab, j + 1)) for slab in range(slabs_x) for j in range(odd, slabs_y, 2)]
        )

    def upward(by):
        pairs = [(place(slab, j), place(slab + 1, j)) for slab in range(last) for j in range(slabs_y)]
        return pairs + [(place(last, j + by), place(0, j)) for j in range(slabs_y)]

    def downward():
        return [(place(slab + 1, j), place(slab, j)) for slab in range(last) for j in range(slabs_y)]

    def around(by):
        return [(place(0, j - by), place(last, j)) for j in range(slabs_y)]

    last = slabs_x - 1

    def cost(flops, moved=10**6):
        return pl.CostEstimate(flops=flops, bytes_accessed=moved, transcendentals=0)

    weights = pl.pallas_call(
        weight_kernel,
        out_shape=jax.ShapeDtypeStruct((2 * LANES, 2 * LANES), jnp.bfloat16),
        out_specs=vmem,
        compiler_params=params,
        cost_estimate=cost(2 * 10**8),
    )()

    def in_hbm(value):
        return pltpu.with_memory_space_constraint(value, pltpu.HBM)

    def faces_of(state):
        return pl.pallas_call(
            functools.partial(face_kernel, cells_x),
            out_shape=[shape(7, 3, cells_y, LANES)] * 2,
            in_specs=[vmem],
            out_specs=[vmem] * 2,
            compiler_params=params,
        )(state)

    up = down = None
    if slabs_y > digit:
        up, down = faces_of(state)
        where_x = lax.axis_index("gx")
        at_low, at_high = where_x == 0, where_x == last
        groups = steps // digit
        amount = jnp.where(at_high, groups, slabs_y // digit - groups) % (slabs_y // digit)
        across = jnp.where(at_high, up, down)
        hop = 1
        while hop < slabs_y // digit:
            pairs = [(i, (i - hop * digit) % slabs_y) for i in range(slabs_y)]
            moved = lax.ppermute(across, "yz", pairs)
            across = jnp.where((amount // hop) % 2 == 1, moved, across)
            hop *= 2
        up = jnp.where(at_high, across, up)
        down = jnp.where(at_low, across, down)

    def exchange(by, operands):
        up, down, state, register, forcing, weights, lean = operands
        plane = state.shape[1:]
        if up is None:
            up, down = faces_of(state)
        x_high = send(down, downward())
        x_low = send(up, upward(by))
        y_near, y_far = pl.pallas_call(
            functools.partial(row_kernel, cells_x, cells_y),
            out_shape=[shape(21 * cells_x, LANES), shape(21 * cells_x, LANES)],
            in_specs=[vmem],
            out_specs=[vmem] * 2,
            compiler_params=params,
        )(state)
        y_far = send(y_far, y_pairs(1))
        y_near = send(y_near, y_pairs(0))
        hbm = pl.BlockSpec(memory_space=pltpu.HBM)
        dz, dzz, force = pl.pallas_call(
            functools.partial(own_z_kernel, cells_x),
            out_shape=[shape(7, *plane), shape(5, *plane), shape(*forcing.shape)],
            in_specs=[vmem] * 2 + [hbm],
            out_specs=[vmem] * 3,
            scratch_shapes=[pltpu.SemaphoreType.DMA],
            compiler_params=params,
            cost_estimate=cost(10**8),
        )(state, weights, forcing)

        def keep(received, after):
            return pl.pallas_call(
                keep_kernel,
                out_shape=shape(*up.shape),
                in_specs=[vmem, anyspace],
                out_specs=vmem,
                compiler_params=params,
                cost_estimate=cost(NEAR, 1),
            )(received, after)

        high = keep(x_high, dz)
        low = keep(x_low, high)
        wrapped = send(down, around(by))
        faces, far, near = pl.pallas_call(
            functools.partial(corner_kernel, slabs_x),
            out_shape=[shape(2, *up.shape), shape(160, LANES), shape(160, LANES)],
            in_specs=[vmem] * 3,
            out_specs=[vmem] * 3,
            compiler_params=params,
            cost_estimate=cost(1, 1),
        )(low, high, wrapped)
        far = send(far, y_pairs(1))
        near = send(near, y_pairs(0))
        x_parts = pl.pallas_call(
            functools.partial(across_kernel, cells_x),
            out_shape=shape(13, cells_x - 6, *plane[1:]),
            in_specs=[vmem] * 2 + [anyspace],
            out_specs=vmem,
            compiler_params=params,
            cost_estimate=cost(1, 1),
        )(state, dz, faces)
        side_terms = pl.pallas_call(
            functools.partial(side_kernel, cells_x),
            out_shape=shape(13, *plane),
            in_specs=[vmem] * 6 + [anyspace],
            out_specs=vmem,
            scratch_shapes=[
                pltpu.VMEM((7, cells_x, TALL, LANES), jnp.float32),
                pltpu.VMEM((4, cells_x, TALL, LANES), jnp.float32),
            ],
            compiler_params=params,
            cost_estimate=cost(2 * 10**8),
        )(state, weights, y_far, y_near, dz, dzz, x_parts)
        early, late = EARLY, cells_x - 6 - EARLY
        new_state, new_register, late_state, late_register = pl.pallas_call(
            functools.partial(inner_kernel, cells_x, 1.0 / total_x),
            out_shape=[shape(*state.shape)] * 2 + [shape(7, late, *plane[1:])] * 2,
            in_specs=[vmem] * 6,
            out_specs=[anyspace] * 2 + [vmem] * 2,
            scratch_shapes=[
                pltpu.VMEM((7, early, *plane[1:]), jnp.float32),
                pltpu.VMEM((7, early, *plane[1:]), jnp.float32),
                pltpu.SemaphoreType.DMA((14,)),
            ],
            compiler_params=params,
            cost_estimate=cost(2 * 10**8),
        )(state, register, force, dz, x_parts, side_terms)
        return pl.pallas_call(
            functools.partial(edge_kernel, cells_x, slabs_x, 1.0 / total_x),
            out_shape=[shape(*state.shape)] * 2,
            in_specs=[vmem] * 12 + [anyspace] * 2,
            out_specs=[anyspace] * 2,
            input_output_aliases={12: 0, 13: 1},
            scratch_shapes=[
                pltpu.VMEM((2, 7, 3, 40, LANES), jnp.float32),
                pltpu.VMEM((2, 7, 9, 8, LANES), jnp.float32),
                pltpu.VMEM((2, 4, 9, 8, LANES), jnp.float32),
                pltpu.VMEM((2, 4, 9, 8, LANES), jnp.float32),
                pltpu.VMEM((2, 7, 3, 8, LANES), jnp.float32),
                pltpu.VMEM((2, 7, 3, 8, LANES), jnp.float32),
                pltpu.SemaphoreType.DMA((42,)),
            ],
            compiler_params=params,
        )(
            lean, state, register, force, weights, dz, side_terms,
            faces, far, near, late_state, late_register, new_state, new_register,
        )

    return lax.switch(
        steps % digit,
        [functools.partial(exchange, by) for by in range(digit)],
        (up, down, state, register, in_hbm(forcing), weights, lean),
    )


def solution(mesh):
    spec = P(None, "gx", "yz", None)
    return jax.shard_map(
        functools.partial(per_device, mesh.shape["gx"], mesh.shape["yz"]),
        mesh=mesh,
        in_specs=(spec, spec, spec, P()),
        out_specs=(spec, spec),
        check_vma=False,
    )
```

```python
import functools

import jax
import jax.numpy as jnp
from jax import lax
from jax.experimental import pallas as pl
from jax.experimental.pallas import tpu as pltpu
from jax.sharding import PartitionSpec as P

LANES = 128
FIRST = ((1, 45.0), (2, -9.0), (3, 1.0))
SECOND = ((1, 270.0), (2, -27.0), (3, 2.0))
MIXED = (0, 1, 3, 4)
PLAIN = (2, 5, 6)
DEEP = (0, 2, 3, 5)
SHEAR_Z = (1, 2, 4, 5)
ROW = 8
CORNER = 10**10
ACROSS = 10**7
EARLY = 6
TALL = 24
VMEM = 32 * 1024 * 1024


def z_weights():
    source = lax.broadcasted_iota(jnp.int32, (LANES, LANES), 0)
    cell = lax.broadcasted_iota(jnp.int32, (LANES, LANES), 1)
    ahead = (source - cell) & (LANES - 1)
    first = jnp.zeros((LANES, LANES), jnp.float32)
    second = jnp.where(ahead == 0, -490.0, 0.0)
    for step, weight in FIRST:
        first = jnp.where(ahead == step, weight, jnp.where(ahead == LANES - step, -weight, first))
    for step, weight in SECOND:
        second = jnp.where((ahead == step) | (ahead == LANES - step), weight, second)
    one = jnp.concatenate([first, second], axis=1)
    return jnp.concatenate([one, one]).astype(jnp.bfloat16)


def along_z(value, weights):
    upper = value.astype(jnp.bfloat16)
    rest = (value - upper.astype(jnp.float32)).astype(jnp.bfloat16)
    return jnp.dot(
        jnp.concatenate([upper, rest], axis=1), weights, preferred_element_type=jnp.float32
    )


def first_diff(part):
    return (
        0.75 * (part(1) - part(-1))
        - 0.15 * (part(2) - part(-2))
        + (1.0 / 60.0) * (part(3) - part(-3))
    )


def second_diff(part):
    return (
        (-490.0 / 180.0) * part(0)
        + 1.5 * (part(1) + part(-1))
        - 0.15 * (part(2) + part(-2))
        + (1.0 / 90.0) * (part(3) + part(-3))
    )


def x_terms(planes_of, deep_of):
    grad = [first_diff(planes_of(field)) for field in range(7)]
    viscous = [
        (4.0 / 3.0) * second_diff(planes_of(0)) + (1.0 / 3.0) * first_diff(deep_of(2)),
        second_diff(planes_of(1)),
        second_diff(planes_of(2)) + (1.0 / 3.0) * first_diff(deep_of(0)),
    ]
    current = [
        first_diff(deep_of(5)),
        -second_diff(planes_of(4)),
        first_diff(deep_of(3)) - second_diff(planes_of(5)),
    ]
    return grad + viscous + current


def xy_terms(parts, side_of):
    parts = list(parts)
    parts[7] = parts[7] + (1.0 / 3.0) * first_diff(side_of(1))
    parts[8] = parts[8] + (1.0 / 3.0) * first_diff(side_of(0))
    parts[10] = parts[10] + first_diff(side_of(4))
    parts[11] = parts[11] + first_diff(side_of(3))
    return parts


def rates_of(center, force, index, inv_width, grads, viscous, curr):
    velx, vely, velz, potx, poty, potz, logr = center
    grad_x, grad_y, grad_z = grads
    field_x = grad_y[5] - grad_z[4]
    field_y = grad_z[3] - grad_x[5]
    field_z = grad_x[4] - grad_y[3] + 0.5
    lorentz = (
        curr[1] * field_z - curr[2] * field_y,
        curr[2] * field_x - curr[0] * field_z,
        curr[0] * field_y - curr[1] * field_x,
    )
    emf = (
        vely * field_z - velz * field_y,
        velz * field_x - velx * field_z,
        velx * field_y - vely * field_x,
    )
    inv_rho = jnp.exp(-logr)
    flow = -1.5 * ((index.astype(jnp.float32) + 0.5) * inv_width - 0.5)
    shear_rate = -1.5 * inv_width
    carried = vely + flow
    divu = grad_x[0] + grad_y[1] + grad_z[2]

    def advect(comp):
        return velx * grad_x[comp] + carried * grad_y[comp] + velz * grad_z[comp]

    rates = []
    for comp in range(3):
        total = (-2.0 / 3.0) * divu * grads[comp][6]
        for col in range(3):
            total = total + (grads[col][comp] + grads[comp][col]) * grads[col][6]
        rate = lorentz[comp] * inv_rho - advect(comp) - grads[comp][6] + force[comp]
        rate = rate + 0.05 * (viscous[comp] + total)
        if comp == 0:
            rate = rate + vely
        if comp == 1:
            rate = rate - (1.0 + shear_rate) * velx
        rates.append(rate)
    for comp in range(3):
        rate = emf[comp] - flow * grad_y[3 + comp] - 0.05 * curr[comp]
        if comp == 0:
            rate = rate - shear_rate * poty
        rates.append(rate)
    rates.append(-advect(6) - divu)
    return rates


def face_kernel(cells_x, state, x_near, x_far):
    x_odd = lax.axis_index("gx") % 2

    def planes(first, then):
        first[...] = state[:, cells_x - 3 :]
        then[...] = state[:, :3]

    pl.when(x_odd == 0)(functools.partial(planes, x_near, x_far))
    pl.when(x_odd == 1)(functools.partial(planes, x_far, x_near))


def row_kernel(cells_x, cells_y, state, y_near, y_far):
    y_odd = lax.axis_index("yz") % 2

    def rows(first, then):
        for field in range(7):
            for plane in range(cells_x):
                at = 3 * (field * cells_x + plane)
                first[at : at + 3] = state[field, plane, cells_y - 3 :]
                then[at : at + 3] = state[field, plane, :3]

    pl.when(y_odd == 0)(functools.partial(rows, y_near, y_far))
    pl.when(y_odd == 1)(functools.partial(rows, y_far, y_near))


def weight_kernel(weights):
    weights[...] = z_weights()


def own_z_kernel(cells_x, state, weights, forcing, dz, dzz, force, sem):
    copy = pltpu.make_async_copy(forcing, force, sem)
    copy.start()
    got = along_z(state[...].reshape(7 * cells_x * 8, LANES), weights[...])
    dz[...] = (got[:, :LANES] * (1.0 / 60.0)).reshape(7, cells_x, 8, LANES)
    dzz[...] = (got[: 5 * cells_x * 8, LANES:] * (1.0 / 180.0)).reshape(5, cells_x, 8, LANES)
    copy.wait()


def across_kernel(cells_x, state, dz, after, x_parts):
    def plane_step(plane):
        terms = x_terms(
            lambda field: lambda step: state[field, plane + step],
            lambda field: lambda step: dz[field, plane + step],
        )
        for number, term in enumerate(terms):
            x_parts[number, plane - 3] = term

    in_pairs(3, cells_x - 3, plane_step)


def side_kernel(
    cells_x, state, weights, y_far, y_near, dz, dzz, after, side_terms, block, z_block
):
    own = slice(ROW, ROW + 8)
    y_odd = lax.axis_index("yz") % 2
    block[:, :, own] = state[...]
    for number, field in enumerate(SHEAR_Z):
        z_block[number, :, own] = dz[field]
    count = 3 * cells_x
    got = along_z(
        jnp.concatenate(
            [rows[field * count : (field + 1) * count] for rows in (y_near, y_far) for field in SHEAR_Z]
        ),
        weights[:, :LANES],
    ) * (1.0 / 60.0)

    def ghosts(target, rows, begin):
        for field in range(7):
            for plane in range(cells_x):
                at = 3 * (field * cells_x + plane)
                block[field, plane, target : target + 3] = rows[at : at + 3]
        for number in range(4):
            for plane in range(cells_x):
                at = begin + 3 * (number * cells_x + plane)
                z_block[number, plane, target : target + 3] = got[at : at + 3]

    @pl.when(y_odd == 0)
    def _():
        ghosts(ROW + 8, y_near, 0)
        ghosts(ROW - 3, y_far, 4 * count)

    @pl.when(y_odd == 1)
    def _():
        ghosts(ROW - 3, y_near, 0)
        ghosts(ROW + 8, y_far, 4 * count)

    def yz_step(plane):
        def rows_of(field):
            return lambda step: block[field, plane, ROW + step : ROW + 8 + step]

        def z_rows_of(number):
            return lambda step: z_block[number, plane, ROW + step : ROW + 8 + step]

        grad = [first_diff(rows_of(field)) for field in range(7)]
        cross = [first_diff(z_rows_of(number)) for number in range(4)]
        terms = grad + [
            second_diff(rows_of(0)) + dzz[0, plane],
            (4.0 / 3.0) * second_diff(rows_of(1)) + dzz[1, plane] + (1.0 / 3.0) * cross[1],
            second_diff(rows_of(2)) + (4.0 / 3.0) * dzz[2, plane] + (1.0 / 3.0) * cross[0],
            -(second_diff(rows_of(3)) + dzz[3, plane]),
            cross[3] - dzz[4, plane],
            cross[2] - second_diff(rows_of(5)),
        ]
        for number, term in enumerate(terms):
            side_terms[number, plane] = term

    in_pairs(0, cells_x, yz_step)


def in_pairs(begin, end, step):
    def two(number, carry):
        step(begin + 2 * number)
        step(begin + 2 * number + 1)
        return carry

    lax.fori_loop(0, (end - begin) // 2, two, 0)


def corner_kernel(slabs_x, x_far, x_near, after, faces, far, near):
    where_x = lax.axis_index("gx")
    y_odd = lax.axis_index("yz") % 2

    def order(low, high):
        faces[0] = low[...]
        faces[1] = high[...]

    pl.when(where_x % 2 == 0)(functools.partial(order, x_far, x_near))
    pl.when(where_x % 2 == 1)(functools.partial(order, x_near, x_far))

    def fill(to_next, to_last):
        for side in range(2):
            for number, field in enumerate(MIXED):
                for plane in range(3):
                    at = 3 * (3 * (4 * side + number) + plane)
                    to_next[at : at + 3] = faces[side, field, plane, 5:8]
                    to_last[at : at + 3] = faces[side, field, plane, 0:3]

        def sheared(side):
            for number, field in enumerate(MIXED + PLAIN):
                for plane in range(3):
                    at = 72 + 4 * (3 * number + plane)
                    row = 1 if field in MIXED else 4
                    to_next[at : at + 4] = faces[side, field, plane, row : row + 4]
                    row = 3 if field in MIXED else 0
                    to_last[at : at + 4] = faces[side, field, plane, row : row + 4]

        pl.when(where_x == 0)(functools.partial(sheared, 0))
        pl.when(where_x == slabs_x - 1)(functools.partial(sheared, 1))

    pl.when(y_odd == 0)(functools.partial(fill, near, far))
    pl.when(y_odd == 1)(functools.partial(fill, far, near))


def copies_out(parts, finals, begin, count, sems, base):
    return [
        pltpu.make_async_copy(part, final.at[:, pl.ds(begin, count)], sems.at[base + which])
        for which, (part, final) in enumerate(zip(parts, finals))
    ]


def finish(inv_width, index, center, force, old, x_parts, side, grad_z):
    rates = rates_of(
        center,
        force,
        index,
        inv_width,
        (x_parts[:7], side[:7], grad_z),
        [x_parts[7 + comp] + side[7 + comp] for comp in range(3)],
        [x_parts[10 + comp] + side[10 + comp] for comp in range(3)],
    )
    fresh = [(-5.0 / 9.0) * old[field] + 0.15 * rates[field] for field in range(7)]
    return [center[field] + (15.0 / 16.0) * fresh[field] for field in range(7)], fresh


def inner_kernel(
    cells_x, inv_width,
    state, register, forcing, dz, x_parts, side_terms,
    new_state, new_register, late_state, late_register,
    fresh_state, fresh_register, sems,
):
    first = lax.axis_index("gx") * cells_x
    early = EARLY

    def step_into(states_out, registers_out, begin):
        def plane_step(plane):
            states, registers = finish(
                inv_width,
                first + plane,
                [state[field, plane] for field in range(7)],
                [forcing[comp, plane] for comp in range(3)],
                [register[field, plane] for field in range(7)],
                xy_terms(
                    [x_parts[number, plane - 3] for number in range(13)],
                    lambda field: lambda step: side_terms[field, plane + step],
                ),
                [side_terms[number, plane] for number in range(13)],
                [dz[field, plane] for field in range(7)],
            )
            for field in range(7):
                registers_out[field, plane - begin] = registers[field]
                states_out[field, plane - begin] = states[field]

        return plane_step

    in_pairs(3, 3 + early, step_into(fresh_state, fresh_register, 3))
    copies = copies_out((fresh_state, fresh_register), (new_state, new_register), 3, early, sems, 0)
    for copy in copies:
        copy.start()
    in_pairs(3 + early, cells_x - 3, step_into(late_state, late_register, 3 + early))
    for copy in copies:
        copy.wait()


def edge_kernel(
    cells_x, slabs_x, inv_width,
    lean_tile, state, register, forcing, weights, dz, side_terms,
    planes, far, near, late_state, late_register, kept_state, kept_register,
    new_state, new_register,
    ghost, fields, deep, slope, fresh_state, fresh_register, sems,
):
    finals = (new_state, new_register)
    late = copies_out((late_state, late_register), finals, 3 + EARLY, cells_x - 6 - EARLY, sems, 0)
    for copy in late:
        copy.start()
    where_x = lax.axis_index("gx")
    y_odd = lax.axis_index("yz") % 2
    first = where_x * cells_x
    lean = lean_tile[...][0, 0]
    at_low, at_high = where_x == 0, where_x == slabs_x - 1
    for field in range(7):
        fields[0, field, 3:9] = state[field, 0:6]
        fields[1, field, 0:6] = state[field, cells_x - 6 :]
    for number, field in enumerate(DEEP):
        deep[0, number, 3:9] = dz[field, 0:6]
        deep[1, number, 0:6] = dz[field, cells_x - 6 :]
    for number, field in enumerate(MIXED):
        slope[0, number, 3:9] = side_terms[field, 0:6]
        slope[1, number, 0:6] = side_terms[field, cells_x - 6 :]
    for side in range(2):
        for field in range(7):
            for plane in range(3):
                ghost[side, field, plane, 16:24] = planes[side, field, plane]

    def put(from_last, from_next):
        for side in range(2):
            for number, field in enumerate(MIXED):
                for plane in range(3):
                    at = 3 * (3 * (4 * side + number) + plane)
                    ghost[side, field, plane, 13:16] = from_last[at : at + 3]
                    ghost[side, field, plane, 24:27] = from_next[at : at + 3]

        def sheared(side):
            for number, field in enumerate(MIXED + PLAIN):
                for plane in range(3):
                    at = 72 + 4 * (3 * number + plane)
                    row = 9 if field in MIXED else 12
                    ghost[side, field, plane, row : row + 4] = from_last[at : at + 4]
                    row = 27 if field in MIXED else 24
                    ghost[side, field, plane, row : row + 4] = from_next[at : at + 4]

        pl.when(at_low)(functools.partial(sheared, 0))
        pl.when(at_high)(functools.partial(sheared, 1))

    pl.when(y_odd == 0)(functools.partial(put, far, near))
    pl.when(y_odd == 1)(functools.partial(put, near, far))
    for side, shift in enumerate((jnp.where(at_low, lean, 0), jnp.where(at_high, -lean, 0))):
        for field in range(7):
            for plane in range(3):
                low = ghost[side, field, plane, pl.ds(shift + 13, 8)]
                if field in MIXED:
                    high = ghost[side, field, plane, pl.ds(shift + 21, 8)]
                    ghost[side, field, plane, 0:8] = low
                    ghost[side, field, plane, 8:16] = high
                    fields[side, field, plane + 6 * side] = ghost[side, field, plane, 3:11]
                else:
                    fields[side, field, plane + 6 * side] = ghost[side, field, plane, pl.ds(shift + 16, 8)]
    got = along_z(
        jnp.concatenate(
            [
                fields[side, field, 6 * side : 6 * side + 3].reshape(24, LANES)
                for side in range(2)
                for field in DEEP
            ]
        ),
        weights[:, :LANES],
    ) * (1.0 / 60.0)
    for side in range(2):
        for number in range(4):
            at = 24 * (4 * side + number)
            deep[side, number, 6 * side : 6 * side + 3] = got[at : at + 24].reshape(3, 8, LANES)
        for number, field in enumerate(MIXED):
            for plane in range(3):
                slope[side, number, plane + 6 * side] = first_diff(
                    lambda step: ghost[side, field, plane, 3 + step : 11 + step]
                )

    def copies_of(side):
        parts = (fresh_state.at[side], fresh_register.at[side])
        return copies_out(parts, finals, side * (cells_x - 3), 3, sems, 2 * (side + 1))

    for side in range(2):
        for local in range(3):
            plane = side * (cells_x - 3) + local
            states, registers = finish(
                inv_width,
                first + plane,
                [state[field, plane] for field in range(7)],
                [forcing[comp, plane] for comp in range(3)],
                [register[field, plane] for field in range(7)],
                xy_terms(
                    x_terms(
                        lambda field: lambda step: fields[side, field, local + 3 + step],
                        lambda field: lambda step: deep[side, DEEP.index(field), local + 3 + step],
                    ),
                    lambda field: lambda step: slope[side, MIXED.index(field), local + 3 + step],
                ),
                [side_terms[number, plane] for number in range(13)],
                [dz[field, plane] for field in range(7)],
            )
            for field in range(7):
                fresh_register[side, field, local] = registers[field]
                fresh_state[side, field, local] = states[field]
        for copy in copies_of(side):
            copy.start()
    for copy in late + copies_of(0) + copies_of(1):
        copy.wait()


def per_device(slabs_x, slabs_y, state, register, forcing, y_shift):
    cells_x, cells_y = state.shape[1], state.shape[2]
    total_x, total_y = cells_x * slabs_x, cells_y * slabs_y
    offset = y_shift[0]
    steps = (offset + cells_y // 2) // cells_y

    def shape(*dims):
        return jax.ShapeDtypeStruct(dims, jnp.float32)

    vmem = pl.BlockSpec(memory_space=pltpu.VMEM)
    anyspace = pl.BlockSpec(memory_space=pl.ANY)
    params = pltpu.CompilerParams(vmem_limit_bytes=VMEM)
    lean = lax.optimization_barrier(jnp.full((8, LANES), offset - steps * cells_y, jnp.int32))

    digit = min(slabs_y, 8)

    def place(slab, along):
        return along % slabs_y * slabs_x + slab

    def send(value, pairs):
        return lax.ppermute(value, ("yz", "gx"), pairs)

    def both(pairs):
        return pairs + [(b, a) for a, b in pairs]

    def y_pairs(odd):
        return both(
            [(place(slab, j), place(slab, j + 1)) for slab in range(slabs_x) for j in range(odd, slabs_y, 2)]
        )

    def x_pairs(odd, by):
        return both(
            [
                (place(slab, j + by * (slab == last)), place((slab + 1) % slabs_x, j))
                for slab in range(odd, slabs_x, 2)
                for j in range(slabs_y)
            ]
        )

    last = slabs_x - 1

    def cost(flops):
        return pl.CostEstimate(flops=flops, bytes_accessed=10**6, transcendentals=0)

    weights = pl.pallas_call(
        weight_kernel,
        out_shape=jax.ShapeDtypeStruct((2 * LANES, 2 * LANES), jnp.bfloat16),
        out_specs=vmem,
        compiler_params=params,
        cost_estimate=cost(2 * 10**8),
    )()

    def in_hbm(value):
        return pltpu.with_memory_space_constraint(value, pltpu.HBM)

    def faces_of(state):
        return pl.pallas_call(
            functools.partial(face_kernel, cells_x),
            out_shape=[shape(7, 3, cells_y, LANES)] * 2,
            in_specs=[vmem],
            out_specs=[vmem] * 2,
            compiler_params=params,
        )(state)

    x_near = x_far = None
    if slabs_y > digit:
        x_near, x_far = faces_of(state)
        where_x = lax.axis_index("gx")
        at_low, at_high = where_x == 0, where_x == last
        groups = steps // digit
        amount = jnp.where(at_high, groups, slabs_y // digit - groups) % (slabs_y // digit)
        across = x_far
        hop = 1
        while hop < slabs_y // digit:
            pairs = [(i, (i - hop * digit) % slabs_y) for i in range(slabs_y)]
            moved = lax.ppermute(across, "yz", pairs)
            across = jnp.where((amount // hop) % 2 == 1, moved, across)
            hop *= 2
        x_far = jnp.where(at_low | at_high, across, x_far)

    def exchange(by, operands):
        x_near, x_far, state, register, forcing, weights, lean = operands
        plane = state.shape[1:]
        if x_far is None:
            x_near, x_far = faces_of(state)
        x_far = send(x_far, x_pairs(1, by))
        x_near = send(x_near, x_pairs(0, 0))
        y_near, y_far = pl.pallas_call(
            functools.partial(row_kernel, cells_x, cells_y),
            out_shape=[shape(21 * cells_x, LANES), shape(21 * cells_x, LANES)],
            in_specs=[vmem],
            out_specs=[vmem] * 2,
            compiler_params=params,
        )(state)
        y_far = send(y_far, y_pairs(1))
        y_near = send(y_near, y_pairs(0))
        dz, dzz, force = pl.pallas_call(
            functools.partial(own_z_kernel, cells_x),
            out_shape=[shape(7, *plane), shape(5, *plane), shape(*forcing.shape)],
            in_specs=[vmem] * 2 + [pl.BlockSpec(memory_space=pltpu.HBM)],
            out_specs=[vmem] * 3,
            scratch_shapes=[pltpu.SemaphoreType.DMA],
            compiler_params=params,
            cost_estimate=cost(10**8),
        )(state, weights, forcing)
        faces, far, near = pl.pallas_call(
            functools.partial(corner_kernel, slabs_x),
            out_shape=[shape(2, *x_far.shape), shape(160, LANES), shape(160, LANES)],
            in_specs=[vmem] * 2 + [anyspace],
            out_specs=[vmem] * 3,
            compiler_params=params,
            cost_estimate=cost(CORNER),
        )(x_far, x_near, dz)
        far = send(far, y_pairs(1))
        near = send(near, y_pairs(0))
        x_parts = pl.pallas_call(
            functools.partial(across_kernel, cells_x),
            out_shape=shape(13, cells_x - 6, *plane[1:]),
            in_specs=[vmem] * 2 + [anyspace],
            out_specs=vmem,
            compiler_params=params,
            cost_estimate=cost(ACROSS),
        )(state, dz, faces)
        side_terms = pl.pallas_call(
            functools.partial(side_kernel, cells_x),
            out_shape=shape(13, *plane),
            in_specs=[vmem] * 6 + [anyspace],
            out_specs=vmem,
            scratch_shapes=[
                pltpu.VMEM((7, cells_x, TALL, LANES), jnp.float32),
                pltpu.VMEM((4, cells_x, TALL, LANES), jnp.float32),
            ],
            compiler_params=params,
            cost_estimate=cost(2 * 10**8),
        )(state, weights, y_far, y_near, dz, dzz, x_parts)
        early, late = EARLY, cells_x - 6 - EARLY
        new_state, new_register, late_state, late_register = pl.pallas_call(
            functools.partial(inner_kernel, cells_x, 1.0 / total_x),
            out_shape=[shape(*state.shape)] * 2 + [shape(7, late, *plane[1:])] * 2,
            in_specs=[vmem] * 6,
            out_specs=[anyspace] * 2 + [vmem] * 2,
            scratch_shapes=[
                pltpu.VMEM((7, early, *plane[1:]), jnp.float32),
                pltpu.VMEM((7, early, *plane[1:]), jnp.float32),
                pltpu.SemaphoreType.DMA((2,)),
            ],
            compiler_params=params,
            cost_estimate=cost(2 * 10**8),
        )(state, register, force, dz, x_parts, side_terms)
        return pl.pallas_call(
            functools.partial(edge_kernel, cells_x, slabs_x, 1.0 / total_x),
            out_shape=[shape(*state.shape)] * 2,
            in_specs=[vmem] * 12 + [anyspace] * 2,
            out_specs=[anyspace] * 2,
            input_output_aliases={12: 0, 13: 1},
            scratch_shapes=[
                pltpu.VMEM((2, 7, 3, 40, LANES), jnp.float32),
                pltpu.VMEM((2, 7, 9, 8, LANES), jnp.float32),
                pltpu.VMEM((2, 4, 9, 8, LANES), jnp.float32),
                pltpu.VMEM((2, 4, 9, 8, LANES), jnp.float32),
                pltpu.VMEM((2, 7, 3, 8, LANES), jnp.float32),
                pltpu.VMEM((2, 7, 3, 8, LANES), jnp.float32),
                pltpu.SemaphoreType.DMA((6,)),
            ],
            compiler_params=params,
        )(
            lean, state, register, force, weights, dz, side_terms,
            faces, far, near, late_state, late_register, new_state, new_register,
        )

    return lax.switch(
        steps % digit,
        [functools.partial(exchange, by) for by in range(digit)],
        (x_near, x_far, state, register, in_hbm(forcing), weights, lean),
    )


def solution(mesh):
    spec = P(None, "gx", "yz", None)
    return jax.shard_map(
        functools.partial(per_device, mesh.shape["gx"], mesh.shape["yz"]),
        mesh=mesh,
        in_specs=(spec, spec, spec, P()),
        out_specs=(spec, spec),
        check_vma=False,
    )
```

```python
import functools

import jax
import jax.numpy as jnp
from jax import lax
from jax.experimental import pallas as pl
from jax.experimental.pallas import tpu as pltpu
from jax.sharding import PartitionSpec as P

LANES = 128
FIRST = ((1, 45.0), (2, -9.0), (3, 1.0))
SECOND = ((1, 270.0), (2, -27.0), (3, 2.0))
MIXED = (0, 1, 3, 4)
PLAIN = (2, 5, 6)
DEEP = (0, 2, 3, 5)
SHEAR_Z = (1, 2, 4, 5)
ROW = 8
CORNER = 10**10
ACROSS = 10**7
EARLY = 6
TALL = 24
VMEM = 32 * 1024 * 1024


def z_weights():
    source = lax.broadcasted_iota(jnp.int32, (LANES, LANES), 0)
    cell = lax.broadcasted_iota(jnp.int32, (LANES, LANES), 1)
    ahead = (source - cell) & (LANES - 1)
    first = jnp.zeros((LANES, LANES), jnp.float32)
    second = jnp.where(ahead == 0, -490.0, 0.0)
    for step, weight in FIRST:
        first = jnp.where(ahead == step, weight, jnp.where(ahead == LANES - step, -weight, first))
    for step, weight in SECOND:
        second = jnp.where((ahead == step) | (ahead == LANES - step), weight, second)
    one = jnp.concatenate([first, second], axis=1)
    return jnp.concatenate([one, one]).astype(jnp.bfloat16)


def along_z(value, weights):
    upper = value.astype(jnp.bfloat16)
    rest = (value - upper.astype(jnp.float32)).astype(jnp.bfloat16)
    return jnp.dot(
        jnp.concatenate([upper, rest], axis=1), weights, preferred_element_type=jnp.float32
    )


def first_diff(part):
    return (
        0.75 * (part(1) - part(-1))
        - 0.15 * (part(2) - part(-2))
        + (1.0 / 60.0) * (part(3) - part(-3))
    )


def second_diff(part):
    return (
        (-490.0 / 180.0) * part(0)
        + 1.5 * (part(1) + part(-1))
        - 0.15 * (part(2) + part(-2))
        + (1.0 / 90.0) * (part(3) + part(-3))
    )


def x_terms(planes_of, deep_of):
    grad = [first_diff(planes_of(field)) for field in range(7)]
    viscous = [
        (4.0 / 3.0) * second_diff(planes_of(0)) + (1.0 / 3.0) * first_diff(deep_of(2)),
        second_diff(planes_of(1)),
        second_diff(planes_of(2)) + (1.0 / 3.0) * first_diff(deep_of(0)),
    ]
    current = [
        first_diff(deep_of(5)),
        -second_diff(planes_of(4)),
        first_diff(deep_of(3)) - second_diff(planes_of(5)),
    ]
    return grad + viscous + current


def xy_terms(parts, side_of):
    parts = list(parts)
    parts[7] = parts[7] + (1.0 / 3.0) * first_diff(side_of(1))
    parts[8] = parts[8] + (1.0 / 3.0) * first_diff(side_of(0))
    parts[10] = parts[10] + first_diff(side_of(4))
    parts[11] = parts[11] + first_diff(side_of(3))
    return parts


def rates_of(center, force, index, inv_width, grads, viscous, curr):
    velx, vely, velz, potx, poty, potz, logr = center
    grad_x, grad_y, grad_z = grads
    field_x = grad_y[5] - grad_z[4]
    field_y = grad_z[3] - grad_x[5]
    field_z = grad_x[4] - grad_y[3] + 0.5
    lorentz = (
        curr[1] * field_z - curr[2] * field_y,
        curr[2] * field_x - curr[0] * field_z,
        curr[0] * field_y - curr[1] * field_x,
    )
    emf = (
        vely * field_z - velz * field_y,
        velz * field_x - velx * field_z,
        velx * field_y - vely * field_x,
    )
    inv_rho = jnp.exp(-logr)
    flow = -1.5 * ((index.astype(jnp.float32) + 0.5) * inv_width - 0.5)
    shear_rate = -1.5 * inv_width
    carried = vely + flow
    divu = grad_x[0] + grad_y[1] + grad_z[2]

    def advect(comp):
        return velx * grad_x[comp] + carried * grad_y[comp] + velz * grad_z[comp]

    rates = []
    for comp in range(3):
        total = (-2.0 / 3.0) * divu * grads[comp][6]
        for col in range(3):
            total = total + (grads[col][comp] + grads[comp][col]) * grads[col][6]
        rate = lorentz[comp] * inv_rho - advect(comp) - grads[comp][6] + force[comp]
        rate = rate + 0.05 * (viscous[comp] + total)
        if comp == 0:
            rate = rate + vely
        if comp == 1:
            rate = rate - (1.0 + shear_rate) * velx
        rates.append(rate)
    for comp in range(3):
        rate = emf[comp] - flow * grad_y[3 + comp] - 0.05 * curr[comp]
        if comp == 0:
            rate = rate - shear_rate * poty
        rates.append(rate)
    rates.append(-advect(6) - divu)
    return rates


def face_kernel(cells_x, state, x_near, x_far):
    x_odd = lax.axis_index("gx") % 2

    def planes(first, then):
        first[...] = state[:, cells_x - 3 :]
        then[...] = state[:, :3]

    pl.when(x_odd == 0)(functools.partial(planes, x_near, x_far))
    pl.when(x_odd == 1)(functools.partial(planes, x_far, x_near))


def row_kernel(cells_x, cells_y, state, y_near, y_far):
    y_odd = lax.axis_index("yz") % 2

    def rows(first, then):
        for field in range(7):
            for plane in range(cells_x):
                at = 3 * (field * cells_x + plane)
                first[at : at + 3] = state[field, plane, cells_y - 3 :]
                then[at : at + 3] = state[field, plane, :3]

    pl.when(y_odd == 0)(functools.partial(rows, y_near, y_far))
    pl.when(y_odd == 1)(functools.partial(rows, y_far, y_near))


def weight_kernel(weights):
    weights[...] = z_weights()


def own_z_kernel(cells_x, state, weights, forcing, dz, dzz, force, sem):
    copy = pltpu.make_async_copy(forcing, force, sem)
    copy.start()
    got = along_z(state[...].reshape(7 * cells_x * 8, LANES), weights[...])
    dz[...] = (got[:, :LANES] * (1.0 / 60.0)).reshape(7, cells_x, 8, LANES)
    dzz[...] = (got[: 5 * cells_x * 8, LANES:] * (1.0 / 180.0)).reshape(5, cells_x, 8, LANES)
    copy.wait()


def across_kernel(cells_x, state, dz, after, x_parts):
    def plane_step(plane):
        terms = x_terms(
            lambda field: lambda step: state[field, plane + step],
            lambda field: lambda step: dz[field, plane + step],
        )
        for number, term in enumerate(terms):
            x_parts[number, plane - 3] = term

    in_pairs(3, cells_x - 3, plane_step)


def side_kernel(
    cells_x, state, weights, y_far, y_near, dz, dzz, after, side_terms, block, z_block
):
    own = slice(ROW, ROW + 8)
    y_odd = lax.axis_index("yz") % 2
    block[:, :, own] = state[...]
    for number, field in enumerate(SHEAR_Z):
        z_block[number, :, own] = dz[field]
    count = 3 * cells_x
    got = along_z(
        jnp.concatenate(
            [rows[field * count : (field + 1) * count] for rows in (y_near, y_far) for field in SHEAR_Z]
        ),
        weights[:, :LANES],
    ) * (1.0 / 60.0)

    def ghosts(target, rows, begin):
        for field in range(7):
            for plane in range(cells_x):
                at = 3 * (field * cells_x + plane)
                block[field, plane, target : target + 3] = rows[at : at + 3]
        for number in range(4):
            for plane in range(cells_x):
                at = begin + 3 * (number * cells_x + plane)
                z_block[number, plane, target : target + 3] = got[at : at + 3]

    @pl.when(y_odd == 0)
    def _():
        ghosts(ROW + 8, y_near, 0)
        ghosts(ROW - 3, y_far, 4 * count)

    @pl.when(y_odd == 1)
    def _():
        ghosts(ROW - 3, y_near, 0)
        ghosts(ROW + 8, y_far, 4 * count)

    def yz_step(plane):
        def rows_of(field):
            return lambda step: block[field, plane, ROW + step : ROW + 8 + step]

        def z_rows_of(number):
            return lambda step: z_block[number, plane, ROW + step : ROW + 8 + step]

        grad = [first_diff(rows_of(field)) for field in range(7)]
        cross = [first_diff(z_rows_of(number)) for number in range(4)]
        terms = grad + [
            second_diff(rows_of(0)) + dzz[0, plane],
            (4.0 / 3.0) * second_diff(rows_of(1)) + dzz[1, plane] + (1.0 / 3.0) * cross[1],
            second_diff(rows_of(2)) + (4.0 / 3.0) * dzz[2, plane] + (1.0 / 3.0) * cross[0],
            -(second_diff(rows_of(3)) + dzz[3, plane]),
            cross[3] - dzz[4, plane],
            cross[2] - second_diff(rows_of(5)),
        ]
        for number, term in enumerate(terms):
            side_terms[number, plane] = term

    in_pairs(0, cells_x, yz_step)


def in_pairs(begin, end, step):
    def two(number, carry):
        step(begin + 2 * number)
        step(begin + 2 * number + 1)
        return carry

    lax.fori_loop(0, (end - begin) // 2, two, 0)


def corner_kernel(slabs_x, x_far, x_near, after, faces, far, near):
    where_x = lax.axis_index("gx")
    y_odd = lax.axis_index("yz") % 2

    def order(low, high):
        faces[0] = low[...]
        faces[1] = high[...]

    pl.when(where_x % 2 == 0)(functools.partial(order, x_far, x_near))
    pl.when(where_x % 2 == 1)(functools.partial(order, x_near, x_far))

    def fill(to_next, to_last):
        for side in range(2):
            for number, field in enumerate(MIXED):
                for plane in range(3):
                    at = 3 * (3 * (4 * side + number) + plane)
                    to_next[at : at + 3] = faces[side, field, plane, 5:8]
                    to_last[at : at + 3] = faces[side, field, plane, 0:3]

        def sheared(side):
            for number, field in enumerate(MIXED + PLAIN):
                for plane in range(3):
                    at = 72 + 4 * (3 * number + plane)
                    row = 1 if field in MIXED else 4
                    to_next[at : at + 4] = faces[side, field, plane, row : row + 4]
                    row = 3 if field in MIXED else 0
                    to_last[at : at + 4] = faces[side, field, plane, row : row + 4]

        pl.when(where_x == 0)(functools.partial(sheared, 0))
        pl.when(where_x == slabs_x - 1)(functools.partial(sheared, 1))

    pl.when(y_odd == 0)(functools.partial(fill, near, far))
    pl.when(y_odd == 1)(functools.partial(fill, far, near))


def copies_out(parts, finals, begin, count, sems, base):
    return [
        pltpu.make_async_copy(part, final.at[:, pl.ds(begin, count)], sems.at[base + which])
        for which, (part, final) in enumerate(zip(parts, finals))
    ]


def finish(inv_width, index, center, force, old, x_parts, side, grad_z):
    rates = rates_of(
        center,
        force,
        index,
        inv_width,
        (x_parts[:7], side[:7], grad_z),
        [x_parts[7 + comp] + side[7 + comp] for comp in range(3)],
        [x_parts[10 + comp] + side[10 + comp] for comp in range(3)],
    )
    fresh = [(-5.0 / 9.0) * old[field] + 0.15 * rates[field] for field in range(7)]
    return [center[field] + (15.0 / 16.0) * fresh[field] for field in range(7)], fresh


def inner_kernel(
    cells_x, inv_width,
    state, register, forcing, dz, x_parts, side_terms,
    new_state, new_register, late_state, late_register,
    fresh_state, fresh_register, sems,
):
    first = lax.axis_index("gx") * cells_x
    early = EARLY

    def step_into(states_out, registers_out, begin):
        def plane_step(plane):
            states, registers = finish(
                inv_width,
                first + plane,
                [state[field, plane] for field in range(7)],
                [forcing[comp, plane] for comp in range(3)],
                [register[field, plane] for field in range(7)],
                xy_terms(
                    [x_parts[number, plane - 3] for number in range(13)],
                    lambda field: lambda step: side_terms[field, plane + step],
                ),
                [side_terms[number, plane] for number in range(13)],
                [dz[field, plane] for field in range(7)],
            )
            for field in range(7):
                registers_out[field, plane - begin] = registers[field]
                states_out[field, plane - begin] = states[field]

        return plane_step

    in_pairs(3, 3 + early, step_into(fresh_state, fresh_register, 3))
    copies = copies_out((fresh_state, fresh_register), (new_state, new_register), 3, early, sems, 0)
    for copy in copies:
        copy.start()
    in_pairs(3 + early, cells_x - 3, step_into(late_state, late_register, 3 + early))
    for copy in copies:
        copy.wait()


def edge_kernel(
    cells_x, slabs_x, inv_width,
    lean_tile, state, register, forcing, weights, dz, side_terms,
    planes, far, near, late_state, late_register, kept_state, kept_register,
    new_state, new_register,
    ghost, fields, deep, slope, fresh_state, fresh_register, sems,
):
    finals = (new_state, new_register)
    late = copies_out((late_state, late_register), finals, 3 + EARLY, cells_x - 6 - EARLY, sems, 0)
    for copy in late:
        copy.start()
    where_x = lax.axis_index("gx")
    y_odd = lax.axis_index("yz") % 2
    first = where_x * cells_x
    lean = lean_tile[...][0, 0]
    at_low, at_high = where_x == 0, where_x == slabs_x - 1
    for field in range(7):
        fields[0, field, 3:9] = state[field, 0:6]
        fields[1, field, 0:6] = state[field, cells_x - 6 :]
    for number, field in enumerate(DEEP):
        deep[0, number, 3:9] = dz[field, 0:6]
        deep[1, number, 0:6] = dz[field, cells_x - 6 :]
    for number, field in enumerate(MIXED):
        slope[0, number, 3:9] = side_terms[field, 0:6]
        slope[1, number, 0:6] = side_terms[field, cells_x - 6 :]
    for side in range(2):
        for field in range(7):
            for plane in range(3):
                ghost[side, field, plane, 16:24] = planes[side, field, plane]

    def put(from_last, from_next):
        for side in range(2):
            for number, field in enumerate(MIXED):
                for plane in range(3):
                    at = 3 * (3 * (4 * side + number) + plane)
                    ghost[side, field, plane, 13:16] = from_last[at : at + 3]
                    ghost[side, field, plane, 24:27] = from_next[at : at + 3]

        def sheared(side):
            for number, field in enumerate(MIXED + PLAIN):
                for plane in range(3):
                    at = 72 + 4 * (3 * number + plane)
                    row = 9 if field in MIXED else 12
                    ghost[side, field, plane, row : row + 4] = from_last[at : at + 4]
                    row = 27 if field in MIXED else 24
                    ghost[side, field, plane, row : row + 4] = from_next[at : at + 4]

        pl.when(at_low)(functools.partial(sheared, 0))
        pl.when(at_high)(functools.partial(sheared, 1))

    pl.when(y_odd == 0)(functools.partial(put, far, near))
    pl.when(y_odd == 1)(functools.partial(put, near, far))
    for side, shift in enumerate((jnp.where(at_low, lean, 0), jnp.where(at_high, -lean, 0))):
        for field in range(7):
            for plane in range(3):
                low = ghost[side, field, plane, pl.ds(shift + 13, 8)]
                if field in MIXED:
                    high = ghost[side, field, plane, pl.ds(shift + 21, 8)]
                    ghost[side, field, plane, 0:8] = low
                    ghost[side, field, plane, 8:16] = high
                    fields[side, field, plane + 6 * side] = ghost[side, field, plane, 3:11]
                else:
                    fields[side, field, plane + 6 * side] = ghost[side, field, plane, pl.ds(shift + 16, 8)]
    got = along_z(
        jnp.concatenate(
            [
                fields[side, field, 6 * side : 6 * side + 3].reshape(24, LANES)
                for side in range(2)
                for field in DEEP
            ]
        ),
        weights[:, :LANES],
    ) * (1.0 / 60.0)
    for side in range(2):
        for number in range(4):
            at = 24 * (4 * side + number)
            deep[side, number, 6 * side : 6 * side + 3] = got[at : at + 24].reshape(3, 8, LANES)
        for number, field in enumerate(MIXED):
            for plane in range(3):
                slope[side, number, plane + 6 * side] = first_diff(
                    lambda step: ghost[side, field, plane, 3 + step : 11 + step]
                )

    def copies_of(side, begin, count, base):
        parts = [fresh.at[side, :, pl.ds(begin, count)] for fresh in (fresh_state, fresh_register)]
        return copies_out(parts, finals, side * (cells_x - 3) + begin, count, sems, base)

    pieces = {(0, 2): copies_of(0, 0, 3, 2), (1, 1): copies_of(1, 0, 2, 4), (1, 2): copies_of(1, 2, 1, 6)}
    for side in range(2):
        for local in range(3):
            plane = side * (cells_x - 3) + local
            states, registers = finish(
                inv_width,
                first + plane,
                [state[field, plane] for field in range(7)],
                [forcing[comp, plane] for comp in range(3)],
                [register[field, plane] for field in range(7)],
                xy_terms(
                    x_terms(
                        lambda field: lambda step: fields[side, field, local + 3 + step],
                        lambda field: lambda step: deep[side, DEEP.index(field), local + 3 + step],
                    ),
                    lambda field: lambda step: slope[side, MIXED.index(field), local + 3 + step],
                ),
                [side_terms[number, plane] for number in range(13)],
                [dz[field, plane] for field in range(7)],
            )
            for field in range(7):
                fresh_register[side, field, local] = registers[field]
                fresh_state[side, field, local] = states[field]
            for copy in pieces.get((side, local), ()):
                copy.start()
    for copy in late + sum(pieces.values(), []):
        copy.wait()


def per_device(slabs_x, slabs_y, state, register, forcing, y_shift):
    cells_x, cells_y = state.shape[1], state.shape[2]
    total_x, total_y = cells_x * slabs_x, cells_y * slabs_y
    offset = y_shift[0]
    steps = (offset + cells_y // 2) // cells_y

    def shape(*dims):
        return jax.ShapeDtypeStruct(dims, jnp.float32)

    vmem = pl.BlockSpec(memory_space=pltpu.VMEM)
    anyspace = pl.BlockSpec(memory_space=pl.ANY)
    params = pltpu.CompilerParams(vmem_limit_bytes=VMEM)
    lean = lax.optimization_barrier(jnp.full((8, LANES), offset - steps * cells_y, jnp.int32))

    digit = min(slabs_y, 8)

    def place(slab, along):
        return along % slabs_y * slabs_x + slab

    def send(value, pairs):
        return lax.ppermute(value, ("yz", "gx"), pairs)

    def both(pairs):
        return pairs + [(b, a) for a, b in pairs]

    def y_pairs(odd):
        return both(
            [(place(slab, j), place(slab, j + 1)) for slab in range(slabs_x) for j in range(odd, slabs_y, 2)]
        )

    def x_pairs(odd, by):
        return both(
            [
                (place(slab, j + by * (slab == last)), place((slab + 1) % slabs_x, j))
                for slab in range(odd, slabs_x, 2)
                for j in range(slabs_y)
            ]
        )

    last = slabs_x - 1

    def cost(flops):
        return pl.CostEstimate(flops=flops, bytes_accessed=10**6, transcendentals=0)

    weights = pl.pallas_call(
        weight_kernel,
        out_shape=jax.ShapeDtypeStruct((2 * LANES, 2 * LANES), jnp.bfloat16),
        out_specs=vmem,
        compiler_params=params,
        cost_estimate=cost(2 * 10**8),
    )()

    def in_hbm(value):
        return pltpu.with_memory_space_constraint(value, pltpu.HBM)

    def faces_of(state):
        return pl.pallas_call(
            functools.partial(face_kernel, cells_x),
            out_shape=[shape(7, 3, cells_y, LANES)] * 2,
            in_specs=[vmem],
            out_specs=[vmem] * 2,
            compiler_params=params,
        )(state)

    x_near = x_far = None
    if slabs_y > digit:
        x_near, x_far = faces_of(state)
        where_x = lax.axis_index("gx")
        at_low, at_high = where_x == 0, where_x == last
        groups = steps // digit
        amount = jnp.where(at_high, groups, slabs_y // digit - groups) % (slabs_y // digit)
        across = x_far
        hop = 1
        while hop < slabs_y // digit:
            pairs = [(i, (i - hop * digit) % slabs_y) for i in range(slabs_y)]
            moved = lax.ppermute(across, "yz", pairs)
            across = jnp.where((amount // hop) % 2 == 1, moved, across)
            hop *= 2
        x_far = jnp.where(at_low | at_high, across, x_far)

    def exchange(by, operands):
        x_near, x_far, state, register, forcing, weights, lean = operands
        plane = state.shape[1:]
        if x_far is None:
            x_near, x_far = faces_of(state)
        x_far = send(x_far, x_pairs(1, by))
        x_near = send(x_near, x_pairs(0, 0))
        y_near, y_far = pl.pallas_call(
            functools.partial(row_kernel, cells_x, cells_y),
            out_shape=[shape(21 * cells_x, LANES), shape(21 * cells_x, LANES)],
            in_specs=[vmem],
            out_specs=[vmem] * 2,
            compiler_params=params,
        )(state)
        y_far = send(y_far, y_pairs(1))
        y_near = send(y_near, y_pairs(0))
        dz, dzz, force = pl.pallas_call(
            functools.partial(own_z_kernel, cells_x),
            out_shape=[shape(7, *plane), shape(5, *plane), shape(*forcing.shape)],
            in_specs=[vmem] * 2 + [pl.BlockSpec(memory_space=pltpu.HBM)],
            out_specs=[vmem] * 3,
            scratch_shapes=[pltpu.SemaphoreType.DMA],
            compiler_params=params,
            cost_estimate=cost(10**8),
        )(state, weights, forcing)
        faces, far, near = pl.pallas_call(
            functools.partial(corner_kernel, slabs_x),
            out_shape=[shape(2, *x_far.shape), shape(160, LANES), shape(160, LANES)],
            in_specs=[vmem] * 2 + [anyspace],
            out_specs=[vmem] * 3,
            compiler_params=params,
            cost_estimate=cost(CORNER),
        )(x_far, x_near, dz)
        far = send(far, y_pairs(1))
        near = send(near, y_pairs(0))
        x_parts = pl.pallas_call(
            functools.partial(across_kernel, cells_x),
            out_shape=shape(13, cells_x - 6, *plane[1:]),
            in_specs=[vmem] * 2 + [anyspace],
            out_specs=vmem,
            compiler_params=params,
            cost_estimate=cost(ACROSS),
        )(state, dz, faces)
        side_terms = pl.pallas_call(
            functools.partial(side_kernel, cells_x),
            out_shape=shape(13, *plane),
            in_specs=[vmem] * 6 + [anyspace],
            out_specs=vmem,
            scratch_shapes=[
                pltpu.VMEM((7, cells_x, TALL, LANES), jnp.float32),
                pltpu.VMEM((4, cells_x, TALL, LANES), jnp.float32),
            ],
            compiler_params=params,
            cost_estimate=cost(2 * 10**8),
        )(state, weights, y_far, y_near, dz, dzz, x_parts)
        early, late = EARLY, cells_x - 6 - EARLY
        new_state, new_register, late_state, late_register = pl.pallas_call(
            functools.partial(inner_kernel, cells_x, 1.0 / total_x),
            out_shape=[shape(*state.shape)] * 2 + [shape(7, late, *plane[1:])] * 2,
            in_specs=[vmem] * 6,
            out_specs=[anyspace] * 2 + [vmem] * 2,
            scratch_shapes=[
                pltpu.VMEM((7, early, *plane[1:]), jnp.float32),
                pltpu.VMEM((7, early, *plane[1:]), jnp.float32),
                pltpu.SemaphoreType.DMA((2,)),
            ],
            compiler_params=params,
            cost_estimate=cost(2 * 10**8),
        )(state, register, force, dz, x_parts, side_terms)
        return pl.pallas_call(
            functools.partial(edge_kernel, cells_x, slabs_x, 1.0 / total_x),
            out_shape=[shape(*state.shape)] * 2,
            in_specs=[vmem] * 12 + [anyspace] * 2,
            out_specs=[anyspace] * 2,
            input_output_aliases={12: 0, 13: 1},
            scratch_shapes=[
                pltpu.VMEM((2, 7, 3, 40, LANES), jnp.float32),
                pltpu.VMEM((2, 7, 9, 8, LANES), jnp.float32),
                pltpu.VMEM((2, 4, 9, 8, LANES), jnp.float32),
                pltpu.VMEM((2, 4, 9, 8, LANES), jnp.float32),
                pltpu.VMEM((2, 7, 3, 8, LANES), jnp.float32),
                pltpu.VMEM((2, 7, 3, 8, LANES), jnp.float32),
                pltpu.SemaphoreType.DMA((8,)),
            ],
            compiler_params=params,
        )(
            lean, state, register, force, weights, dz, side_terms,
            faces, far, near, late_state, late_register, new_state, new_register,
        )

    return lax.switch(
        steps % digit,
        [functools.partial(exchange, by) for by in range(digit)],
        (x_near, x_far, state, register, in_hbm(forcing), weights, lean),
    )


def solution(mesh):
    spec = P(None, "gx", "yz", None)
    return jax.shard_map(
        functools.partial(per_device, mesh.shape["gx"], mesh.shape["yz"]),
        mesh=mesh,
        in_specs=(spec, spec, spec, P()),
        out_specs=(spec, spec),
        check_vma=False,
    )
```
